32 devices in a mesh: groups: 2 (over y), seq: 16 (over z, x, core).
Axes of the slice: x: 2, y: 2, z: 4, core: 2. Of those that a mesh axis runs over, the one named last changes fastest.
Arguments:
- queries: bfloat16 [8192, 768], P(('groups', 'seq')), parts along dimension 0, may hold values from -6 to 6
- keys: bfloat16 [8192, 768], P(('groups', 'seq')), parts along dimension 0, may hold values from -6 to 6
- values: bfloat16 [8192, 768], P(('groups', 'seq')), parts along dimension 0, may hold values from -6 to 6
- out_grad: bfloat16 [8192, 768], P(('groups', 'seq')), parts along dimension 0, may hold values from -6 to 6
- slide_lengths: int32 [16], P('groups'), parts along dimension 0, may hold values from 1 to 2560, 4096 in all
- head_offsets: int32 [3, 16], replicated, may hold values from 0 to 3
Outputs:
- attended: bfloat16 [8192, 768], P(('groups', 'seq')), parts along dimension 0
- query_grad: bfloat16 [8192, 768], P(('groups', 'seq')), parts along dimension 0
- key_grad: bfloat16 [8192, 768], P(('groups', 'seq')), parts along dimension 0
- value_grad: bfloat16 [8192, 768], P(('groups', 'seq')), parts along dimension 0
The draws below stay inside these ranges and needn't reach their ends.
There are 2 independent parts, one for each index of `groups`. The reference program is written for one: setup_inputs(seed, part) draws one part's arguments, and reference() takes and returns one part's arrays. A program takes and returns all parts, laid end to end along the dimension named above; an argument that names none is the same for every part. Nothing has to cross between parts.
Inputs may be any that keep to these rules, and one draw needn't show every extreme that they name: `slide_lengths`: the slides lie end to end over the 4096 tokens of a part, in order.
All inputs are finite; a program needn't handle non-finite values.
Results may differ from the reference program's by a relative error of at most 0.03.
Values may be sent and summed in bfloat16 or wider, within the bound.
No kernel may reach another device: no remote copies, remote signals or barrier semaphores. Data moves between devices by JAX's collectives and lax.ppermute only.
A program may use at most 128 MiB of HBM per device.

```python
import math
import jax
import jax.numpy as jnp
import numpy as np
from jax import lax

HEADS = 16
HEAD_DIM = 48
WIDTH = 768
SEG0 = 1024
LEVELS = 3
SLIDES = 8
TOKENS = 4096
SLIDE_MOST = 2560


def draw_queries(key, part):
    key = jax.random.fold_in(key, 11)
    base_draw = jnp.clip(jax.random.normal(key, (TOKENS, HEADS * HEAD_DIM), jnp.float32), -6.0, 6.0)
    return base_draw.astype(jnp.bfloat16)


def draw_keys(key, part):
    key = jax.random.fold_in(key, 12)
    base_draw = jnp.clip(jax.random.normal(key, (TOKENS, HEADS * HEAD_DIM), jnp.float32), -6.0, 6.0)
    return base_draw.astype(jnp.bfloat16)


def plant(values, key, least, top_value):
    longest = values.shape.index(max(values.shape))
    spots = []
    for shift in (0, 1):
        where = [jax.random.randint(jax.random.fold_in(key, axis), (), 0, length) for axis, length in enumerate(values.shape)]
        where[longest] = (where[longest] + shift) % values.shape[longest]
        spots.append(tuple(where))
    return values.at[spots[0]].set(least).at[spots[1]].set(top_value)


def levels(stream_key, extent, shards, low, top_value):
    level, own = 1.0, jax.random.fold_in(stream_key, 6)
    for axis_at, shards_of in shards:
        steps = jnp.exp(jax.random.uniform(jax.random.fold_in(own, axis_at), (shards_of,), jnp.float32, low / len(shards), top_value / len(shards)))
        level = level * jnp.repeat(steps, extent[axis_at] // shards_of).reshape([-1 if axis == axis_at else 1 for axis in range(len(extent))])
    return level


def length_profile(count, total, most, slope):
    loads = [(1 << 20) // math.isqrt(rank ** slope) + 1 for rank in range(2, count + 1)]
    spare, holding = total - most - (count - 1), [1] * (count - 1)
    while spare > 0:
        movable = [i for i in range(count - 1) if holding[i] < most]
        mass, budget = sum([loads[i] for i in movable]), spare
        for i in movable:
            extra = min(most - holding[i], max(1, budget * loads[i] // mass), spare)
            holding[i] = holding[i] + extra
            spare = spare - extra
    return np.array([most] + holding)


def uneven(own_key, number_of, total, limit, lean):
    if number_of == 2:
        one = jax.random.randint(own_key, (), max(1, total - limit), min(limit, total - 1) + 1)
        return jnp.stack([one, total - one])
    tallies = jnp.asarray(length_profile(number_of, total, limit, lean), jnp.int32)
    couples = (number_of - 1) // 2
    giver, receiver = tallies[1:1 + 2 * couples:2], tallies[2:2 + 2 * couples:2]
    room = jnp.minimum(giver - 1, limit - receiver)
    passed = jax.random.randint(jax.random.fold_in(own_key, 1), (couples,), 0, 1 << 20) % (room + 1)
    tallies = tallies.at[1:1 + 2 * couples:2].set(giver - passed).at[2:2 + 2 * couples:2].set(receiver + passed)
    return tallies[jax.random.permutation(jax.random.fold_in(own_key, 2), number_of)]


def normal_values(stream_key, dims, scale, bound, cuts=(), kind=jnp.bfloat16):
    gain = levels(stream_key, dims, cuts, -0.22, 0.18) if cuts else 1.0
    entries = jax.random.normal(stream_key, dims, jnp.float32) * scale * gain
    return jnp.minimum(jnp.maximum(entries, -bound), bound).astype(kind)


def setup_inputs(seed: int = 0, part: int = 0) -> dict:
    arg_keys = jax.random.split(jax.random.key(seed), 7)
    own_keys = jax.random.split(jax.random.fold_in(arg_keys[6], part), 7)
    queries = draw_queries(jax.random.fold_in(jax.random.fold_in(arg_keys[6], part), 71), part)
    keys = draw_keys(jax.random.fold_in(jax.random.fold_in(arg_keys[6], part), 71), part)
    values = normal_values(own_keys[2], (TOKENS, WIDTH), 1.0, 6.0, ((0, 16),))
    out_grad = normal_values(own_keys[3], (TOKENS, WIDTH), 1.0, 6.0, ((0, 16),))
    slide_lengths = uneven(own_keys[4], SLIDES, TOKENS, SLIDE_MOST, 2).astype(jnp.int32)
    head_offsets = plant(jax.random.randint(arg_keys[5], (LEVELS, HEADS), 0, TOKENS // SEG0), jax.random.fold_in(arg_keys[5], 1), 0, (TOKENS // SEG0) - 1).astype(jnp.int32)
    return {"queries": queries, "keys": keys, "values": values, "out_grad": out_grad, "slide_lengths": slide_lengths, "head_offsets": head_offsets}


def slide_of(positions, slide_lengths):
    slide_ends = jnp.cumsum(slide_lengths).astype(jnp.int32)
    return jnp.sum((positions[..., None] >= slide_ends).astype(jnp.int32), axis=-1).astype(jnp.int32)


def select_rows(source, picked, segment_count, row_count, stride):
    shaped = source.reshape((segment_count, row_count, stride) + source.shape[1:])
    keep_mask = picked.reshape((1, 1) + picked.shape + (1,) * (source.ndim - 2))
    chosen = jnp.sum(jnp.where(keep_mask, shaped, jnp.zeros((), source.dtype)), axis=2)
    return chosen.astype(source.dtype)


def spread_rows(chosen, picked, fill_value):
    keep_mask = picked.reshape((1, 1) + picked.shape + (1,) * (chosen.ndim - 3))
    spread_out = jnp.where(keep_mask, chosen[:, :, None], jnp.asarray(fill_value, chosen.dtype))
    return spread_out.reshape((-1,) + chosen.shape[2:])


def block_scores(query_block, key_block, slide_block):
    score_scale = HEAD_DIM ** -0.5
    raw_scores = jnp.einsum('qhd,khd->hqk', query_block.astype(jnp.float32), key_block.astype(jnp.float32)) * score_scale
    allowed = slide_block.T[:, :, None] == slide_block.T[:, None, :]
    return jnp.where(allowed, raw_scores, -jnp.inf)


def forward_block(pieces):
    query_block, key_block, value_block, slide_block = pieces
    scores = block_scores(query_block, key_block, slide_block)
    row_peak = jnp.max(scores, axis=-1)
    exp_terms = jnp.exp(scores - row_peak[..., None])
    softmax_sum = jnp.sum(exp_terms, axis=-1)
    weights = lax.optimization_barrier(exp_terms.astype(jnp.bfloat16))
    weighted = jnp.einsum('hqk,khd->qhd', weights.astype(jnp.float32), value_block.astype(jnp.float32))
    return row_peak.T, softmax_sum.T, weighted


def backward_block(pieces):
    query_block, key_block, value_block, grad_block, total_block, dot_block, slide_block = pieces
    score_scale = HEAD_DIM ** -0.5
    scores = block_scores(query_block, key_block, slide_block)
    probability = jnp.exp(scores - total_block.T[..., None])
    prob_half = lax.optimization_barrier(probability.astype(jnp.bfloat16))
    value_part = jnp.einsum('hqk,qhd->khd', prob_half.astype(jnp.float32), grad_block.astype(jnp.float32))
    prob_grad = jnp.einsum('qhd,khd->hqk', grad_block.astype(jnp.float32), value_block.astype(jnp.float32))
    score_half = lax.optimization_barrier((probability * (prob_grad - dot_block.T[..., None])).astype(jnp.bfloat16))
    query_part = jnp.einsum('hqk,khd->qhd', score_half.astype(jnp.float32), key_block.astype(jnp.float32)) * score_scale
    key_part = jnp.einsum('hqk,qhd->khd', score_half.astype(jnp.float32), query_block.astype(jnp.float32)) * score_scale
    return query_part, key_part, value_part


def reference(queries, keys, values, out_grad, slide_lengths, head_offsets):
    split_shape = (TOKENS, HEADS, HEAD_DIM)
    query_heads = queries.reshape(split_shape)
    key_heads = keys.reshape(split_shape)
    value_heads = values.reshape(split_shape)
    grad_heads = out_grad.reshape(split_shape)
    layouts = []
    peaks = []
    sums = []
    weighted_all = []
    for level_index in range(LEVELS):
        stride = 2 ** level_index if level_index < LEVELS - 1 else TOKENS // SEG0
        segment_span = min(SEG0 * stride, TOKENS)
        segment_count = TOKENS // segment_span
        row_count = segment_span // stride
        offsets = (head_offsets[level_index] % stride).astype(jnp.int32)
        picked = jnp.arange(stride, dtype=jnp.int32)[:, None] == offsets[None, :]
        lane_positions = (jnp.arange(segment_count, dtype=jnp.int32)[:, None, None] * segment_span
                          + jnp.arange(row_count, dtype=jnp.int32)[None, :, None] * stride
                          + offsets[None, None, :]).astype(jnp.int32)
        slide_block = slide_of(lane_positions, slide_lengths)
        query_sel = select_rows(query_heads, picked, segment_count, row_count, stride)
        key_sel = select_rows(key_heads, picked, segment_count, row_count, stride)
        value_sel = select_rows(value_heads, picked, segment_count, row_count, stride)
        row_peak, softmax_sum, weighted = lax.map(forward_block, (query_sel, key_sel, value_sel, slide_block))
        peaks.append(spread_rows(row_peak, picked, -jnp.inf))
        sums.append(spread_rows(softmax_sum, picked, 0.0))
        weighted_all.append(spread_rows(weighted, picked, 0.0))
        layouts.append((stride, segment_count, row_count, picked, query_sel, key_sel, value_sel, slide_block))
    overall_peak = jnp.max(jnp.stack(peaks), axis=0)
    grand_total = jnp.zeros((TOKENS, HEADS), jnp.float32)
    merged = jnp.zeros((TOKENS, HEADS, HEAD_DIM), jnp.float32)
    for level_index in range(LEVELS):
        factor = jnp.exp(peaks[level_index] - overall_peak)
        grand_total = grand_total + factor * sums[level_index]
        merged = merged + factor[..., None] * weighted_all[level_index]
    attended = lax.optimization_barrier((merged / grand_total[..., None]).astype(jnp.bfloat16))
    log_total = overall_peak + jnp.log(grand_total)
    grad_dot = jnp.sum(grad_heads.astype(jnp.float32) * attended.astype(jnp.float32), axis=-1)
    query_total = jnp.zeros((TOKENS, HEADS, HEAD_DIM), jnp.float32)
    key_total = jnp.zeros((TOKENS, HEADS, HEAD_DIM), jnp.float32)
    value_total = jnp.zeros((TOKENS, HEADS, HEAD_DIM), jnp.float32)
    for stride, segment_count, row_count, picked, query_sel, key_sel, value_sel, slide_block in layouts:
        grad_sel = select_rows(grad_heads, picked, segment_count, row_count, stride)
        total_sel = select_rows(log_total, picked, segment_count, row_count, stride)
        dot_sel = select_rows(grad_dot, picked, segment_count, row_count, stride)
        query_part, key_part, value_part = lax.map(backward_block, (query_sel, key_sel, value_sel, grad_sel, total_sel, dot_sel, slide_block))
        query_total = query_total + spread_rows(query_part, picked, 0.0)
        key_total = key_total + spread_rows(key_part, picked, 0.0)
        value_total = value_total + spread_rows(value_part, picked, 0.0)
    flat_shape = (TOKENS, WIDTH)
    return (attended.reshape(flat_shape),
            query_total.astype(jnp.bfloat16).reshape(flat_shape),
            key_total.astype(jnp.bfloat16).reshape(flat_shape),
            value_total.astype(jnp.bfloat16).reshape(flat_shape))
```

```python
from functools import partial
import math

import jax
import jax.numpy as jnp
from jax import lax
from jax.experimental import pallas as pl
from jax.experimental.pallas import tpu as pltpu
from jax.sharding import PartitionSpec as P

SEG0 = 1024
BIG = 2.0**100
LOG2E = math.log2(math.e)
BF16 = jnp.bfloat16
F32 = jnp.float32
VMEM_LIMIT = 44 << 20


class Plan:
    def __init__(self, tok_rows, model_width, level_count, head_count, slide_count, device_count):
        self.tok = tok_rows
        self.levels = level_count
        self.heads = head_count
        self.hd = model_width // head_count
        self.slides = slide_count
        self.devices = device_count
        self.stride = device_count * tok_rows // SEG0
        self.bits = self.stride.bit_length() - 1
        self.near = min((SEG0 << (level_count - 2)) // tok_rows, device_count)
        self.far = device_count // self.near
        self.chunks = head_count // self.near
        self.segs = self.near * tok_rows // SEG0
        self.seg_dev = SEG0 // tok_rows
        self.cdev = tok_rows // self.stride
        self.cseg = SEG0 // self.stride
        self.rows = self.near * tok_rows
        self.last_rows = self.segs * self.cseg
        self.tiles = []
        for level in range(level_count - 1):
            for first in range(0, self.segs, 1 << level):
                self.tiles.append((level, first))
        self.all_rows = len(self.tiles) * SEG0
        self.half = tok_rows // 2
        self.slide_pad = -(-slide_count // 8) * 8
        assert 2 * self.hd + 8 + self.slide_pad <= 128 and 4 * self.hd <= 256


def reversed_bits(value, bits):
    out = value * 0
    for b in range(bits):
        out = out + ((value >> b) & 1) * (1 << (bits - 1 - b))
    return out


def dot(a, b):
    return lax.dot_general(a, b, (((1,), (0,)), ((), ())), preferred_element_type=F32)


def iota(shape, axis):
    return lax.broadcasted_iota(jnp.int32, shape, axis)


def kernel_call(body, out_shape, in_specs, scratch=(), flops=0, name=None):
    return pl.pallas_call(
        body,
        out_shape=out_shape,
        in_specs=in_specs,
        scratch_shapes=list(scratch),
        name=name,
        compiler_params=pltpu.CompilerParams(vmem_limit_bytes=VMEM_LIMIT),
        cost_estimate=pl.CostEstimate(flops=flops, bytes_accessed=1 << 20, transcendentals=0),
    )


VMEM = pl.BlockSpec(memory_space=pltpu.VMEM)
SMEM = pl.BlockSpec(memory_space=pltpu.SMEM)


def class_of_token(plan, shape, axis_row, axis_tok):
    row, tok = iota(shape, axis_row), iota(shape, axis_tok)
    want = (row % plan.cdev) * plan.stride + reversed_bits(row // plan.cdev, plan.bits)
    return jnp.where(want == tok, 1.0, 0.0).astype(BF16)


def pack_body(plan, q_ref, k_ref, v_ref, g_ref, off_ref, *outs):
    main_refs, last_ref = outs[:-1], outs[-1]
    order = class_of_token(plan, (plan.tok, plan.tok), 0, 1)
    sorted_rows = [dot(order, ref[...]) for ref in (q_ref, k_ref, v_ref, g_ref)]
    hd, half = plan.hd, plan.half
    for chunk in range(plan.chunks):
        for dest in range(plan.near):
            col = (chunk * plan.near + dest) * hd
            parts = [
                x[h * half : (h + 1) * half, col : col + hd] for h in range(2) for x in sorted_rows
            ]
            main_refs[chunk][dest] = jnp.concatenate(parts, axis=1).astype(BF16)
    last_rows(plan, sorted_rows[1], sorted_rows[2], off_ref, last_ref)


def last_rows(plan, k, v, off_ref, last_ref):
    hd, cdev = plan.hd, plan.cdev
    classes = range(plan.stride)
    pad = jnp.zeros((cdev, 128 - 2 * hd), F32)
    for dest in range(plan.near):
        blocks = []
        for chunk in range(plan.chunks):
            head = chunk * plan.near + dest
            col = head * hd
            place = reversed_bits(off_ref[plan.levels - 1, head] % plan.stride, plan.bits)
            both = jnp.concatenate([k[:, col : col + hd], v[:, col : col + hd]], axis=1)
            got = jnp.zeros((cdev, 2 * hd), F32)
            for c in classes:
                got = jnp.where(place == c, both[c * cdev : (c + 1) * cdev], got)
            blocks.append(jnp.concatenate([got, pad], axis=1))
        rows = jnp.concatenate(blocks, axis=0).astype(BF16)
        for group in range(plan.far):
            last_ref[group * plan.near + dest] = rows


def slide_rows(plan, pos, len_ref):
    slide = jnp.zeros(pos.shape, jnp.int32)
    end = 0
    for i in range(plan.slides):
        end = end + len_ref[i]
        slide = slide + jnp.where(pos >= end, 1, 0)
    shape = (plan.slide_pad, pos.shape[1])
    return jnp.where(iota(shape, 0) == slide, 1.0, 0.0)


def key_features(plan, k, one_hot):
    n = k.shape[1]
    rest = 128 - 2 * plan.hd - 8 - plan.slide_pad
    return jnp.concatenate([k, k, jnp.ones((8, n), F32), one_hot, jnp.zeros((rest, n), F32)], axis=0)


def query_features(plan, q, one_hot):
    n = q.shape[1]
    rest = 128 - 2 * plan.hd - 8 - plan.slide_pad
    q = q * (plan.hd**-0.5 * LOG2E)
    high = q.astype(BF16).astype(F32)
    return jnp.concatenate(
        [high, q - high, jnp.zeros((8, n), F32), (one_hot - 1.0) * BIG, jnp.zeros((rest, n), F32)],
        axis=0,
    )


def value_features(plan, v):
    n = v.shape[1]
    return jnp.concatenate([v, jnp.ones((8, n), F32), jnp.zeros((64 - plan.hd - 8, n), F32)], axis=0)


def forward_tile(plan, keys, queries_t, values_t):
    s = dot(keys, queries_t)
    peak = jnp.max(s, axis=0, keepdims=True)
    p = jnp.exp2(s - peak).astype(BF16)
    o = dot(values_t, p)
    n = o.shape[1]
    hd = plan.hd
    full = jnp.concatenate(
        [o[: hd + 8], jnp.broadcast_to(peak, (8, n)), jnp.zeros((128 - hd - 16, n), F32)], axis=0
    )
    return full.T


def merged(plan, a, b):
    at = plan.hd + 8
    peak_a, peak_b = a[:, at : at + 1], b[:, at : at + 1]
    peak = jnp.maximum(peak_a, peak_b)
    both = a * jnp.exp2(peak_a - peak) + b * jnp.exp2(peak_b - peak)
    return jnp.where(iota(a.shape, 1) >= at, peak, both)


def level_start(plan, off_ref, level, chunk):
    head = chunk * plan.near + lax.rem(lax.axis_index("seq"), plan.near)
    bits = level if level < plan.levels - 1 else plan.bits
    rows = SEG0 >> bits
    return reversed_bits(off_ref[level, head] % (1 << bits), bits) * rows, rows


def tile_pieces(plan, off_ref, chunk, tile):
    level, first = plan.tiles[tile]
    start, rows = level_start(plan, off_ref, level, chunk)
    return [
        (pl.multiple_of((first + i) * SEG0 + start, 128), i * rows, rows) for i in range(1 << level)
    ]


def forward_body(plan, chunk, x_ref, len_ref, off_ref, ka, kat, qa0, ga0, vat, gt, qt, acc_ref, xs, qat, res):
    hd, half = plan.hd, plan.half
    base = lax.axis_index("seq") // plan.near * plan.rows
    for src in range(plan.near):
        seg, at = src // plan.seg_dev, src % plan.seg_dev
        block = x_ref[src].astype(F32)
        for c in range(plan.stride):
            side = c * plan.cdev // half
            row = c * plan.cdev - side * half
            dst = seg * SEG0 + c * plan.cseg + at * plan.cdev
            xs[dst : dst + plan.cdev, 0 : 4 * hd] = block[
                row : row + plan.cdev, side * 4 * hd : (side + 1) * 4 * hd
            ]
    for seg in range(plan.segs):
        rows = slice(seg * SEG0, (seg + 1) * SEG0)
        xt = xs[rows, :].T
        q, k, v, g = (xt[i * hd : (i + 1) * hd] for i in range(4))
        n = iota((1, SEG0), 1)
        pos = base + seg * SEG0 + (n % plan.cseg) * plan.stride + reversed_bits(n // plan.cseg, plan.bits)
        one_hot = slide_rows(plan, pos, len_ref)
        key_f = key_features(plan, k, one_hot)
        query_f = query_features(plan, q, one_hot)
        kat[:, rows] = key_f.astype(BF16)
        ka[rows, :] = key_f.T.astype(BF16)
        qat[:, rows] = query_f.astype(BF16)
        qa0[rows, :] = query_f.T.astype(BF16)
        vat[:, rows] = value_features(plan, v).astype(BF16)
        gt[:, rows] = g.astype(BF16)
        qt[:, rows] = q.astype(BF16)
        ga0[rows, :] = jnp.concatenate([g, jnp.zeros((128 - hd, SEG0), F32)], axis=0).T.astype(BF16)
    for tile in range(plan.segs, len(plan.tiles)):
        for src, at, count in tile_pieces(plan, off_ref, chunk, tile):
            dst = slice(tile * SEG0 + at, tile * SEG0 + at + count)
            src = pl.ds(src, count)
            ka[dst, :] = ka[src, :]
            for ref in (kat, qat, vat, gt, qt):
                ref[:, dst] = ref[:, src]

    def step(tile, carry):
        rows = pl.ds(pl.multiple_of(tile * SEG0, SEG0), SEG0)
        res[rows, :] = forward_tile(plan, ka[rows, :], qat[:, rows], vat[:, rows])
        return carry

    lax.fori_loop(0, len(plan.tiles), step, 0)
    acc_ref[...] = res[0 : plan.rows, :]
    for tile in range(plan.segs, len(plan.tiles)):
        for src, at, count in tile_pieces(plan, off_ref, chunk, tile):
            rows = pl.ds(src, count)
            acc_ref[rows, :] = merged(
                plan, acc_ref[rows, :], res[tile * SEG0 + at : tile * SEG0 + at + count, :]
            )


def split3(x):
    a = x.astype(BF16).astype(F32)
    b = (x - a).astype(BF16).astype(F32)
    return a, b, x - a - b


def put_lanes(base, first, values):
    lane = iota(base.shape, 1)
    for i, v in enumerate(values):
        base = jnp.where(lane == first + i, v, base)
    return base


def backward_tile(plan, qa, kat, ga, vat, gt, qt, ka):
    p = jnp.exp2(dot(qa, kat))
    value_t = dot(gt, p.astype(BF16))
    ds = (p * dot(ga, vat)).astype(BF16)
    key_t = dot(qt, ds)
    n = key_t.shape[1]
    both = jnp.concatenate([key_t, value_t, jnp.zeros((128 - 2 * plan.hd, n), F32)], axis=0)
    return dot(ds, ka), both.T


def last_body(
    plan, chunk, l_ref, len_ref, off_ref, qa0, ga0, acc_ref,
    qa, ga, att_ref, dq_ref, near_ref, far_ref, acc, pair,
):
    hd, cdev = plan.hd, plan.cdev
    group = lax.axis_index("seq") // plan.near
    start, count = level_start(plan, off_ref, plan.levels - 1, chunk)
    rows_of = [
        pl.ds(pl.multiple_of(seg * SEG0 + start, plan.cseg), count) for seg in range(plan.segs)
    ]
    acc[...] = acc_ref[...]
    low = chunk * cdev
    x = jnp.concatenate([l_ref[d].astype(F32)[low : low + cdev] for d in range(plan.devices)], axis=0)
    xt = x.T
    head = chunk * plan.near + lax.rem(lax.axis_index("seq"), plan.near)
    n = iota((1, SEG0), 1)
    pos = n * plan.stride + off_ref[plan.levels - 1, head] % plan.stride
    kat2 = key_features(plan, xt[0:hd], slide_rows(plan, pos, len_ref))
    ka2 = kat2.T.astype(BF16)
    kat2 = kat2.astype(BF16)
    vat2 = value_features(plan, xt[hd : 2 * hd]).astype(BF16)
    q2t = jnp.concatenate([qa0[rows, :] for rows in rows_of], axis=0).astype(F32).T
    res = forward_tile(plan, ka2, q2t.astype(BF16), vat2)
    for seg, rows in enumerate(rows_of):
        acc[rows, :] = merged(plan, acc[rows, :], res[seg * count : (seg + 1) * count])
    for seg in range(plan.segs):
        rows = slice(seg * SEG0, (seg + 1) * SEG0)
        a = acc[rows, :]
        total = a[:, hd : hd + 1]
        att = jnp.where(iota(a.shape, 1) < hd, a / total, 0.0).astype(BF16)
        att_ref[rows, :] = att
        log_total = a[:, hd + 8 : hd + 9] + jnp.log2(total)
        g = ga0[rows, :].astype(F32)
        grad_dot = jnp.sum(g * att.astype(F32), axis=1, keepdims=True)
        query_f = put_lanes(qa0[rows, :].astype(F32), 2 * hd, split3(-log_total))
        qa[rows, :] = query_f.astype(BF16)
        ga[rows, :] = put_lanes(g, hd, split3(-grad_dot)).astype(BF16)
    for tile in range(plan.segs, len(plan.tiles)):
        for src, at, count1 in tile_pieces(plan, off_ref, chunk, tile):
            dst = slice(tile * SEG0 + at, tile * SEG0 + at + count1)
            qa[dst, :] = qa[pl.ds(src, count1), :]
            ga[dst, :] = ga[pl.ds(src, count1), :]
    qa2 = jnp.concatenate([qa[rows, :] for rows in rows_of], axis=0)
    ga2 = jnp.concatenate([ga[rows, :] for rows in rows_of], axis=0)
    g2t = ga2.astype(F32).T[0:hd].astype(BF16)
    q2 = (q2t[0:hd] + q2t[hd : 2 * hd]) * (1.0 / (plan.hd**-0.5 * LOG2E))
    dq, both = backward_tile(plan, qa2, kat2, ga2[:, 0:64], vat2, g2t, q2.astype(BF16), ka2)
    dq_ref[...] = dq
    pair[...] = both
    n2 = plan.last_rows
    near_ref[...] = pair[pl.ds(pl.multiple_of(group * n2, n2), n2), :]
    for s in range(1, plan.far):
        to = lax.rem(group + s, plan.far)
        far_ref[s - 1] = pair[pl.ds(pl.multiple_of(to * n2, n2), n2), :].astype(BF16)


def backward_body(
    plan, chunk, off_ref, qa, kat, ga, vat, gt, qt, ka, att_ref, dq2, near2, *rest,
):
    far_refs, (out_ref, dq, pair) = rest[: plan.far - 1], rest[plan.far - 1 :]
    hd = plan.hd

    def step(tile, carry):
        rows = pl.ds(pl.multiple_of(tile * SEG0, SEG0), SEG0)
        dq[rows, :], pair[rows, :] = backward_tile(
            plan, qa[rows, :], kat[:, rows], ga[rows, 0:64], vat[:, rows], gt[:, rows], qt[:, rows], ka[rows, :]
        )
        return carry

    lax.fori_loop(0, len(plan.tiles), step, 0)
    for tile in range(plan.segs, len(plan.tiles)):
        for src, at, count in tile_pieces(plan, off_ref, chunk, tile):
            rows = pl.ds(src, count)
            part = slice(tile * SEG0 + at, tile * SEG0 + at + count)
            dq[rows, :] = dq[rows, :] + dq[part, :]
            pair[rows, :] = pair[rows, :] + pair[part, :]
    start, count = level_start(plan, off_ref, plan.levels - 1, chunk)
    for seg in range(plan.segs):
        rows = pl.ds(pl.multiple_of(seg * SEG0 + start, plan.cseg), count)
        part = slice(seg * count, (seg + 1) * count)
        dq[rows, :] = dq[rows, :] + dq2[part, :]
        more = near2[part, :]
        for ref in far_refs:
            more = more + ref[part, :].astype(F32)
        pair[rows, :] = pair[rows, :] + more
    scale = hd**-0.5
    for src in range(plan.near):
        seg, at = src // plan.seg_dev, src % plan.seg_dev
        blocks = []
        for c in range(plan.stride):
            first = seg * SEG0 + c * plan.cseg + at * plan.cdev
            rows = slice(first, first + plan.cdev)
            blocks.append((att_ref[rows, :].astype(F32), dq[rows, :] * scale, pair[rows, :]))
        att, dqs, pairs = (jnp.concatenate(list(x), axis=0) for x in zip(*blocks))
        half = plan.half
        parts = []
        for h in range(2):
            r = slice(h * half, (h + 1) * half)
            parts += [att[r, 0:hd], dqs[r, 0:hd], pairs[r, 0:hd] * scale, pairs[r, hd : 2 * hd]]
        out_ref[src] = jnp.concatenate(parts, axis=1).astype(BF16)


def unpack_body(plan, *refs):
    ins, outs = refs[: plan.chunks], refs[plan.chunks :]
    hd = plan.hd
    order = class_of_token(plan, (plan.tok, plan.tok), 1, 0)
    for chunk in range(plan.chunks):
        got = [ins[chunk][d].astype(F32) for d in range(plan.near)]
        for i in range(4):
            halves = []
            for h in range(2):
                col = (4 * h + i) * hd
                halves.append(jnp.concatenate([x[:, col : col + hd] for x in got], axis=1))
            block = jnp.concatenate(halves, axis=0).astype(BF16)
            width = plan.near * hd
            outs[i][:, chunk * width : (chunk + 1) * width] = dot(order, block).astype(BF16)


def body(queries, keys, values, out_grad, slide_lengths, head_offsets):
    tok_rows, model_width = queries.shape
    level_count, head_count = head_offsets.shape
    device_count = lax.axis_size("seq")
    plan = Plan(tok_rows, model_width, level_count, head_count, slide_lengths.shape[0], device_count)
    near_groups = [
        list(range(i, i + plan.near)) for i in range(0, device_count, plan.near)
    ]
    sds = jax.ShapeDtypeStruct
    chunk_shape = sds((plan.near, plan.half, 8 * plan.hd), BF16)
    packed = kernel_call(
        partial(pack_body, plan),
        [chunk_shape] * plan.chunks + [sds((device_count, plan.chunks * plan.cdev, 128), BF16)],
        [VMEM] * 4 + [SMEM],
        name="pack",
    )(queries, keys, values, out_grad, head_offsets)
    swap = partial(lax.all_to_all, axis_name="seq", split_axis=0, concat_axis=0, tiled=True)
    blocks = [swap(packed[0], axis_index_groups=near_groups)]
    last = swap(packed[-1])
    blocks += [swap(x, axis_index_groups=near_groups) for x in packed[1:-1]]

    n, n3, n2 = plan.rows, plan.all_rows, plan.last_rows
    pair_flops = 2 * 128 * SEG0 * SEG0
    states = []
    for chunk in range(plan.chunks):
        ka, kat, qa0, ga0, vat, gt, qt, acc = kernel_call(
            partial(forward_body, plan, chunk),
            [
                sds((n3, 128), BF16),
                sds((128, n3), BF16),
                sds((n, 128), BF16),
                sds((n, 128), BF16),
                sds((64, n3), BF16),
                sds((plan.hd, n3), BF16),
                sds((plan.hd, n3), BF16),
                sds((n, 128), F32),
            ],
            [VMEM, SMEM, SMEM],
            [pltpu.VMEM((n, 256), F32), pltpu.VMEM((128, n3), BF16), pltpu.VMEM((n3, 128), F32)],
            flops=len(plan.tiles) * 2 * pair_flops,
            name=f"forward{chunk}",
        )(blocks[chunk], slide_lengths, head_offsets)
        qa, ga, att, dq2, near2, far2 = kernel_call(
            partial(last_body, plan, chunk),
            [
                sds((n3, 128), BF16),
                sds((n3, 128), BF16),
                sds((n, 128), BF16),
                sds((n2, 128), F32),
                sds((n2, 128), F32),
                sds((max(plan.far - 1, 1), n2, 128), BF16),
            ],
            [VMEM, SMEM, SMEM, VMEM, VMEM, VMEM],
            [pltpu.VMEM((n, 128), F32), pltpu.VMEM((SEG0, 128), F32)],
            flops=4 * pair_flops,
            name=f"last{chunk}",
        )(last, slide_lengths, head_offsets, qa0, ga0, acc)
        back = []
        for s in range(1, plan.far):
            pairs = [(i, (i + s * plan.near) % device_count) for i in range(device_count)]
            back.append(lax.ppermute(far2[s - 1], "seq", pairs))
        states.append((qa, kat, ga, vat, gt, qt, ka, att, dq2, near2, *back))
    results = []
    for chunk in range(plan.chunks):
        out = kernel_call(
            partial(backward_body, plan, chunk),
            chunk_shape,
            [SMEM] + [VMEM] * len(states[chunk]),
            [pltpu.VMEM((n3, 128), F32), pltpu.VMEM((n3, 128), F32)],
            flops=len(plan.tiles) * 5 * pair_flops,
            name=f"backward{chunk}",
        )(head_offsets, *states[chunk])
        results.append(swap(out, axis_index_groups=near_groups))
    return kernel_call(
        partial(unpack_body, plan),
        [sds((tok_rows, model_width), BF16)] * 4,
        [VMEM] * plan.chunks,
        name="unpack",
    )(*results)


def solution(mesh):
    rows = P(("groups", "seq"), None)
    return jax.shard_map(
        body,
        mesh=mesh,
        in_specs=(rows, rows, rows, rows, P("groups"), P()),
        out_specs=(rows, rows, rows, rows),
        check_vma=False,
    )
```

```python
from functools import partial
import math

import jax
import jax.numpy as jnp
from jax import lax
from jax.experimental import pallas as pl
from jax.experimental.pallas import tpu as pltpu
from jax.sharding import PartitionSpec as P

SEG0 = 1024
BIG = 2.0**100
LOG2E = math.log2(math.e)
BF16 = jnp.bfloat16
F32 = jnp.float32
VMEM_LIMIT = 36 << 20


class Plan:
    def __init__(self, tok_rows, model_width, level_count, head_count, slide_count, device_count):
        self.tok = tok_rows
        self.width = model_width
        self.levels = level_count
        self.hd = model_width // head_count
        self.slides = slide_count
        self.devices = device_count
        self.stride = device_count * tok_rows // SEG0
        self.bits = self.stride.bit_length() - 1
        self.near = min((SEG0 << (level_count - 2)) // tok_rows, device_count)
        self.far = device_count // self.near
        self.chunks = head_count // self.near
        self.segs = self.near * tok_rows // SEG0
        self.seg_dev = SEG0 // tok_rows
        self.cdev = tok_rows // self.stride
        self.cseg = SEG0 // self.stride
        self.rows = self.near * tok_rows
        self.last = self.segs * self.cseg
        self.tiles = []
        for level in range(level_count - 1):
            for first in range(0, self.segs, 1 << level):
                self.tiles.append((level, first))
        self.all_rows = len(self.tiles) * SEG0
        self.slide_pad = -(-slide_count // 8) * 8
        self.rest = 128 - 2 * self.hd - 8 - self.slide_pad
        self.aligned = self.cseg % 128 == 0
        assert self.rest >= 0 and self.hd + 16 <= 64


def reversed_bits(value, bits):
    out = value * 0
    for b in range(bits):
        out = out + ((value >> b) & 1) * (1 << (bits - 1 - b))
    return out


def dot(a, b, ca=1, cb=0, precision=None):
    return lax.dot_general(
        a, b, (((ca,), (cb,)), ((), ())), preferred_element_type=F32, precision=precision
    )


def iota(shape, axis):
    return lax.broadcasted_iota(jnp.int32, shape, axis)


def kernel_call(body, out_shape, in_specs, scratch=(), flops=0, name=None, **more):
    return pl.pallas_call(
        body,
        out_shape=out_shape,
        in_specs=in_specs,
        scratch_shapes=list(scratch),
        name=name,
        compiler_params=pltpu.CompilerParams(vmem_limit_bytes=VMEM_LIMIT),
        cost_estimate=pl.CostEstimate(flops=flops, bytes_accessed=1 << 20, transcendentals=0),
        **more,
    )


VMEM = pl.BlockSpec(memory_space=pltpu.VMEM)
SMEM = pl.BlockSpec(memory_space=pltpu.SMEM)
ANY = pl.BlockSpec(memory_space=pl.ANY)
TOKEN = jax.ShapeDtypeStruct((8, 128), F32)


def class_order(count, stride, shape, axis_row, axis_tok):
    row, tok = iota(shape, axis_row), iota(shape, axis_tok)
    size = count // stride
    want = (row % size) * stride + reversed_bits(row // size, stride.bit_length() - 1)
    return jnp.where(want == tok, 1.0, 0.0).astype(BF16)


def pack_body(plan, *refs):
    out_ref, ins = refs[-1], refs[:-1]
    order = class_order(plan.tok, plan.stride, (plan.tok, plan.tok), 0, 1)
    hd = plan.hd
    for i, ref in enumerate(ins):
        x = dot(ref[...], order, 0, 1).astype(BF16)
        for dest in range(plan.near):
            out_ref[dest, i * hd : (i + 1) * hd, :] = x[dest * hd : (dest + 1) * hd, :]


def segment_from(plan, blocks):
    if plan.cdev % 64 == 0:
        return jnp.concatenate(
            [x[:, c * plan.cdev : (c + 1) * plan.cdev] for c in range(plan.stride) for x in blocks],
            axis=1,
        )
    x = jnp.concatenate(blocks, axis=1).astype(BF16)
    return dot(x, device_lanes(plan, 1, 0))


def device_lanes(plan, axis_dev, axis_seg):
    shape = (SEG0, SEG0)
    seg, dev = iota(shape, axis_dev), iota(shape, axis_seg)
    cls, inside = seg // plan.cseg, seg % plan.cseg
    want = inside // plan.cdev * plan.tok + cls * plan.cdev + inside % plan.cdev
    return jnp.where(want == dev, 1.0, 0.0).astype(BF16)


def segment_to(plan, x):
    if plan.cdev % 64 == 0:
        return [
            jnp.concatenate(
                [
                    x[:, c * plan.cseg + d * plan.cdev : c * plan.cseg + (d + 1) * plan.cdev]
                    for c in range(plan.stride)
                ],
                axis=1,
            )
            for d in range(plan.seg_dev)
        ]
    x = dot(x.astype(BF16), device_lanes(plan, 0, 1))
    return [x[:, d * plan.tok : (d + 1) * plan.tok] for d in range(plan.seg_dev)]


def slide_rows(plan, pos, len_ref):
    slide = jnp.zeros(pos.shape, jnp.int32)
    end = 0
    for i in range(plan.slides):
        end = end + len_ref[i]
        slide = slide + jnp.where(pos >= end, 1, 0)
    shape = (plan.slide_pad, pos.shape[1])
    return jnp.where(iota(shape, 0) == slide, 1.0, 0.0)


def key_features(plan, k, one_hot):
    n = k.shape[1]
    return jnp.concatenate(
        [k, k, jnp.ones((8, n), F32), one_hot, jnp.zeros((plan.rest, n), F32)], axis=0
    )


def query_features(plan, q, one_hot):
    n = q.shape[1]
    q = q * (plan.hd**-0.5 * LOG2E)
    high = q.astype(BF16).astype(F32)
    mask = (one_hot - 1.0) * BIG
    return jnp.concatenate(
        [high, q - high, jnp.zeros((8, n), F32), mask, jnp.zeros((plan.rest, n), F32)], axis=0
    )


def value_features(plan, v):
    n = v.shape[1]
    return jnp.concatenate([v, jnp.ones((8, n), F32), jnp.zeros((56 - plan.hd, n), F32)], axis=0)


def three_rows(x):
    a = x.astype(BF16).astype(F32)
    b = (x - a).astype(BF16).astype(F32)
    row = iota((8, x.shape[1]), 0)
    return jnp.where(row == 0, a, jnp.where(row == 1, b, jnp.where(row == 2, x - a - b, 0.0)))


def forward_tile(plan, keys, queries_t, values_t):
    s = dot(keys, queries_t)
    peak = jnp.max(s, axis=0, keepdims=True)
    p = jnp.exp2(s - peak).astype(BF16)
    o = dot(values_t, p)
    return jnp.concatenate(
        [o[: plan.hd + 8], jnp.broadcast_to(peak, (56 - plan.hd, o.shape[1]))], axis=0
    )


def merged(plan, a, b):
    at = plan.hd + 8
    peak_a, peak_b = a[at : at + 1], b[at : at + 1]
    peak = jnp.maximum(peak_a, peak_b)
    both = a[:at] * jnp.exp2(peak_a - peak) + b[:at] * jnp.exp2(peak_b - peak)
    return jnp.concatenate([both, jnp.broadcast_to(peak, (64 - at, a.shape[1]))], axis=0)


def backward_tile(plan, qa, kat, ga, vat, gt, qt):
    p = jnp.exp2(dot(qa, kat))
    value_t = dot(gt, p.astype(BF16))
    ds = (p * dot(ga, vat)).astype(BF16)
    key_t = dot(qt, ds)
    return dot(kat[: plan.hd], ds, 1, 1), key_t, value_t


def level_start(plan, off_ref, level, chunk):
    head = chunk * plan.near + lax.rem(lax.axis_index("seq"), plan.near)
    bits = level if level < plan.levels - 1 else plan.bits
    rows = SEG0 >> bits
    return reversed_bits(off_ref[level, head] % (1 << bits), bits) * rows, rows


def tile_pieces(plan, off_ref, chunk, tile):
    level, first = plan.tiles[tile]
    start, rows = level_start(plan, off_ref, level, chunk)
    out = []
    for i in range(1 << level):
        src = pl.ds(pl.multiple_of((first + i) * SEG0 + start, 128), rows)
        out.append((src, slice(tile * SEG0 + i * rows, tile * SEG0 + (i + 1) * rows)))
    return out


def last_slices(plan, off_ref, chunk):
    start, count = level_start(plan, off_ref, plan.levels - 1, chunk)
    return [
        pl.ds(pl.multiple_of(seg * SEG0 + start, plan.cseg), count) for seg in range(plan.segs)
    ]


def last_places(plan, off_ref, chunk, shape, axis_seg, axis_last):
    start, _ = level_start(plan, off_ref, plan.levels - 1, chunk)
    hit = iota(shape, axis_seg) == start + iota(shape, axis_last)
    return jnp.where(hit, 1.0, 0.0)


def last_lanes(plan, off_ref, chunk, ref):
    if plan.aligned:
        return jnp.concatenate([ref[:, s] for s in last_slices(plan, off_ref, chunk)], axis=1)
    place = last_places(plan, off_ref, chunk, (SEG0, plan.cseg), 0, 1)
    exact = lax.Precision.HIGHEST
    parts = [
        dot(ref[:, g * SEG0 : (g + 1) * SEG0].astype(F32), place, precision=exact)
        for g in range(plan.segs)
    ]
    return jnp.concatenate(parts, axis=1).astype(ref.dtype)


def last_update(plan, off_ref, chunk, ref, rows, part, update, fill):
    if plan.aligned:
        for seg, s in enumerate(last_slices(plan, off_ref, chunk)):
            ref[rows, s] = update(ref[rows, s], part[:, seg * plan.cseg : (seg + 1) * plan.cseg])
        return
    place = last_places(plan, off_ref, chunk, (plan.cseg, SEG0), 1, 0)
    hit = jnp.max(place, axis=0, keepdims=True) > 0
    for seg in range(plan.segs):
        own = part[:, seg * plan.cseg : (seg + 1) * plan.cseg]
        own = jnp.where(hit, dot(own, place, precision=lax.Precision.HIGHEST), fill)
        s = slice(seg * SEG0, (seg + 1) * SEG0)
        ref[rows, s] = update(ref[rows, s], own)


def no_level(plan):
    return jnp.where(iota((64, 1), 0) >= plan.hd + 8, -BIG, 0.0)


def segment_of(plan, x_ref, first, count, seg):
    return segment_from(
        plan,
        [
            x_ref[seg * plan.seg_dev + d, first : first + count * plan.hd, :].astype(F32)
            for d in range(plan.seg_dev)
        ],
    )


def segment_slides(plan, seg, len_ref):
    base = lax.axis_index("seq") // plan.near * plan.rows + seg * SEG0
    n = iota((1, SEG0), 1)
    pos = base + (n % plan.cseg) * plan.stride + reversed_bits(n // plan.cseg, plan.bits)
    return slide_rows(plan, pos, len_ref)


def forward_body(
    plan, chunk, first, x_ref, len_ref, off_ref, tok_in, acc_ref, q2, kv2, tok_out, ka, qat, vat, raw, res
):
    hd = plan.hd
    tok_out[...] = jnp.zeros_like(tok_out)
    for seg in range(plan.segs):
        rows = slice(seg * SEG0, (seg + 1) * SEG0)
        xt = segment_of(plan, x_ref, first, 3, seg)
        raw[:, rows] = xt.astype(BF16)
        q, k, v = (xt[i * hd : (i + 1) * hd] for i in range(3))
        one_hot = segment_slides(plan, seg, len_ref)
        ka[rows, :] = key_features(plan, k, one_hot).T.astype(BF16)
        qat[:, rows] = query_features(plan, q, one_hot).astype(BF16)
        vat[:, rows] = value_features(plan, v).astype(BF16)
    for tile in range(plan.segs, len(plan.tiles)):
        for src, dst in tile_pieces(plan, off_ref, chunk, tile):
            ka[dst, :] = ka[src, :]
            for ref in (qat, vat):
                ref[:, dst] = ref[:, src]
    last = last_lanes(plan, off_ref, chunk, raw)
    q2[...] = last[0:hd]
    kv2[...] = last[hd:]

    def step(tile, carry):
        rows = pl.ds(pl.multiple_of(tile * SEG0, SEG0), SEG0)
        res[:, rows] = forward_tile(plan, ka[rows, :], qat[:, rows], vat[:, rows])
        return carry

    lax.fori_loop(0, len(plan.tiles), step, 0)
    acc_ref[...] = res[:, 0 : plan.rows]
    for tile in range(plan.segs, len(plan.tiles)):
        for src, dst in tile_pieces(plan, off_ref, chunk, tile):
            acc_ref[:, src] = merged(plan, acc_ref[:, src], res[:, dst])


def last_body(plan, chunk, first, g_ref, len_ref, off_ref, tok_in, acc_ref, q2, kv2, *rest):
    far_in, (att_ref, ld_ref, grad_ref, far_ref, tok_out, acc, gt) = (
        rest[: plan.far - 1],
        rest[plan.far - 1 :],
    )
    hd = plan.hd
    tok_out[...] = jnp.zeros_like(tok_out)
    group = lax.axis_index("seq") // plan.near
    head = chunk * plan.near + lax.rem(lax.axis_index("seq"), plan.near)
    acc[...] = acc_ref[...]
    x = jnp.concatenate([ref[...].astype(F32) for ref in (kv2,) + far_in], axis=1)
    n = iota((1, SEG0), 1)
    owner = group - n // plan.last
    owner = jnp.where(owner < 0, owner + plan.far, owner)
    pos = owner * plan.rows + (n % plan.last) * plan.stride + off_ref[plan.levels - 1, head] % plan.stride
    one_hot = slide_rows(plan, pos, len_ref)
    key_f = key_features(plan, x[0:hd], one_hot)
    query_f = query_features(plan, q2[...].astype(F32), one_hot[:, 0 : plan.last])
    vat2 = value_features(plan, x[hd : 2 * hd]).astype(BF16)
    res = forward_tile(plan, key_f.T.astype(BF16), query_f.astype(BF16), vat2)
    last_update(plan, off_ref, chunk, acc, slice(None), res, partial(merged, plan), no_level(plan))
    for seg in range(plan.segs):
        rows = slice(seg * SEG0, (seg + 1) * SEG0)
        a = acc[:, rows]
        total = a[hd : hd + 1]
        att = (a[0:hd] / total).astype(BF16)
        att_ref[:, rows] = att
        log_total = a[hd + 8 : hd + 9] + jnp.log2(total)
        g = segment_of(plan, g_ref, first, 1, seg)
        gt[:, rows] = g.astype(BF16)
        grad_dot = jnp.sum(g * att.astype(F32), axis=0, keepdims=True)
        ld_ref[:, rows] = jnp.where(iota((8, SEG0), 0) == 0, log_total, grad_dot)
    g2 = last_lanes(plan, off_ref, chunk, gt)
    ld2 = last_lanes(plan, off_ref, chunk, ld_ref)
    qa2, ga2 = backward_queries(plan, query_f, g2.astype(F32), ld2)
    dq, dk, dv = backward_tile(plan, qa2, key_f.astype(BF16), ga2[:, 0:64], vat2, g2, q2[...])
    grad_ref[...] = jnp.concatenate(
        [dq, dk[:, 0 : plan.last], dv[:, 0 : plan.last]], axis=0
    )
    both = jnp.concatenate([dk, dv], axis=0)
    for s in range(1, plan.far):
        far_ref[s - 1] = both[:, s * plan.last : (s + 1) * plan.last].astype(BF16)


def backward_queries(plan, query_f, g, ld):
    hd = plan.hd
    query_f = jnp.concatenate(
        [query_f[0 : 2 * hd], three_rows(-ld[0:1]), query_f[2 * hd + 8 :]], axis=0
    )
    grad_f = jnp.concatenate(
        [g, three_rows(-ld[1:2]), jnp.zeros((120 - hd, g.shape[1]), F32)], axis=0
    )
    return query_f.T.astype(BF16), grad_f.T.astype(BF16)


def backward_body(plan, chunk, places, atts, x_ref, g_ref, len_ref, off_ref, tok_in, *refs):
    att_refs, refs = refs[:atts], refs[atts:]
    (ld_ref, grad2), refs = refs[:2], refs[2:]
    far_refs, refs = refs[: plan.far - 1], refs[plan.far - 1 :]
    out_ref, tok_out, qa, kat, ga, vat, gt, qt, grads = refs
    hd = plan.hd
    tok_out[...] = jnp.zeros_like(tok_out)
    for seg in range(plan.segs):
        rows = slice(seg * SEG0, (seg + 1) * SEG0)
        xt = segment_of(plan, x_ref, places[0], 3, seg)
        q, k, v = (xt[i * hd : (i + 1) * hd] for i in range(3))
        g = segment_of(plan, g_ref, places[1], 1, seg)
        one_hot = segment_slides(plan, seg, len_ref)
        kat[:, rows] = key_features(plan, k, one_hot).astype(BF16)
        vat[:, rows] = value_features(plan, v).astype(BF16)
        qt[:, rows] = q.astype(BF16)
        gt[:, rows] = g.astype(BF16)
        qa[rows, :], ga[rows, :] = backward_queries(
            plan, query_features(plan, q, one_hot), g, ld_ref[:, rows]
        )
    for tile in range(plan.segs, len(plan.tiles)):
        for src, dst in tile_pieces(plan, off_ref, chunk, tile):
            qa[dst, :] = qa[src, :]
            ga[dst, :] = ga[src, :]
            for ref in (kat, vat, gt, qt):
                ref[:, dst] = ref[:, src]

    def step(tile, carry):
        rows = pl.ds(pl.multiple_of(tile * SEG0, SEG0), SEG0)
        parts = backward_tile(
            plan, qa[rows, :], kat[:, rows], ga[rows, 0:64], vat[:, rows], gt[:, rows], qt[:, rows]
        )
        for i, part in enumerate(parts):
            grads[i * hd : (i + 1) * hd, rows] = part
        return carry

    lax.fori_loop(0, len(plan.tiles), step, 0)
    for tile in range(plan.segs, len(plan.tiles)):
        for src, dst in tile_pieces(plan, off_ref, chunk, tile):
            grads[:, src] = grads[:, src] + grads[:, dst]
    more = grad2[...]
    if far_refs:
        far = sum(ref[...].astype(F32) for ref in far_refs)
        more = jnp.concatenate([more[0:hd], more[hd:] + far], axis=0)
    last_update(plan, off_ref, chunk, grads, slice(None), more, jnp.add, 0.0)
    scale = hd**-0.5
    for seg in range(plan.segs):
        rows = slice(seg * SEG0, (seg + 1) * SEG0)
        parts = [ref[:, rows].astype(F32) for ref in att_refs]
        parts += [grads[0 : 2 * hd, rows] * scale, grads[2 * hd : 3 * hd, rows]]
        for d, x in enumerate(segment_to(plan, jnp.concatenate(parts, axis=0))):
            out_ref[seg * plan.seg_dev + d] = x.astype(BF16)


def unpack_body(plan, places, y_ref, *refs):
    outs = refs[-len(places) :]
    hd, width = plan.hd, plan.near * plan.hd
    order = class_order(plan.tok, plan.stride, (plan.tok, plan.tok), 1, 0)
    for out_ref, first in zip(outs, places):
        for col in range(out_ref.shape[1] // width):
            i = first + col
            x = jnp.concatenate([y_ref[d, i * hd : (i + 1) * hd, :] for d in range(plan.near)], axis=0)
            out_ref[:, col * width : (col + 1) * width] = dot(order, x, 1, 1).astype(BF16)


def body(queries, keys, values, out_grad, slide_lengths, head_offsets):
    tok_rows, model_width = queries.shape
    level_count, head_count = head_offsets.shape
    device_count = lax.axis_size("seq")
    plan = Plan(tok_rows, model_width, level_count, head_count, slide_lengths.shape[0], device_count)
    hd, chunks = plan.hd, plan.chunks
    groups = [list(range(i, i + plan.near)) for i in range(0, device_count, plan.near)]
    sds = jax.ShapeDtypeStruct
    swap = partial(
        lax.all_to_all, axis_name="seq", split_axis=0, concat_axis=0, tiled=True, axis_index_groups=groups
    )

    def shifted(x, steps):
        shift = steps * plan.near
        return lax.ppermute(x, "seq", [(i, (i + shift) % device_count) for i in range(device_count)])

    exchanges = [[(c, i) for i in range(3)] for c in range(chunks)]
    for c in range(chunks):
        exchanges[min(c + 1, chunks - 1)].append((c, 3))
    arrays = (queries, keys, values, out_grad)
    width = plan.near * hd
    received, where = [], {}
    for pieces in exchanges:
        packed = kernel_call(
            partial(pack_body, plan),
            sds((plan.near, len(pieces) * hd, plan.tok), BF16),
            [pl.BlockSpec((plan.tok, width), lambda i, c=c: (0, c)) for c, _ in pieces],
            name="pack",
            grid=(1,),
            out_specs=pl.BlockSpec((plan.near, len(pieces) * hd, plan.tok), lambda i: (0, 0, 0)),
        )(*(arrays[i] for _, i in pieces))
        for place, piece in enumerate(pieces):
            where[piece] = (len(received), place * hd)
        received.append(swap(packed))

    n, n3, n2 = plan.rows, plan.all_rows, plan.last
    pair_flops = 20 * 2 * 128 * SEG0 * SEG0
    scalars = (slide_lengths, head_offsets)
    token = jnp.zeros(TOKEN.shape, TOKEN.dtype)
    fronts = []
    for chunk in range(chunks):
        source, first = where[chunk, 0]
        acc, q2, kv2, token = kernel_call(
            partial(forward_body, plan, chunk, first),
            [sds((64, n), F32), sds((hd, n2), BF16), sds((2 * hd, n2), BF16), TOKEN],
            [VMEM, SMEM, SMEM, ANY],
            [
                pltpu.VMEM((n3, 128), BF16),
                pltpu.VMEM((128, n3), BF16),
                pltpu.VMEM((64, n3), BF16),
                pltpu.VMEM((3 * hd, n), BF16),
                pltpu.VMEM((64, n3), F32),
            ],
            flops=len(plan.tiles) * 2 * pair_flops,
            name=f"forward{chunk}",
        )(received[source], *scalars, token)
        fronts.append((acc, q2, kv2, *(shifted(kv2, s) for s in range(1, plan.far))))
    states = []
    for chunk, front in enumerate(fronts):
        source, first = where[chunk, 3]
        att, ld, grad2, far2, token = kernel_call(
            partial(last_body, plan, chunk, first),
            [
                sds((hd, n), BF16),
                sds((8, n), F32),
                sds((3 * hd, n2), F32),
                sds((max(plan.far - 1, 1), 2 * hd, n2), BF16),
                TOKEN,
            ],
            [VMEM, SMEM, SMEM, ANY] + [VMEM] * len(front),
            [pltpu.VMEM((64, n), F32), pltpu.VMEM((hd, n), BF16)],
            flops=4 * pair_flops,
            name=f"last{chunk}",
        )(received[source], *scalars, token, *front)
        states.append((att, (ld, grad2, *(shifted(far2[s - 1], -s) for s in range(1, plan.far)))))
    for chunk, (_, state) in enumerate(states):
        atts = [s[0] for s in states] if chunk == 0 else []
        count = len(atts) + 3
        sources = [where[chunk, 0], where[chunk, 3]]
        out, token = kernel_call(
            partial(backward_body, plan, chunk, [first for _, first in sources], len(atts)),
            [sds((plan.near, count * hd, plan.tok), BF16), TOKEN],
            [VMEM, VMEM, SMEM, SMEM, ANY] + [VMEM] * (len(atts) + len(state)),
            [
                pltpu.VMEM((n3, 128), BF16),
                pltpu.VMEM((128, n3), BF16),
                pltpu.VMEM((n3, 128), BF16),
                pltpu.VMEM((64, n3), BF16),
                pltpu.VMEM((hd, n3), BF16),
                pltpu.VMEM((hd, n3), BF16),
                pltpu.VMEM((3 * hd, n3), F32),
            ],
            flops=len(plan.tiles) * 5 * pair_flops,
            name=f"backward{chunk}",
        )(*(received[source] for source, _ in sources), *scalars, token, *atts, *state)
        y = swap(out)
        full = sds((tok_rows, model_width), BF16)
        whole = pl.BlockSpec(out.shape, lambda i: (0, 0, 0))
        column = pl.BlockSpec((tok_rows, width), lambda i, c=chunk: (0, c))
        if chunk == 0:
            attended, *outs = kernel_call(
                partial(unpack_body, plan, [0] + [chunks + i for i in range(3)]),
                [full] * 4,
                [whole],
                name="unpack",
                grid=(1,),
                out_specs=[pl.BlockSpec(full.shape, lambda i: (0, 0))] + [column] * 3,
            )(y)
        else:
            outs = kernel_call(
                partial(unpack_body, plan, list(range(3))),
                [full] * 3,
                [whole] + [ANY] * 3,
                name="unpack",
                grid=(1,),
                out_specs=[column] * 3,
                input_output_aliases={1: 0, 2: 1, 3: 2},
            )(y, *outs)
    return (attended, *outs)


def solution(mesh):
    rows = P(("groups", "seq"), None)
    return jax.shard_map(
        body,
        mesh=mesh,
        in_specs=(rows, rows, rows, rows, P("groups"), P()),
        out_specs=(rows, rows, rows, rows),
        check_vma=False,
    )
```

```python
from functools import partial
import math

import jax
import jax.numpy as jnp
from jax import lax
from jax.experimental import pallas as pl
from jax.experimental.pallas import tpu as pltpu
from jax.sharding import PartitionSpec as P

SEG0 = 1024
BIG = 2.0**100
LOG2E = math.log2(math.e)
BF16 = jnp.bfloat16
F32 = jnp.float32
VMEM_LIMIT = 36 << 20
PACK_LIMIT = 63 << 20


class Plan:
    def __init__(self, tok_rows, model_width, level_count, head_count, slide_count, device_count):
        self.tok = tok_rows
        self.width = model_width
        self.levels = level_count
        self.hd = model_width // head_count
        self.slides = slide_count
        self.devices = device_count
        self.stride = device_count * tok_rows // SEG0
        self.bits = self.stride.bit_length() - 1
        self.near = min((SEG0 << (level_count - 2)) // tok_rows, device_count)
        self.far = device_count // self.near
        self.chunks = head_count // self.near
        self.segs = self.near * tok_rows // SEG0
        self.seg_dev = SEG0 // tok_rows
        self.cdev = tok_rows // self.stride
        self.cseg = SEG0 // self.stride
        self.rows = self.near * tok_rows
        self.last = self.segs * self.cseg
        self.tiles = []
        for level in range(level_count - 1):
            for first in range(0, self.segs, 1 << level):
                self.tiles.append((level, first))
        self.all_rows = len(self.tiles) * SEG0
        self.slide_pad = -(-slide_count // 8) * 8
        self.rest = 128 - 2 * self.hd - 8 - self.slide_pad
        self.aligned = self.cseg % 128 == 0
        assert self.rest >= 0 and self.hd + 16 <= 64 and self.hd % 16 == 0


def reversed_bits(value, bits):
    out = value * 0
    for b in range(bits):
        out = out + ((value >> b) & 1) * (1 << (bits - 1 - b))
    return out


def dot(a, b, ca=1, cb=0, precision=None):
    return lax.dot_general(
        a, b, (((ca,), (cb,)), ((), ())), preferred_element_type=F32, precision=precision
    )


def iota(shape, axis):
    return lax.broadcasted_iota(jnp.int32, shape, axis)


def kernel_call(body, out_shape, in_specs, scratch=(), flops=0, name=None, limit=VMEM_LIMIT, **more):
    return pl.pallas_call(
        body,
        out_shape=out_shape,
        in_specs=in_specs,
        scratch_shapes=list(scratch),
        name=name,
        compiler_params=pltpu.CompilerParams(vmem_limit_bytes=limit),
        cost_estimate=pl.CostEstimate(flops=flops, bytes_accessed=1 << 20, transcendentals=0),
        **more,
    )


VMEM = pl.BlockSpec(memory_space=pltpu.VMEM)
SMEM = pl.BlockSpec(memory_space=pltpu.SMEM)
ANY = pl.BlockSpec(memory_space=pl.ANY)
TOKEN = jax.ShapeDtypeStruct((8, 128), F32)


def class_order(count, stride, shape, axis_row, axis_tok):
    row, tok = iota(shape, axis_row), iota(shape, axis_tok)
    size = count // stride
    want = (row % size) * stride + reversed_bits(row // size, stride.bit_length() - 1)
    return jnp.where(want == tok, 1.0, 0.0).astype(BF16)


def near_index(plan):
    return lax.rem(lax.axis_index("seq"), plan.near)


def pack_body(plan, columns, count_out, *refs):
    count = len(columns)
    ins, outs, (tok_out, rows, turned, sems) = refs[:count], refs[-4 - count_out : -4], refs[-4:]
    tok_out[...] = jnp.zeros_like(tok_out)
    hd, width = plan.hd, plan.near * plan.hd
    copies = [
        pltpu.make_async_copy(ref.at[:, c * width : (c + 1) * width], rows.at[i], sems.at[i])
        for i, (ref, c) in enumerate(zip(ins, columns))
    ]
    for copy in copies:
        copy.start()
    order = class_order(plan.tok, plan.stride, (plan.tok, plan.tok), 0, 1)
    me = near_index(plan)
    for i, copy in enumerate(copies):
        copy.wait()
        turned[...] = dot(rows[i], order, 0, 1).astype(BF16)
        for j in range(plan.near):
            if len(outs) == 1:
                outs[0][j, i * hd : (i + 1) * hd, :] = turned[j * hd : (j + 1) * hd, :]
            else:
                first = pl.multiple_of((me ^ j) * hd, 16)
                outs[j][i * hd : (i + 1) * hd, :] = turned[pl.ds(first, hd), :]


def segment_from(plan, blocks):
    if plan.cdev % 64 == 0:
        return jnp.concatenate(
            [x[:, c * plan.cdev : (c + 1) * plan.cdev] for c in range(plan.stride) for x in blocks],
            axis=1,
        )
    x = jnp.concatenate(blocks, axis=1).astype(BF16)
    return dot(x, device_lanes(plan, 1, 0))


def device_lanes(plan, axis_dev, axis_seg):
    shape = (SEG0, SEG0)
    seg, dev = iota(shape, axis_dev), iota(shape, axis_seg)
    cls, inside = seg // plan.cseg, seg % plan.cseg
    want = inside // plan.cdev * plan.tok + cls * plan.cdev + inside % plan.cdev
    return jnp.where(want == dev, 1.0, 0.0).astype(BF16)


def segment_to(plan, x):
    if plan.cdev % 64 == 0:
        return [
            jnp.concatenate(
                [
                    x[:, c * plan.cseg + d * plan.cdev : c * plan.cseg + (d + 1) * plan.cdev]
                    for c in range(plan.stride)
                ],
                axis=1,
            )
            for d in range(plan.seg_dev)
        ]
    x = dot(x.astype(BF16), device_lanes(plan, 0, 1))
    return [x[:, d * plan.tok : (d + 1) * plan.tok] for d in range(plan.seg_dev)]


def slide_rows(plan, pos, len_ref):
    slide = jnp.zeros(pos.shape, jnp.int32)
    end = 0
    for i in range(plan.slides):
        end = end + len_ref[i]
        slide = slide + jnp.where(pos >= end, 1, 0)
    shape = (plan.slide_pad, pos.shape[1])
    return jnp.where(iota(shape, 0) == slide, 1.0, 0.0)


def key_features(plan, k, one_hot):
    n = k.shape[1]
    return jnp.concatenate(
        [k, k, jnp.ones((8, n), F32), one_hot, jnp.zeros((plan.rest, n), F32)], axis=0
    )


def query_features(plan, q, one_hot):
    n = q.shape[1]
    q = q * (plan.hd**-0.5 * LOG2E)
    high = q.astype(BF16).astype(F32)
    mask = (one_hot - 1.0) * BIG
    return jnp.concatenate(
        [high, q - high, jnp.zeros((8, n), F32), mask, jnp.zeros((plan.rest, n), F32)], axis=0
    )


def value_features(plan, v):
    n = v.shape[1]
    return jnp.concatenate([v, jnp.ones((8, n), F32), jnp.zeros((56 - plan.hd, n), F32)], axis=0)


def three_rows(x):
    a = x.astype(BF16).astype(F32)
    b = (x - a).astype(BF16).astype(F32)
    row = iota((8, x.shape[1]), 0)
    return jnp.where(row == 0, a, jnp.where(row == 1, b, jnp.where(row == 2, x - a - b, 0.0)))


def forward_tile(plan, keys, queries_t, values_t):
    s = dot(keys, queries_t)
    peak = jnp.max(s, axis=0, keepdims=True)
    p = jnp.exp2(s - peak).astype(BF16)
    o = dot(values_t, p)
    return jnp.concatenate(
        [o[: plan.hd + 8], jnp.broadcast_to(peak, (56 - plan.hd, o.shape[1]))], axis=0
    )


def merged(plan, a, b):
    at = plan.hd + 8
    peak_a, peak_b = a[at : at + 1], b[at : at + 1]
    peak = jnp.maximum(peak_a, peak_b)
    both = a[:at] * jnp.exp2(peak_a - peak) + b[:at] * jnp.exp2(peak_b - peak)
    return jnp.concatenate([both, jnp.broadcast_to(peak, (64 - at, a.shape[1]))], axis=0)


def backward_tile(plan, qa, kat, ga, vat, gt, qt):
    p = jnp.exp2(dot(qa, kat))
    value_t = dot(gt, p.astype(BF16))
    ds = (p * dot(ga, vat)).astype(BF16)
    key_t = dot(qt, ds)
    return dot(kat[: plan.hd], ds, 1, 1), key_t, value_t


def level_start(plan, off_ref, level, chunk):
    head = chunk * plan.near + lax.rem(lax.axis_index("seq"), plan.near)
    bits = level if level < plan.levels - 1 else plan.bits
    rows = SEG0 >> bits
    return reversed_bits(off_ref[level, head] % (1 << bits), bits) * rows, rows


def tile_pieces(plan, off_ref, chunk, tile):
    level, first = plan.tiles[tile]
    start, rows = level_start(plan, off_ref, level, chunk)
    out = []
    for i in range(1 << level):
        src = pl.ds(pl.multiple_of((first + i) * SEG0 + start, 128), rows)
        out.append((src, slice(tile * SEG0 + i * rows, tile * SEG0 + (i + 1) * rows)))
    return out


def last_slices(plan, off_ref, chunk):
    start, count = level_start(plan, off_ref, plan.levels - 1, chunk)
    return [
        pl.ds(pl.multiple_of(seg * SEG0 + start, plan.cseg), count) for seg in range(plan.segs)
    ]


def last_places(plan, off_ref, chunk, shape, axis_seg, axis_last):
    start, _ = level_start(plan, off_ref, plan.levels - 1, chunk)
    hit = iota(shape, axis_seg) == start + iota(shape, axis_last)
    return jnp.where(hit, 1.0, 0.0)


def last_lanes(plan, off_ref, chunk, ref):
    if plan.aligned:
        return jnp.concatenate([ref[:, s] for s in last_slices(plan, off_ref, chunk)], axis=1)
    place = last_places(plan, off_ref, chunk, (SEG0, plan.cseg), 0, 1)
    exact = lax.Precision.HIGHEST
    parts = [
        dot(ref[:, g * SEG0 : (g + 1) * SEG0].astype(F32), place, precision=exact)
        for g in range(plan.segs)
    ]
    return jnp.concatenate(parts, axis=1).astype(ref.dtype)


def last_update(plan, off_ref, chunk, ref, rows, part, update, fill):
    if plan.aligned:
        for seg, s in enumerate(last_slices(plan, off_ref, chunk)):
            ref[rows, s] = update(ref[rows, s], part[:, seg * plan.cseg : (seg + 1) * plan.cseg])
        return
    place = last_places(plan, off_ref, chunk, (plan.cseg, SEG0), 1, 0)
    hit = jnp.max(place, axis=0, keepdims=True) > 0
    for seg in range(plan.segs):
        own = part[:, seg * plan.cseg : (seg + 1) * plan.cseg]
        own = jnp.where(hit, dot(own, place, precision=lax.Precision.HIGHEST), fill)
        s = slice(seg * SEG0, (seg + 1) * SEG0)
        ref[rows, s] = update(ref[rows, s], own)


def no_level(plan):
    return jnp.where(iota((64, 1), 0) >= plan.hd + 8, -BIG, 0.0)


def slots_of(plan, refs):
    if len(refs) > 1:
        return refs
    return [refs[0].at[near_index(plan) ^ j] for j in range(plan.near)]


def segment_of(plan, slots, first, count, seg):
    return segment_from(
        plan,
        [
            slots[seg * plan.seg_dev + d][first : first + count * plan.hd, :].astype(F32)
            for d in range(plan.seg_dev)
        ],
    )


def slot_tokens(plan, seg, slot, inside):
    me = near_index(plan)
    seg = (me // plan.seg_dev) ^ seg
    return seg * SEG0 + (lax.rem(me, plan.seg_dev) ^ slot) * plan.tok + inside


def segment_slides(plan, seg, len_ref):
    n = iota((1, SEG0), 1)
    inside = (n % plan.cdev) * plan.stride + reversed_bits(n // plan.cseg, plan.bits)
    pos = slot_tokens(plan, seg, n % plan.cseg // plan.cdev, inside)
    return slide_rows(plan, lax.axis_index("seq") // plan.near * plan.rows + pos, len_ref)


def forward_body(
    plan, chunk, first, blocks, len_ref, off_ref, tok_in, *refs
):
    acc_ref, q2, kv2, tok_out, ka, qat, vat, raw, res = refs[blocks:]
    slots = slots_of(plan, refs[:blocks])
    hd = plan.hd
    tok_out[...] = jnp.zeros_like(tok_out)
    for seg in range(plan.segs):
        rows = slice(seg * SEG0, (seg + 1) * SEG0)
        xt = segment_of(plan, slots, first, 3, seg)
        raw[:, rows] = xt.astype(BF16)
        q, k, v = (xt[i * hd : (i + 1) * hd] for i in range(3))
        one_hot = segment_slides(plan, seg, len_ref)
        ka[rows, :] = key_features(plan, k, one_hot).T.astype(BF16)
        qat[:, rows] = query_features(plan, q, one_hot).astype(BF16)
        vat[:, rows] = value_features(plan, v).astype(BF16)
    for tile in range(plan.segs, len(plan.tiles)):
        for src, dst in tile_pieces(plan, off_ref, chunk, tile):
            ka[dst, :] = ka[src, :]
            for ref in (qat, vat):
                ref[:, dst] = ref[:, src]
    last = last_lanes(plan, off_ref, chunk, raw)
    q2[...] = last[0:hd]
    kv2[...] = last[hd:]

    def step(tile, carry):
        rows = pl.ds(pl.multiple_of(tile * SEG0, SEG0), SEG0)
        res[:, rows] = forward_tile(plan, ka[rows, :], qat[:, rows], vat[:, rows])
        return carry

    lax.fori_loop(0, len(plan.tiles), step, 0)
    acc_ref[...] = res[:, 0 : plan.rows]
    for tile in range(plan.segs, len(plan.tiles)):
        for src, dst in tile_pieces(plan, off_ref, chunk, tile):
            acc_ref[:, src] = merged(plan, acc_ref[:, src], res[:, dst])


def last_body(plan, chunk, first, blocks, len_ref, off_ref, tok_in, acc_ref, q2, kv2, *rest):
    slots, rest = slots_of(plan, rest[:blocks]), rest[blocks:]
    far_in, (att_ref, ld_ref, grad_ref, far_ref, tok_out, acc, gt) = (
        rest[: plan.far - 1],
        rest[plan.far - 1 :],
    )
    hd = plan.hd
    tok_out[...] = jnp.zeros_like(tok_out)
    group = lax.axis_index("seq") // plan.near
    head = chunk * plan.near + lax.rem(lax.axis_index("seq"), plan.near)
    acc[...] = acc_ref[...]
    x = jnp.concatenate([ref[...].astype(F32) for ref in (kv2,) + far_in], axis=1)
    n = iota((1, SEG0), 1)
    owner = group - n // plan.last
    owner = jnp.where(owner < 0, owner + plan.far, owner)
    inside = (n % plan.cdev) * plan.stride + off_ref[plan.levels - 1, head] % plan.stride
    seg, slot = n % plan.last // plan.cseg, n % plan.cseg // plan.cdev
    pos = owner * plan.rows + slot_tokens(plan, seg, slot, inside)
    one_hot = slide_rows(plan, pos, len_ref)
    key_f = key_features(plan, x[0:hd], one_hot)
    query_f = query_features(plan, q2[...].astype(F32), one_hot[:, 0 : plan.last])
    vat2 = value_features(plan, x[hd : 2 * hd]).astype(BF16)
    res = forward_tile(plan, key_f.T.astype(BF16), query_f.astype(BF16), vat2)
    last_update(plan, off_ref, chunk, acc, slice(None), res, partial(merged, plan), no_level(plan))
    for seg in range(plan.segs):
        rows = slice(seg * SEG0, (seg + 1) * SEG0)
        a = acc[:, rows]
        total = a[hd : hd + 1]
        att = (a[0:hd] / total).astype(BF16)
        att_ref[:, rows] = att
        log_total = a[hd + 8 : hd + 9] + jnp.log2(total)
        g = segment_of(plan, slots, first, 1, seg)
        gt[:, rows] = g.astype(BF16)
        grad_dot = jnp.sum(g * att.astype(F32), axis=0, keepdims=True)
        ld_ref[:, rows] = jnp.where(iota((8, SEG0), 0) == 0, log_total, grad_dot)
    g2 = last_lanes(plan, off_ref, chunk, gt)
    ld2 = last_lanes(plan, off_ref, chunk, ld_ref)
    qa2, ga2 = backward_queries(plan, query_f, g2.astype(F32), ld2)
    dq, dk, dv = backward_tile(plan, qa2, key_f.astype(BF16), ga2[:, 0:64], vat2, g2, q2[...])
    grad_ref[...] = jnp.concatenate(
        [dq, dk[:, 0 : plan.last], dv[:, 0 : plan.last]], axis=0
    )
    both = jnp.concatenate([dk, dv], axis=0)
    for s in range(1, plan.far):
        far_ref[s - 1] = both[:, s * plan.last : (s + 1) * plan.last].astype(BF16)


def backward_queries(plan, query_f, g, ld):
    hd = plan.hd
    query_f = jnp.concatenate(
        [query_f[0 : 2 * hd], three_rows(-ld[0:1]), query_f[2 * hd + 8 :]], axis=0
    )
    grad_f = jnp.concatenate(
        [g, three_rows(-ld[1:2]), jnp.zeros((120 - hd, g.shape[1]), F32)], axis=0
    )
    return query_f.T.astype(BF16), grad_f.T.astype(BF16)


def backward_body(plan, chunk, places, blocks, atts, slotted, len_ref, off_ref, tok_in, *refs):
    slots, refs = slots_of(plan, refs[: blocks[0]]), refs[blocks[0] :]
    g_slots, refs = slots_of(plan, refs[: blocks[1]]), refs[blocks[1] :]
    att_refs, refs = refs[:atts], refs[atts:]
    (ld_ref, grad2), refs = refs[:2], refs[2:]
    far_refs, refs = refs[: plan.far - 1], refs[plan.far - 1 :]
    outs, (tok_out, qa, kat, ga, vat, gt, qt, grads) = refs[:-8], refs[-8:]
    hd = plan.hd
    tok_out[...] = jnp.zeros_like(tok_out)
    for seg in range(plan.segs):
        rows = slice(seg * SEG0, (seg + 1) * SEG0)
        xt = segment_of(plan, slots, places[0], 3, seg)
        q, k, v = (xt[i * hd : (i + 1) * hd] for i in range(3))
        g = segment_of(plan, g_slots, places[1], 1, seg)
        one_hot = segment_slides(plan, seg, len_ref)
        kat[:, rows] = key_features(plan, k, one_hot).astype(BF16)
        vat[:, rows] = value_features(plan, v).astype(BF16)
        qt[:, rows] = q.astype(BF16)
        gt[:, rows] = g.astype(BF16)
        qa[rows, :], ga[rows, :] = backward_queries(
            plan, query_features(plan, q, one_hot), g, ld_ref[:, rows]
        )
    for tile in range(plan.segs, len(plan.tiles)):
        for src, dst in tile_pieces(plan, off_ref, chunk, tile):
            qa[dst, :] = qa[src, :]
            ga[dst, :] = ga[src, :]
            for ref in (kat, vat, gt, qt):
                ref[:, dst] = ref[:, src]

    def step(tile, carry):
        rows = pl.ds(pl.multiple_of(tile * SEG0, SEG0), SEG0)
        parts = backward_tile(
            plan, qa[rows, :], kat[:, rows], ga[rows, 0:64], vat[:, rows], gt[:, rows], qt[:, rows]
        )
        for i, part in enumerate(parts):
            grads[i * hd : (i + 1) * hd, rows] = part
        return carry

    lax.fori_loop(0, len(plan.tiles), step, 0)
    for tile in range(plan.segs, len(plan.tiles)):
        for src, dst in tile_pieces(plan, off_ref, chunk, tile):
            grads[:, src] = grads[:, src] + grads[:, dst]
    more = grad2[...]
    if far_refs:
        far = sum(ref[...].astype(F32) for ref in far_refs)
        more = jnp.concatenate([more[0:hd], more[hd:] + far], axis=0)
    last_update(plan, off_ref, chunk, grads, slice(None), more, jnp.add, 0.0)
    scale = hd**-0.5
    for seg in range(plan.segs):
        rows = slice(seg * SEG0, (seg + 1) * SEG0)
        parts = [ref[:, rows].astype(F32) for ref in att_refs]
        parts += [grads[0 : 2 * hd, rows] * scale, grads[2 * hd : 3 * hd, rows]]
        for d, x in enumerate(segment_to(plan, jnp.concatenate(parts, axis=0))):
            slot = seg * plan.seg_dev + d
            if slotted:
                outs[slot][...] = x.astype(BF16)
            else:
                outs[0][near_index(plan) ^ slot] = x.astype(BF16)


def unpack_body(plan, places, slotted, *refs):
    if slotted:
        y_ref, outs = refs[-1], refs[-1 - len(places) : -1]
        for j in range(plan.near):
            y_ref[near_index(plan) ^ j] = refs[j][...]
    else:
        y_ref, outs = refs[0], refs[-len(places) :]
    hd, width = plan.hd, plan.near * plan.hd
    order = class_order(plan.tok, plan.stride, (plan.tok, plan.tok), 1, 0)
    for out_ref, first in zip(outs, places):
        for col in range(out_ref.shape[1] // width):
            i = first + col
            x = jnp.concatenate([y_ref[d, i * hd : (i + 1) * hd, :] for d in range(plan.near)], axis=0)
            out_ref[:, col * width : (col + 1) * width] = dot(order, x, 1, 1).astype(BF16)


def body(queries, keys, values, out_grad, slide_lengths, head_offsets):
    tok_rows, model_width = queries.shape
    level_count, head_count = head_offsets.shape
    device_count = lax.axis_size("seq")
    plan = Plan(tok_rows, model_width, level_count, head_count, slide_lengths.shape[0], device_count)
    hd, chunks = plan.hd, plan.chunks
    groups = [list(range(i, i + plan.near)) for i in range(0, device_count, plan.near)]
    sds = jax.ShapeDtypeStruct
    near = plan.near

    def permuted(x, target):
        return lax.ppermute(x, "seq", [(i, target(i)) for i in range(device_count)])

    def swap(x):
        return lax.all_to_all(x, "seq", 0, 0, tiled=True, axis_index_groups=groups)

    def shifted(x, steps):
        return permuted(x, lambda i: (i + steps * near) % device_count)

    def traded(slots):
        return [slots[0]] + [permuted(slots[j], lambda i, j=j: i ^ j) for j in range(near - 1, 0, -1)][::-1]

    exchanges = [[(c, i) for i in range(3)] for c in range(chunks)]
    for c in range(chunks):
        exchanges[min(c + 1, chunks - 1)].append((c, 3))
    arrays = (queries, keys, values, out_grad)
    width = near * hd
    received, where = [], {}
    token = ()
    for pieces in exchanges:
        slotted = len(received) > 0
        block = (len(pieces) * hd, tok_rows)
        *packed, tok = kernel_call(
            partial(pack_body, plan, [c for c, _ in pieces], near if slotted else 1),
            ([sds(block, BF16)] * near if slotted else [sds((near,) + block, BF16)]) + [TOKEN],
            [ANY] * (len(pieces) + len(token)),
            [
                pltpu.VMEM((len(pieces), tok_rows, width), BF16),
                pltpu.VMEM((width, tok_rows), BF16),
                pltpu.SemaphoreType.DMA((len(pieces),)),
            ],
            name="pack",
            limit=PACK_LIMIT,
        )(*(arrays[i] for _, i in pieces), *token)
        token = (tok,)
        for place, piece in enumerate(pieces):
            where[piece] = (len(received), place * hd)
        received.append(traded(packed) if slotted else [swap(packed[0])])

    n, n3, n2 = plan.rows, plan.all_rows, plan.last
    pair_flops = 20 * 2 * 128 * SEG0 * SEG0
    scalars = (slide_lengths, head_offsets)
    (token,) = token
    fronts = []
    for chunk in range(chunks):
        source, first = where[chunk, 0]
        acc, q2, kv2, token = kernel_call(
            partial(forward_body, plan, chunk, first, len(received[source])),
            [sds((64, n), F32), sds((hd, n2), BF16), sds((2 * hd, n2), BF16), TOKEN],
            [SMEM, SMEM, ANY] + [VMEM] * len(received[source]),
            [
                pltpu.VMEM((n3, 128), BF16),
                pltpu.VMEM((128, n3), BF16),
                pltpu.VMEM((64, n3), BF16),
                pltpu.VMEM((3 * hd, n), BF16),
                pltpu.VMEM((64, n3), F32),
            ],
            name=f"forward{chunk}",
        )(*scalars, token, *received[source])
        fronts.append((acc, q2, kv2, *(shifted(kv2, s) for s in range(1, plan.far))))
    states = []
    for chunk, front in enumerate(fronts):
        source, first = where[chunk, 3]
        att, ld, grad2, far2, token = kernel_call(
            partial(last_body, plan, chunk, first, len(received[source])),
            [
                sds((hd, n), BF16),
                sds((8, n), F32),
                sds((3 * hd, n2), F32),
                sds((max(plan.far - 1, 1), 2 * hd, n2), BF16),
                TOKEN,
            ],
            [SMEM, SMEM, ANY] + [VMEM] * (len(front) + len(received[source])),
            [pltpu.VMEM((64, n), F32), pltpu.VMEM((hd, n), BF16)],
            flops=4 * pair_flops,
            name=f"last{chunk}",
        )(*scalars, token, *front[:3], *received[source], *front[3:])
        states.append((att, (ld, grad2, *(shifted(far2[s - 1], -s) for s in range(1, plan.far)))))
    full = sds((tok_rows, model_width), BF16)
    for chunk, (_, state) in enumerate(states):
        atts = [s[0] for s in states] if chunk == 0 else []
        slotted = chunk == chunks - 1
        count = len(atts) + 3
        sources = [where[chunk, 0], where[chunk, 3]]
        blocks = [len(received[x[0]]) for x in sources]
        block = sds((count * hd, tok_rows), BF16)
        *out, token = kernel_call(
            partial(
                backward_body, plan, chunk, [x[1] for x in sources], blocks, len(atts), slotted
            ),
            ([block] * near if slotted else [sds((near,) + block.shape, BF16)]) + [TOKEN],
            [SMEM, SMEM, ANY] + [VMEM] * (sum(blocks) + len(atts) + len(state)),
            [
                pltpu.VMEM((n3, 128), BF16),
                pltpu.VMEM((128, n3), BF16),
                pltpu.VMEM((n3, 128), BF16),
                pltpu.VMEM((64, n3), BF16),
                pltpu.VMEM((hd, n3), BF16),
                pltpu.VMEM((hd, n3), BF16),
                pltpu.VMEM((3 * hd, n3), F32),
            ],
            flops=len(plan.tiles) * 5 * pair_flops,
            name=f"backward{chunk}",
        )(*scalars, token, *received[sources[0][0]], *received[sources[1][0]], *atts, *state)
        y = traded(out) if slotted else [swap(out[0])]
        scratch = [pltpu.VMEM((near,) + block.shape, BF16)] if slotted else []
        column = pl.BlockSpec((tok_rows, width), lambda i, c=chunk: (0, c))
        specs = [pl.BlockSpec(v.shape, lambda i, r=len(v.shape): (0,) * r) for v in y]
        if chunk == 0:
            attended, *outs = kernel_call(
                partial(unpack_body, plan, [0] + [chunks + i for i in range(3)], slotted),
                [full] * 4,
                specs,
                scratch,
                name="unpack",
                grid=(1,),
                out_specs=[pl.BlockSpec(full.shape, lambda i: (0, 0))] + [column] * 3,
            )(*y)
        else:
            outs = kernel_call(
                partial(unpack_body, plan, list(range(3)), slotted),
                [full] * 3,
                specs + [ANY] * 3,
                scratch,
                name="unpack",
                grid=(1,),
                out_specs=[column] * 3,
                input_output_aliases={len(y) + i: i for i in range(3)},
            )(*y, *outs)
    return (attended, *outs)


def solution(mesh):
    rows = P(("groups", "seq"), None)
    return jax.shard_map(
        body,
        mesh=mesh,
        in_specs=(rows, rows, rows, rows, P("groups"), P()),
        out_specs=(rows, rows, rows, rows),
        check_vma=False,
    )
```

```python
from functools import partial
import math

import jax
import jax.numpy as jnp
from jax import lax
from jax.experimental import pallas as pl
from jax.experimental.pallas import tpu as pltpu
from jax.sharding import PartitionSpec as P

SEG0 = 1024
BIG = 2.0**100
LOG2E = math.log2(math.e)
BF16 = jnp.bfloat16
F32 = jnp.float32
VMEM_LIMIT = 36 << 20
PACK_LIMIT = 63 << 20


class Plan:
    def __init__(self, tok_rows, model_width, level_count, head_count, slide_count, device_count):
        self.tok = tok_rows
        self.width = model_width
        self.levels = level_count
        self.hd = model_width // head_count
        self.slides = slide_count
        self.devices = device_count
        self.stride = device_count * tok_rows // SEG0
        self.bits = self.stride.bit_length() - 1
        self.near = min((SEG0 << (level_count - 2)) // tok_rows, device_count)
        self.far = device_count // self.near
        self.chunks = head_count // self.near
        self.segs = self.near * tok_rows // SEG0
        self.seg_dev = SEG0 // tok_rows
        self.cdev = tok_rows // self.stride
        self.cseg = SEG0 // self.stride
        self.rows = self.near * tok_rows
        self.last = self.segs * self.cseg
        self.tiles = []
        for level in range(level_count - 1):
            for first in range(0, self.segs, 1 << level):
                self.tiles.append((level, first))
        self.all_rows = len(self.tiles) * SEG0
        self.slide_pad = -(-slide_count // 8) * 8
        self.rest = 128 - 2 * self.hd - 8 - self.slide_pad
        self.aligned = self.cseg % 128 == 0
        assert self.rest >= 0 and self.hd + 16 <= 64 and self.hd % 16 == 0


def reversed_bits(value, bits):
    out = value * 0
    for b in range(bits):
        out = out + ((value >> b) & 1) * (1 << (bits - 1 - b))
    return out


def dot(a, b, ca=1, cb=0, precision=None):
    return lax.dot_general(
        a, b, (((ca,), (cb,)), ((), ())), preferred_element_type=F32, precision=precision
    )


def iota(shape, axis):
    return lax.broadcasted_iota(jnp.int32, shape, axis)


def kernel_call(body, out_shape, in_specs, scratch=(), flops=0, name=None, limit=VMEM_LIMIT, **more):
    return pl.pallas_call(
        body,
        out_shape=out_shape,
        in_specs=in_specs,
        scratch_shapes=list(scratch),
        name=name,
        compiler_params=pltpu.CompilerParams(vmem_limit_bytes=limit),
        cost_estimate=pl.CostEstimate(flops=flops, bytes_accessed=1 << 20, transcendentals=0),
        **more,
    )


VMEM = pl.BlockSpec(memory_space=pltpu.VMEM)
SMEM = pl.BlockSpec(memory_space=pltpu.SMEM)
ANY = pl.BlockSpec(memory_space=pl.ANY)
TOKEN = jax.ShapeDtypeStruct((8, 128), F32)


def class_order(count, stride, shape, axis_row, axis_tok):
    row, tok = iota(shape, axis_row), iota(shape, axis_tok)
    size = count // stride
    want = (row % size) * stride + reversed_bits(row // size, stride.bit_length() - 1)
    return jnp.where(want == tok, 1.0, 0.0).astype(BF16)


def near_index(plan):
    return lax.rem(lax.axis_index("seq"), plan.near)


def pack_body(plan, columns, count_out, *refs):
    count = len(columns)
    ins, outs, (tok_out, rows, turned, sems) = refs[:count], refs[-4 - count_out : -4], refs[-4:]
    tok_out[...] = jnp.zeros_like(tok_out)
    hd, width = plan.hd, plan.near * plan.hd
    copies = [
        pltpu.make_async_copy(ref.at[:, c * width : (c + 1) * width], rows.at[i], sems.at[i])
        for i, (ref, c) in enumerate(zip(ins, columns))
    ]
    for copy in copies:
        copy.start()
    order = class_order(plan.tok, plan.stride, (plan.tok, plan.tok), 0, 1)
    me = near_index(plan)
    for i, copy in enumerate(copies):
        copy.wait()
        turned[...] = dot(rows[i], order, 0, 1).astype(BF16)
        for j in range(plan.near):
            if len(outs) == 1:
                outs[0][j, i * hd : (i + 1) * hd, :] = turned[j * hd : (j + 1) * hd, :]
            else:
                first = pl.multiple_of((me ^ j) * hd, 16)
                outs[j][i * hd : (i + 1) * hd, :] = turned[pl.ds(first, hd), :]


def segment_from(plan, blocks):
    if plan.cdev % 64 == 0:
        return jnp.concatenate(
            [x[:, c * plan.cdev : (c + 1) * plan.cdev] for c in range(plan.stride) for x in blocks],
            axis=1,
        )
    x = jnp.concatenate(blocks, axis=1).astype(BF16)
    return dot(x, device_lanes(plan, 1, 0))


def device_lanes(plan, axis_dev, axis_seg):
    shape = (SEG0, SEG0)
    seg, dev = iota(shape, axis_dev), iota(shape, axis_seg)
    cls, inside = seg // plan.cseg, seg % plan.cseg
    want = inside // plan.cdev * plan.tok + cls * plan.cdev + inside % plan.cdev
    return jnp.where(want == dev, 1.0, 0.0).astype(BF16)


def segment_to(plan, x):
    if plan.cdev % 64 == 0:
        return [
            jnp.concatenate(
                [
                    x[:, c * plan.cseg + d * plan.cdev : c * plan.cseg + (d + 1) * plan.cdev]
                    for c in range(plan.stride)
                ],
                axis=1,
            )
            for d in range(plan.seg_dev)
        ]
    x = dot(x.astype(BF16), device_lanes(plan, 0, 1))
    return [x[:, d * plan.tok : (d + 1) * plan.tok] for d in range(plan.seg_dev)]


def slide_rows(plan, pos, len_ref):
    slide = jnp.zeros(pos.shape, jnp.int32)
    end = 0
    for i in range(plan.slides):
        end = end + len_ref[i]
        slide = slide + jnp.where(pos >= end, 1, 0)
    shape = (plan.slide_pad, pos.shape[1])
    return jnp.where(iota(shape, 0) == slide, 1.0, 0.0)


def key_features(plan, k, one_hot):
    n = k.shape[1]
    return jnp.concatenate(
        [k, k, jnp.ones((8, n), F32), one_hot, jnp.zeros((plan.rest, n), F32)], axis=0
    )


def query_features(plan, q, one_hot):
    n = q.shape[1]
    q = q * (plan.hd**-0.5 * LOG2E)
    high = q.astype(BF16).astype(F32)
    mask = (one_hot - 1.0) * BIG
    return jnp.concatenate(
        [high, q - high, jnp.zeros((8, n), F32), mask, jnp.zeros((plan.rest, n), F32)], axis=0
    )


def value_features(plan, v):
    n = v.shape[1]
    return jnp.concatenate([v, jnp.ones((8, n), F32), jnp.zeros((56 - plan.hd, n), F32)], axis=0)


def three_rows(x):
    a = x.astype(BF16).astype(F32)
    b = (x - a).astype(BF16).astype(F32)
    row = iota((8, x.shape[1]), 0)
    return jnp.where(row == 0, a, jnp.where(row == 1, b, jnp.where(row == 2, x - a - b, 0.0)))


def forward_tile(plan, s, values_t):
    peak = jnp.max(s, axis=0, keepdims=True)
    p = jnp.exp2(s - peak).astype(BF16)
    o = dot(values_t, p)
    return jnp.concatenate(
        [o[: plan.hd + 8], jnp.broadcast_to(peak, (56 - plan.hd, o.shape[1]))], axis=0
    )


def merged(plan, a, b):
    at = plan.hd + 8
    peak_a, peak_b = a[at : at + 1], b[at : at + 1]
    peak = jnp.maximum(peak_a, peak_b)
    both = a[:at] * jnp.exp2(peak_a - peak) + b[:at] * jnp.exp2(peak_b - peak)
    return jnp.concatenate([both, jnp.broadcast_to(peak, (64 - at, a.shape[1]))], axis=0)


def backward_tile(plan, qa, kat, ga, vat, gt, qt):
    n = qa.shape[0]
    step = min(n, SEG0 // 2)
    parts = [slice(i, i + step) for i in range(0, n, step)]
    weights = []
    for rows in parts:
        dp = dot(ga[rows], vat)
        p = jnp.exp2(dot(qa[rows], kat))
        weights.append((p.astype(BF16), (p * dp).astype(BF16)))
    query_t = [dot(kat[: plan.hd], ds, 1, 1) for _, ds in weights]
    key_t = sum(dot(qt[:, rows], ds) for rows, (_, ds) in zip(parts, weights))
    value_t = sum(dot(gt[:, rows], p) for rows, (p, _) in zip(parts, weights))
    return jnp.concatenate(query_t, axis=1), key_t, value_t


def level_start(plan, off_ref, level, chunk):
    head = chunk * plan.near + lax.rem(lax.axis_index("seq"), plan.near)
    bits = level if level < plan.levels - 1 else plan.bits
    rows = SEG0 >> bits
    return reversed_bits(off_ref[level, head] % (1 << bits), bits) * rows, rows


def tile_pieces(plan, off_ref, chunk, tile):
    level, first = plan.tiles[tile]
    start, rows = level_start(plan, off_ref, level, chunk)
    out = []
    for i in range(1 << level):
        src = pl.ds(pl.multiple_of((first + i) * SEG0 + start, 128), rows)
        out.append((src, slice(tile * SEG0 + i * rows, tile * SEG0 + (i + 1) * rows)))
    return out


def last_slices(plan, off_ref, chunk):
    start, count = level_start(plan, off_ref, plan.levels - 1, chunk)
    return [
        pl.ds(pl.multiple_of(seg * SEG0 + start, plan.cseg), count) for seg in range(plan.segs)
    ]


def last_places(plan, off_ref, chunk, shape, axis_seg, axis_last):
    start, _ = level_start(plan, off_ref, plan.levels - 1, chunk)
    hit = iota(shape, axis_seg) == start + iota(shape, axis_last)
    return jnp.where(hit, 1.0, 0.0)


def last_lanes(plan, off_ref, chunk, ref):
    if plan.aligned:
        return jnp.concatenate([ref[:, s] for s in last_slices(plan, off_ref, chunk)], axis=1)
    place = last_places(plan, off_ref, chunk, (SEG0, plan.cseg), 0, 1)
    exact = lax.Precision.HIGHEST
    parts = [
        dot(ref[:, g * SEG0 : (g + 1) * SEG0].astype(F32), place, precision=exact)
        for g in range(plan.segs)
    ]
    return jnp.concatenate(parts, axis=1).astype(ref.dtype)


def last_update(plan, off_ref, chunk, ref, rows, part, update, fill):
    if plan.aligned:
        for seg, s in enumerate(last_slices(plan, off_ref, chunk)):
            ref[rows, s] = update(ref[rows, s], part[:, seg * plan.cseg : (seg + 1) * plan.cseg])
        return
    place = last_places(plan, off_ref, chunk, (plan.cseg, SEG0), 1, 0)
    hit = jnp.max(place, axis=0, keepdims=True) > 0
    for seg in range(plan.segs):
        own = part[:, seg * plan.cseg : (seg + 1) * plan.cseg]
        own = jnp.where(hit, dot(own, place, precision=lax.Precision.HIGHEST), fill)
        s = slice(seg * SEG0, (seg + 1) * SEG0)
        ref[rows, s] = update(ref[rows, s], own)


def no_level(plan):
    return jnp.where(iota((64, 1), 0) >= plan.hd + 8, -BIG, 0.0)


def slots_of(plan, refs):
    if len(refs) > 1:
        return refs
    return [refs[0].at[near_index(plan) ^ j] for j in range(plan.near)]


def segment_of(plan, slots, first, count, seg):
    return segment_from(
        plan,
        [
            slots[seg * plan.seg_dev + d][first : first + count * plan.hd, :].astype(F32)
            for d in range(plan.seg_dev)
        ],
    )


def slot_tokens(plan, seg, slot, inside):
    me = near_index(plan)
    seg = (me // plan.seg_dev) ^ seg
    return seg * SEG0 + (lax.rem(me, plan.seg_dev) ^ slot) * plan.tok + inside


def segment_slides(plan, seg, len_ref):
    n = iota((1, SEG0), 1)
    inside = (n % plan.cdev) * plan.stride + reversed_bits(n // plan.cseg, plan.bits)
    pos = slot_tokens(plan, seg, n % plan.cseg // plan.cdev, inside)
    return slide_rows(plan, lax.axis_index("seq") // plan.near * plan.rows + pos, len_ref)


def forward_body(
    plan, chunk, first, blocks, len_ref, off_ref, tok_in, *refs
):
    acc_ref, q2, kv2, tok_out, ka, qat, vat, raw, res = refs[blocks:]
    slots = slots_of(plan, refs[:blocks])
    hd = plan.hd
    tok_out[...] = jnp.zeros_like(tok_out)
    for seg in range(plan.segs):
        rows = slice(seg * SEG0, (seg + 1) * SEG0)
        xt = segment_of(plan, slots, first, 3, seg)
        raw[:, rows] = xt.astype(BF16)
        q, k, v = (xt[i * hd : (i + 1) * hd] for i in range(3))
        one_hot = segment_slides(plan, seg, len_ref)
        ka[rows, :] = key_features(plan, k, one_hot).T.astype(BF16)
        qat[:, rows] = query_features(plan, q, one_hot).astype(BF16)
        vat[:, rows] = value_features(plan, v).astype(BF16)
    for tile in range(plan.segs, len(plan.tiles)):
        for src, dst in tile_pieces(plan, off_ref, chunk, tile):
            ka[dst, :] = ka[src, :]
            for ref in (qat, vat):
                ref[:, dst] = ref[:, src]
    last = last_lanes(plan, off_ref, chunk, raw)
    q2[...] = last[0:hd]
    kv2[...] = last[hd:]

    tiles = [slice(t * SEG0, (t + 1) * SEG0) for t in range(len(plan.tiles))]
    scores = [dot(ka[rows, :], qat[:, rows]) for rows in tiles]
    for s, rows in zip(scores, tiles):
        res[:, rows] = forward_tile(plan, s, vat[:, rows])
    acc_ref[...] = res[:, 0 : plan.rows]
    for tile in range(plan.segs, len(plan.tiles)):
        for src, dst in tile_pieces(plan, off_ref, chunk, tile):
            acc_ref[:, src] = merged(plan, acc_ref[:, src], res[:, dst])


def last_body(plan, chunk, first, blocks, len_ref, off_ref, tok_in, acc_ref, q2, kv2, *rest):
    slots, rest = slots_of(plan, rest[:blocks]), rest[blocks:]
    far_in, (att_ref, ld_ref, grad_ref, far_ref, tok_out, acc, gt) = (
        rest[: plan.far - 1],
        rest[plan.far - 1 :],
    )
    hd = plan.hd
    tok_out[...] = jnp.zeros_like(tok_out)
    group = lax.axis_index("seq") // plan.near
    head = chunk * plan.near + lax.rem(lax.axis_index("seq"), plan.near)
    acc[...] = acc_ref[...]
    x = jnp.concatenate([ref[...].astype(F32) for ref in (kv2,) + far_in], axis=1)
    n = iota((1, SEG0), 1)
    owner = group - n // plan.last
    owner = jnp.where(owner < 0, owner + plan.far, owner)
    inside = (n % plan.cdev) * plan.stride + off_ref[plan.levels - 1, head] % plan.stride
    seg, slot = n % plan.last // plan.cseg, n % plan.cseg // plan.cdev
    pos = owner * plan.rows + slot_tokens(plan, seg, slot, inside)
    one_hot = slide_rows(plan, pos, len_ref)
    key_f = key_features(plan, x[0:hd], one_hot)
    query_f = query_features(plan, q2[...].astype(F32), one_hot[:, 0 : plan.last])
    vat2 = value_features(plan, x[hd : 2 * hd]).astype(BF16)
    res = forward_tile(plan, dot(key_f.T.astype(BF16), query_f.astype(BF16)), vat2)
    last_update(plan, off_ref, chunk, acc, slice(None), res, partial(merged, plan), no_level(plan))
    for seg in range(plan.segs):
        rows = slice(seg * SEG0, (seg + 1) * SEG0)
        a = acc[:, rows]
        total = a[hd : hd + 1]
        att = (a[0:hd] / total).astype(BF16)
        att_ref[:, rows] = att
        log_total = a[hd + 8 : hd + 9] + jnp.log2(total)
        g = segment_of(plan, slots, first, 1, seg)
        gt[:, rows] = g.astype(BF16)
        grad_dot = jnp.sum(g * att.astype(F32), axis=0, keepdims=True)
        ld_ref[:, rows] = jnp.where(iota((8, SEG0), 0) == 0, log_total, grad_dot)
    g2 = last_lanes(plan, off_ref, chunk, gt)
    ld2 = last_lanes(plan, off_ref, chunk, ld_ref)
    qa2, ga2 = backward_queries(plan, query_f, g2.astype(F32), ld2)
    dq, dk, dv = backward_tile(plan, qa2, key_f.astype(BF16), ga2[:, 0:64], vat2, g2, q2[...])
    grad_ref[...] = jnp.concatenate(
        [dq, dk[:, 0 : plan.last], dv[:, 0 : plan.last]], axis=0
    )
    both = jnp.concatenate([dk, dv], axis=0)
    for s in range(1, plan.far):
        far_ref[s - 1] = both[:, s * plan.last : (s + 1) * plan.last].astype(BF16)


def backward_queries(plan, query_f, g, ld):
    hd = plan.hd
    query_f = jnp.concatenate(
        [query_f[0 : 2 * hd], three_rows(-ld[0:1]), query_f[2 * hd + 8 :]], axis=0
    )
    grad_f = jnp.concatenate(
        [g, three_rows(-ld[1:2]), jnp.zeros((120 - hd, g.shape[1]), F32)], axis=0
    )
    return query_f.T.astype(BF16), grad_f.T.astype(BF16)


def backward_body(plan, chunk, places, blocks, atts, slotted, len_ref, off_ref, tok_in, *refs):
    slots, refs = slots_of(plan, refs[: blocks[0]]), refs[blocks[0] :]
    g_slots, refs = slots_of(plan, refs[: blocks[1]]), refs[blocks[1] :]
    att_refs, refs = refs[:atts], refs[atts:]
    (ld_ref, grad2), refs = refs[:2], refs[2:]
    far_refs, refs = refs[: plan.far - 1], refs[plan.far - 1 :]
    outs, (tok_out, qa, kat, ga, vat, gt, qt, grads) = refs[:-8], refs[-8:]
    hd = plan.hd
    tok_out[...] = jnp.zeros_like(tok_out)
    for seg in range(plan.segs):
        rows = slice(seg * SEG0, (seg + 1) * SEG0)
        xt = segment_of(plan, slots, places[0], 3, seg)
        q, k, v = (xt[i * hd : (i + 1) * hd] for i in range(3))
        g = segment_of(plan, g_slots, places[1], 1, seg)
        one_hot = segment_slides(plan, seg, len_ref)
        kat[:, rows] = key_features(plan, k, one_hot).astype(BF16)
        vat[:, rows] = value_features(plan, v).astype(BF16)
        qt[:, rows] = q.astype(BF16)
        gt[:, rows] = g.astype(BF16)
        qa[rows, :], ga[rows, :] = backward_queries(
            plan, query_features(plan, q, one_hot), g, ld_ref[:, rows]
        )
    for tile in range(plan.segs, len(plan.tiles)):
        for src, dst in tile_pieces(plan, off_ref, chunk, tile):
            qa[dst, :] = qa[src, :]
            ga[dst, :] = ga[src, :]
            for ref in (kat, vat, gt, qt):
                ref[:, dst] = ref[:, src]

    for tile in range(len(plan.tiles)):
        rows = slice(tile * SEG0, (tile + 1) * SEG0)
        parts = backward_tile(
            plan, qa[rows, :], kat[:, rows], ga[rows, 0:64], vat[:, rows], gt[:, rows], qt[:, rows]
        )
        if tile < plan.segs:
            for i, part in enumerate(parts):
                grads[i * hd : (i + 1) * hd, rows] = part
            continue
        for src, dst in tile_pieces(plan, off_ref, chunk, tile):
            at = slice(dst.start - rows.start, dst.stop - rows.start)
            for i, part in enumerate(parts):
                own = slice(i * hd, (i + 1) * hd)
                grads[own, src] = grads[own, src] + part[:, at]
    more = grad2[...]
    if far_refs:
        far = sum(ref[...].astype(F32) for ref in far_refs)
        more = jnp.concatenate([more[0:hd], more[hd:] + far], axis=0)
    last_update(plan, off_ref, chunk, grads, slice(None), more, jnp.add, 0.0)
    scale = hd**-0.5
    for seg in range(plan.segs):
        rows = slice(seg * SEG0, (seg + 1) * SEG0)
        parts = [ref[:, rows].astype(F32) for ref in att_refs]
        parts += [grads[0 : 2 * hd, rows] * scale, grads[2 * hd : 3 * hd, rows]]
        for d, x in enumerate(segment_to(plan, jnp.concatenate(parts, axis=0))):
            slot = seg * plan.seg_dev + d
            if slotted:
                outs[slot][...] = x.astype(BF16)
            else:
                outs[0][near_index(plan) ^ slot] = x.astype(BF16)


def unpack_body(plan, places, slotted, *refs):
    if slotted:
        y_ref, outs = refs[-1], refs[-1 - len(places) : -1]
        for j in range(plan.near):
            y_ref[near_index(plan) ^ j] = refs[j][...]
    else:
        y_ref, outs = refs[0], refs[-len(places) :]
    hd, width = plan.hd, plan.near * plan.hd
    order = class_order(plan.tok, plan.stride, (plan.tok, plan.tok), 1, 0)
    for out_ref, first in zip(outs, places):
        for col in range(out_ref.shape[1] // width):
            i = first + col
            x = jnp.concatenate([y_ref[d, i * hd : (i + 1) * hd, :] for d in range(plan.near)], axis=0)
            out_ref[:, col * width : (col + 1) * width] = dot(order, x, 1, 1).astype(BF16)


def body(queries, keys, values, out_grad, slide_lengths, head_offsets):
    tok_rows, model_width = queries.shape
    level_count, head_count = head_offsets.shape
    device_count = lax.axis_size("seq")
    plan = Plan(tok_rows, model_width, level_count, head_count, slide_lengths.shape[0], device_count)
    hd, chunks = plan.hd, plan.chunks
    groups = [list(range(i, i + plan.near)) for i in range(0, device_count, plan.near)]
    sds = jax.ShapeDtypeStruct
    near = plan.near

    def permuted(x, target):
        return lax.ppermute(x, "seq", [(i, target(i)) for i in range(device_count)])

    def swap(x):
        return lax.all_to_all(x, "seq", 0, 0, tiled=True, axis_index_groups=groups)

    def shifted(x, steps):
        return permuted(x, lambda i: (i + steps * near) % device_count)

    def traded(slots):
        return [slots[0]] + [permuted(slots[j], lambda i, j=j: i ^ j) for j in range(near - 1, 0, -1)][::-1]

    exchanges = [[(c, i) for i in range(3)] for c in range(chunks)]
    for c in range(chunks):
        exchanges[min(c + 1, chunks - 1)].append((c, 3))
    arrays = (queries, keys, values, out_grad)
    width = near * hd
    received, where = [], {}
    token = ()
    for pieces in exchanges:
        slotted = len(received) > 0
        block = (len(pieces) * hd, tok_rows)
        *packed, tok = kernel_call(
            partial(pack_body, plan, [c for c, _ in pieces], near if slotted else 1),
            ([sds(block, BF16)] * near if slotted else [sds((near,) + block, BF16)]) + [TOKEN],
            [ANY] * (len(pieces) + len(token)),
            [
                pltpu.VMEM((len(pieces), tok_rows, width), BF16),
                pltpu.VMEM((width, tok_rows), BF16),
                pltpu.SemaphoreType.DMA((len(pieces),)),
            ],
            name="pack",
            limit=PACK_LIMIT,
        )(*(arrays[i] for _, i in pieces), *token)
        token = (tok,)
        for place, piece in enumerate(pieces):
            where[piece] = (len(received), place * hd)
        received.append(traded(packed) if slotted else [swap(packed[0])])

    n, n3, n2 = plan.rows, plan.all_rows, plan.last
    pair_flops = 20 * 2 * 128 * SEG0 * SEG0
    scalars = (slide_lengths, head_offsets)
    (token,) = token
    fronts = []
    for chunk in range(chunks):
        source, first = where[chunk, 0]
        acc, q2, kv2, token = kernel_call(
            partial(forward_body, plan, chunk, first, len(received[source])),
            [sds((64, n), F32), sds((hd, n2), BF16), sds((2 * hd, n2), BF16), TOKEN],
            [SMEM, SMEM, ANY] + [VMEM] * len(received[source]),
            [
                pltpu.VMEM((n3, 128), BF16),
                pltpu.VMEM((128, n3), BF16),
                pltpu.VMEM((64, n3), BF16),
                pltpu.VMEM((3 * hd, n), BF16),
                pltpu.VMEM((64, n3), F32),
            ],
            name=f"forward{chunk}",
        )(*scalars, token, *received[source])
        fronts.append((acc, q2, kv2, *(shifted(kv2, s) for s in range(1, plan.far))))
    states = []
    for chunk, front in enumerate(fronts):
        source, first = where[chunk, 3]
        att, ld, grad2, far2, token = kernel_call(
            partial(last_body, plan, chunk, first, len(received[source])),
            [
                sds((hd, n), BF16),
                sds((8, n), F32),
                sds((3 * hd, n2), F32),
                sds((max(plan.far - 1, 1), 2 * hd, n2), BF16),
                TOKEN,
            ],
            [SMEM, SMEM, ANY] + [VMEM] * (len(front) + len(received[source])),
            [pltpu.VMEM((64, n), F32), pltpu.VMEM((hd, n), BF16)],
            flops=4 * pair_flops,
            name=f"last{chunk}",
        )(*scalars, token, *front[:3], *received[source], *front[3:])
        states.append((att, (ld, grad2, *(shifted(far2[s - 1], -s) for s in range(1, plan.far)))))
    full = sds((tok_rows, model_width), BF16)
    for chunk, (_, state) in enumerate(states):
        atts = [s[0] for s in states] if chunk == 0 else []
        slotted = chunk == chunks - 1
        count = len(atts) + 3
        sources = [where[chunk, 0], where[chunk, 3]]
        blocks = [len(received[x[0]]) for x in sources]
        block = sds((count * hd, tok_rows), BF16)
        *out, token = kernel_call(
            partial(
                backward_body, plan, chunk, [x[1] for x in sources], blocks, len(atts), slotted
            ),
            ([block] * near if slotted else [sds((near,) + block.shape, BF16)]) + [TOKEN],
            [SMEM, SMEM, ANY] + [VMEM] * (sum(blocks) + len(atts) + len(state)),
            [
                pltpu.VMEM((n3, 128), BF16),
                pltpu.VMEM((128, n3), BF16),
                pltpu.VMEM((n3, 128), BF16),
                pltpu.VMEM((64, n3), BF16),
                pltpu.VMEM((hd, n3), BF16),
                pltpu.VMEM((hd, n3), BF16),
                pltpu.VMEM((3 * hd, n), F32),
            ],
            flops=len(plan.tiles) * 5 * pair_flops,
            name=f"backward{chunk}",
        )(*scalars, token, *received[sources[0][0]], *received[sources[1][0]], *atts, *state)
        y = traded(out) if slotted else [swap(out[0])]
        scratch = [pltpu.VMEM((near,) + block.shape, BF16)] if slotted else []
        column = pl.BlockSpec((tok_rows, width), lambda i, c=chunk: (0, c))
        specs = [pl.BlockSpec(v.shape, lambda i, r=len(v.shape): (0,) * r) for v in y]
        if chunk == 0:
            attended, *outs = kernel_call(
                partial(unpack_body, plan, [0] + [chunks + i for i in range(3)], slotted),
                [full] * 4,
                specs,
                scratch,
                name="unpack",
                grid=(1,),
                out_specs=[pl.BlockSpec(full.shape, lambda i: (0, 0))] + [column] * 3,
            )(*y)
        else:
            outs = kernel_call(
                partial(unpack_body, plan, list(range(3)), slotted),
                [full] * 3,
                specs + [ANY] * 3,
                scratch,
                name="unpack",
                grid=(1,),
                out_specs=[column] * 3,
                input_output_aliases={len(y) + i: i for i in range(3)},
            )(*y, *outs)
    return (attended, *outs)


def solution(mesh):
    rows = P(("groups", "seq"), None)
    return jax.shard_map(
        body,
        mesh=mesh,
        in_specs=(rows, rows, rows, rows, P("groups"), P()),
        out_specs=(rows, rows, rows, rows),
        check_vma=False,
    )
```

```python
from functools import partial
import math

import jax
import jax.numpy as jnp
from jax import lax
from jax.experimental import pallas as pl
from jax.experimental.pallas import tpu as pltpu
from jax.sharding import PartitionSpec as P

SEG0 = 1024
BIG = 2.0**100
LOG2E = math.log2(math.e)
BF16 = jnp.bfloat16
F32 = jnp.float32
VMEM_LIMIT = 36 << 20
PACK_LIMIT = 63 << 20


class Plan:
    def __init__(self, tok_rows, model_width, level_count, head_count, slide_count, device_count):
        self.tok = tok_rows
        self.width = model_width
        self.levels = level_count
        self.hd = model_width // head_count
        self.slides = slide_count
        self.devices = device_count
        self.stride = device_count * tok_rows // SEG0
        self.bits = self.stride.bit_length() - 1
        self.near = min((SEG0 << (level_count - 2)) // tok_rows, device_count)
        self.far = device_count // self.near
        self.chunks = head_count // self.near
        self.segs = self.near * tok_rows // SEG0
        self.seg_dev = SEG0 // tok_rows
        self.cdev = tok_rows // self.stride
        self.cseg = SEG0 // self.stride
        self.rows = self.near * tok_rows
        self.last = self.segs * self.cseg
        self.tiles = []
        for level in range(level_count - 1):
            for first in range(0, self.segs, 1 << level):
                self.tiles.append((level, first))
        self.all_rows = len(self.tiles) * SEG0
        self.slide_pad = -(-slide_count // 8) * 8
        self.rest = 128 - 2 * self.hd - 8 - self.slide_pad
        self.aligned = self.cseg % 128 == 0
        self.table = (-(-self.table_row(self.chunks, 0) // 8) * 8, 128)
        assert self.rest >= 0 and self.hd + 16 <= 64 and self.hd % 16 == 0 and self.chunks > 1


    def level_bits(self, level):
        return level if level < self.levels - 1 else self.bits

    def table_row(self, chunk, level):
        return self.slide_pad + chunk * (self.levels + 1) + level


def reversed_bits(value, bits):
    out = value * 0
    for b in range(bits):
        out = out + ((value >> b) & 1) * (1 << (bits - 1 - b))
    return out


def dot(a, b, ca=1, cb=0, precision=None):
    return lax.dot_general(
        a, b, (((ca,), (cb,)), ((), ())), preferred_element_type=F32, precision=precision
    )


def iota(shape, axis):
    return lax.broadcasted_iota(jnp.int32, shape, axis)


def kernel_call(body, out_shape, in_specs, scratch=(), flops=0, name=None, limit=VMEM_LIMIT, **more):
    return pl.pallas_call(
        body,
        out_shape=out_shape,
        in_specs=in_specs,
        scratch_shapes=list(scratch),
        name=name,
        compiler_params=pltpu.CompilerParams(vmem_limit_bytes=limit),
        cost_estimate=pl.CostEstimate(flops=flops, bytes_accessed=1 << 20, transcendentals=0),
        **more,
    )


VMEM = pl.BlockSpec(memory_space=pltpu.VMEM)
SMEM = pl.BlockSpec(memory_space=pltpu.SMEM)
ANY = pl.BlockSpec(memory_space=pl.ANY)
TOKEN = jax.ShapeDtypeStruct((8, 128), F32)


def class_order(count, stride, shape, axis_row, axis_tok):
    row, tok = iota(shape, axis_row), iota(shape, axis_tok)
    size = count // stride
    want = (row % size) * stride + reversed_bits(row // size, stride.bit_length() - 1)
    return jnp.where(want == tok, 1.0, 0.0).astype(BF16)


def near_index(plan):
    return lax.rem(lax.axis_index("seq"), plan.near)


def pack_body(plan, columns, count_out, *refs):
    count = len(columns)
    ins, outs, (tok_out, rows, turned, sems) = refs[:count], refs[-4 - count_out : -4], refs[-4:]
    tok_out[...] = jnp.zeros_like(tok_out)
    hd, width = plan.hd, plan.near * plan.hd
    copies = [
        pltpu.make_async_copy(ref.at[:, c * width : (c + 1) * width], rows.at[i], sems.at[i])
        for i, (ref, c) in enumerate(zip(ins, columns))
    ]
    for copy in copies:
        copy.start()
    if count_out > 1:
        fill_table(plan, *refs[count : count + 2], outs[-1])
        outs = outs[:-1]
    order = class_order(plan.tok, plan.stride, (plan.tok, plan.tok), 0, 1)
    me = near_index(plan)
    for i, copy in enumerate(copies):
        copy.wait()
        x = dot(rows[i], order, 0, 1).astype(BF16)
        if len(outs) == 1:
            for j in range(plan.near):
                outs[0][j, i * hd : (i + 1) * hd, :] = x[j * hd : (j + 1) * hd, :]
        else:
            turned[...] = x
            for j in range(plan.near):
                first = pl.multiple_of((me ^ j) * hd, 16)
                outs[j][i * hd : (i + 1) * hd, :] = turned[pl.ds(first, hd), :]


def segment_from(plan, blocks):
    if plan.cdev % 64 == 0:
        return jnp.concatenate(
            [x[:, c * plan.cdev : (c + 1) * plan.cdev] for c in range(plan.stride) for x in blocks],
            axis=1,
        ).astype(F32)
    return dot(jnp.concatenate(blocks, axis=1), device_lanes(plan, 1, 0))


def device_lanes(plan, axis_dev, axis_seg):
    shape = (SEG0, SEG0)
    seg, dev = iota(shape, axis_dev), iota(shape, axis_seg)
    cls, inside = seg // plan.cseg, seg % plan.cseg
    want = inside // plan.cdev * plan.tok + cls * plan.cdev + inside % plan.cdev
    return jnp.where(want == dev, 1.0, 0.0).astype(BF16)


def segment_to(plan, x):
    if plan.cdev % 64 == 0:
        return [
            jnp.concatenate(
                [
                    x[:, c * plan.cseg + d * plan.cdev : c * plan.cseg + (d + 1) * plan.cdev]
                    for c in range(plan.stride)
                ],
                axis=1,
            )
            for d in range(plan.seg_dev)
        ]
    x = dot(x, device_lanes(plan, 0, 1)).astype(BF16)
    return [x[:, d * plan.tok : (d + 1) * plan.tok] for d in range(plan.seg_dev)]


def slide_rows(plan, pos, table):
    slide = jnp.zeros(pos.shape, jnp.int32)
    for i in range(plan.slides):
        slide = slide + jnp.where(pos.astype(F32) >= table[i : i + 1, 0:1], 1, 0)
    shape = (plan.slide_pad, pos.shape[1])
    return jnp.where(iota(shape, 0) == slide, 1.0, 0.0)


def key_features(plan, k, one_hot):
    n = k.shape[1]
    return jnp.concatenate(
        [k, k, jnp.ones((8, n), F32), one_hot, jnp.zeros((plan.rest, n), F32)], axis=0
    )


def query_features(plan, q, one_hot):
    n = q.shape[1]
    q = q * (plan.hd**-0.5 * LOG2E)
    high = q.astype(BF16).astype(F32)
    mask = (one_hot - 1.0) * BIG
    return jnp.concatenate(
        [high, q - high, jnp.zeros((8, n), F32), mask, jnp.zeros((plan.rest, n), F32)], axis=0
    )


def value_features(plan, v):
    n = v.shape[1]
    return jnp.concatenate([v, jnp.ones((8, n), F32), jnp.zeros((56 - plan.hd, n), F32)], axis=0)


def three_rows(x):
    a = x.astype(BF16).astype(F32)
    b = (x - a).astype(BF16).astype(F32)
    row = iota((8, x.shape[1]), 0)
    return jnp.where(row == 0, a, jnp.where(row == 1, b, jnp.where(row == 2, x - a - b, 0.0)))


def forward_tile(plan, s, values_t):
    peak = jnp.max(s, axis=0, keepdims=True)
    p = jnp.exp2(s - peak).astype(BF16)
    o = dot(values_t, p)
    return jnp.concatenate(
        [o[: plan.hd + 8], jnp.broadcast_to(peak, (56 - plan.hd, o.shape[1]))], axis=0
    )


def merged(plan, a, b):
    at = plan.hd + 8
    peak_a, peak_b = a[at : at + 1], b[at : at + 1]
    peak = jnp.maximum(peak_a, peak_b)
    both = a[:at] * jnp.exp2(peak_a - peak) + b[:at] * jnp.exp2(peak_b - peak)
    return jnp.concatenate([both, jnp.broadcast_to(peak, (64 - at, a.shape[1]))], axis=0)


def backward_tile(plan, qa, kat, ga, vat, gt, qt):
    n = qa.shape[0]
    step = min(n, SEG0 // 2)
    parts = [slice(i, i + step) for i in range(0, n, step)]
    weights = []
    for rows in parts:
        dp = dot(ga[rows], vat)
        p = jnp.exp2(dot(qa[rows], kat))
        weights.append((p.astype(BF16), (p * dp).astype(BF16)))
    query_t = [dot(kat[: plan.hd], ds, 1, 1) for _, ds in weights]
    key_t = sum(dot(qt[:, rows], ds) for rows, (_, ds) in zip(parts, weights))
    value_t = sum(dot(gt[:, rows], p) for rows, (p, _) in zip(parts, weights))
    return jnp.concatenate(query_t, axis=1), key_t, value_t


def tile_pieces(plan, starts, tile):
    level, first = plan.tiles[tile]
    rows = SEG0 >> level
    out = []
    for i in range(1 << level):
        src = pl.ds(pl.multiple_of((first + i) * SEG0 + starts[level], 128), rows)
        out.append((src, slice(tile * SEG0 + i * rows, tile * SEG0 + (i + 1) * rows)))
    return out


def last_slices(plan, starts):
    return [
        pl.ds(pl.multiple_of(seg * SEG0 + starts[-1], plan.cseg), plan.cseg) for seg in range(plan.segs)
    ]


def last_places(plan, starts, shape, axis_seg, axis_last):
    hit = iota(shape, axis_seg) == starts[-1] + iota(shape, axis_last)
    return jnp.where(hit, 1.0, 0.0)


def last_lanes(plan, starts, ref):
    if plan.aligned:
        return jnp.concatenate([ref[:, s] for s in last_slices(plan, starts)], axis=1)
    place = last_places(plan, starts, (SEG0, plan.cseg), 0, 1)
    exact = lax.Precision.HIGHEST
    parts = [
        dot(ref[:, g * SEG0 : (g + 1) * SEG0].astype(F32), place, precision=exact)
        for g in range(plan.segs)
    ]
    return jnp.concatenate(parts, axis=1).astype(ref.dtype)


def last_update(plan, starts, ref, rows, part, update, fill):
    if plan.aligned:
        for seg, s in enumerate(last_slices(plan, starts)):
            ref[rows, s] = update(ref[rows, s], part[:, seg * plan.cseg : (seg + 1) * plan.cseg])
        return
    place = last_places(plan, starts, (plan.cseg, SEG0), 1, 0)
    hit = jnp.max(place, axis=0, keepdims=True) > 0
    for seg in range(plan.segs):
        own = part[:, seg * plan.cseg : (seg + 1) * plan.cseg]
        own = jnp.where(hit, dot(own, place, precision=lax.Precision.HIGHEST), fill)
        s = slice(seg * SEG0, (seg + 1) * SEG0)
        ref[rows, s] = update(ref[rows, s], own)


def no_level(plan):
    return jnp.where(iota((64, 1), 0) >= plan.hd + 8, -BIG, 0.0)


def fill_table(plan, len_ref, off_ref, table):
    table[...] = jnp.zeros_like(table)

    def put(row, value):
        table[row : row + 1, :] = jnp.full((1, 128), value, jnp.int32).astype(F32)

    end = 0
    for i in range(plan.slides):
        end = end + len_ref[i]
        put(i, end)
    for chunk in range(plan.chunks):
        head = chunk * plan.near + near_index(plan)
        for level in range(plan.levels):
            bits = plan.level_bits(level)
            first = reversed_bits(off_ref[level, head] % (1 << bits), bits) * (SEG0 >> bits)
            put(plan.table_row(chunk, level), first)
        put(plan.table_row(chunk, plan.levels), off_ref[plan.levels - 1, head] % plan.stride)


def level_starts(plan, table, chunk):
    rows = [plan.table_row(chunk, level) for level in range(plan.levels)]
    return [jnp.max(table[row : row + 1, :]).astype(jnp.int32) for row in rows]


def slots_of(plan, refs):
    if len(refs) > 1:
        return refs
    return [refs[0].at[near_index(plan) ^ j] for j in range(plan.near)]


def segment_of(plan, slots, first, count, seg):
    return segment_from(
        plan,
        [
            slots[seg * plan.seg_dev + d][first : first + count * plan.hd, :]
            for d in range(plan.seg_dev)
        ],
    )


def slot_tokens(plan, seg, slot, inside):
    me = near_index(plan)
    seg = (me // plan.seg_dev) ^ seg
    return seg * SEG0 + (lax.rem(me, plan.seg_dev) ^ slot) * plan.tok + inside


def segment_slides(plan, seg, table):
    n = iota((1, SEG0), 1)
    inside = (n % plan.cdev) * plan.stride + reversed_bits(n // plan.cseg, plan.bits)
    pos = slot_tokens(plan, seg, n % plan.cseg // plan.cdev, inside)
    return slide_rows(plan, lax.axis_index("seq") // plan.near * plan.rows + pos, table)


def forward_body(plan, chunk, first, blocks, parts, table, tok_in, *refs):
    slots, refs = slots_of(plan, refs[:blocks]) if blocks else None, refs[blocks:]
    if parts == "rows":
        q2, kv2, ka, qat, vat, tok_out, raw = refs
    elif parts == "sums":
        ka, qat, vat, acc_ref, tok_out, res = refs
    else:
        q2, kv2, acc_ref, tok_out, raw, ka, qat, vat, res = refs
    tok_out[...] = jnp.zeros_like(tok_out)
    starts = level_starts(plan, table, chunk)
    if parts != "sums":
        forward_operands(plan, first, slots, table, starts, q2, kv2, ka, qat, vat, raw)
    if parts != "rows":
        forward_levels(plan, starts, ka, qat, vat, acc_ref, res)


def forward_operands(plan, first, slots, table, starts, q2, kv2, ka, qat, vat, raw):
    hd = plan.hd
    for seg in range(plan.segs):
        rows = slice(seg * SEG0, (seg + 1) * SEG0)
        xt = segment_of(plan, slots, first, 3, seg)
        raw[:, rows] = xt.astype(BF16)
        q, k, v = (xt[i * hd : (i + 1) * hd] for i in range(3))
        one_hot = segment_slides(plan, seg, table)
        ka[rows, :] = key_features(plan, k, one_hot).T.astype(BF16)
        qat[:, rows] = query_features(plan, q, one_hot).astype(BF16)
        vat[:, rows] = value_features(plan, v).astype(BF16)
    for tile in range(plan.segs, len(plan.tiles)):
        for src, dst in tile_pieces(plan, starts, tile):
            ka[dst, :] = ka[src, :]
            for ref in (qat, vat):
                ref[:, dst] = ref[:, src]
    last = last_lanes(plan, starts, raw)
    q2[...] = last[0:hd]
    kv2[...] = last[hd:]


def forward_levels(plan, starts, ka, qat, vat, acc_ref, res):
    tiles = [slice(t * SEG0, (t + 1) * SEG0) for t in range(len(plan.tiles))]
    scores = [dot(ka[rows, :], qat[:, rows]) for rows in tiles]
    for s, rows in zip(scores, tiles):
        res[:, rows] = forward_tile(plan, s, vat[:, rows])
    acc_ref[...] = res[:, 0 : plan.rows]
    for tile in range(plan.segs, len(plan.tiles)):
        for src, dst in tile_pieces(plan, starts, tile):
            acc_ref[:, src] = merged(plan, acc_ref[:, src], res[:, dst])


def last_body(plan, chunk, first, blocks, table, tok_in, acc_ref, q2, kv2, *rest):
    slots, rest = slots_of(plan, rest[:blocks]), rest[blocks:]
    far_in, (att_ref, ld_ref, grad_ref, far_ref, tok_out, acc, gt) = (
        rest[: plan.far - 1],
        rest[plan.far - 1 :],
    )
    hd = plan.hd
    tok_out[...] = jnp.zeros_like(tok_out)
    group = lax.axis_index("seq") // plan.near
    starts = level_starts(plan, table, chunk)
    row = plan.table_row(chunk, plan.levels)
    acc[...] = acc_ref[...]
    x = jnp.concatenate([ref[...].astype(F32) for ref in (kv2,) + far_in], axis=1)
    n = iota((1, SEG0), 1)
    owner = group - n // plan.last
    owner = jnp.where(owner < 0, owner + plan.far, owner)
    inside = (n % plan.cdev) * plan.stride + table[row : row + 1, 0:1].astype(jnp.int32)
    seg, slot = n % plan.last // plan.cseg, n % plan.cseg // plan.cdev
    pos = owner * plan.rows + slot_tokens(plan, seg, slot, inside)
    one_hot = slide_rows(plan, pos, table)
    key_f = key_features(plan, x[0:hd], one_hot)
    query_f = query_features(plan, q2[...].astype(F32), one_hot[:, 0 : plan.last])
    vat2 = value_features(plan, x[hd : 2 * hd]).astype(BF16)
    res = forward_tile(plan, dot(key_f.T.astype(BF16), query_f.astype(BF16)), vat2)
    last_update(plan, starts, acc, slice(None), res, partial(merged, plan), no_level(plan))
    for seg in range(plan.segs):
        rows = slice(seg * SEG0, (seg + 1) * SEG0)
        a = acc[:, rows]
        total = a[hd : hd + 1]
        att = (a[0:hd] / total).astype(BF16)
        att_ref[:, rows] = att
        log_total = a[hd + 8 : hd + 9] + jnp.log2(total)
        g = segment_of(plan, slots, first, 1, seg)
        gt[:, rows] = g.astype(BF16)
        grad_dot = jnp.sum(g * att.astype(F32), axis=0, keepdims=True)
        ld_ref[:, rows] = jnp.where(iota((8, SEG0), 0) == 0, log_total, grad_dot)
    g2 = last_lanes(plan, starts, gt)
    ld2 = last_lanes(plan, starts, ld_ref)
    qa2, ga2 = backward_queries(plan, query_f, g2.astype(F32), ld2)
    dq, dk, dv = backward_tile(plan, qa2, key_f.astype(BF16), ga2[:, 0:64], vat2, g2, q2[...])
    grad_ref[...] = jnp.concatenate(
        [dq, dk[:, 0 : plan.last], dv[:, 0 : plan.last]], axis=0
    )
    both = jnp.concatenate([dk, dv], axis=0)
    for s in range(1, plan.far):
        far_ref[s - 1] = both[:, s * plan.last : (s + 1) * plan.last].astype(BF16)


def backward_queries(plan, query_f, g, ld):
    hd = plan.hd
    query_f = jnp.concatenate(
        [query_f[0 : 2 * hd], three_rows(-ld[0:1]), query_f[2 * hd + 8 :]], axis=0
    )
    grad_f = jnp.concatenate(
        [g, three_rows(-ld[1:2]), jnp.zeros((120 - hd, g.shape[1]), F32)], axis=0
    )
    return query_f.T.astype(BF16), grad_f.T.astype(BF16)


def backward_body(plan, chunk, places, blocks, ends, table, tok_in, ld_ref, *refs):
    slots, refs = slots_of(plan, refs[: blocks[0]]), refs[blocks[0] :]
    g_slots, refs = slots_of(plan, refs[: blocks[1]]), refs[blocks[1] :]
    if ends:
        grad2, far_refs, outs, refs = refs[0], refs[1 : plan.far], refs[plan.far : -8], refs[-8:]
        tok_out, qa, kat, ga, vat, gt, qt, grads = refs
    else:
        grads, tok_out, qa, kat, ga, vat, gt, qt = refs
    hd = plan.hd
    tok_out[...] = jnp.zeros_like(tok_out)
    starts = level_starts(plan, table, chunk)
    for seg in range(plan.segs):
        rows = slice(seg * SEG0, (seg + 1) * SEG0)
        xt = segment_of(plan, slots, places[0], 3, seg)
        q, k, v = (xt[i * hd : (i + 1) * hd] for i in range(3))
        g = segment_of(plan, g_slots, places[1], 1, seg)
        one_hot = segment_slides(plan, seg, table)
        kat[:, rows] = key_features(plan, k, one_hot).astype(BF16)
        vat[:, rows] = value_features(plan, v).astype(BF16)
        qt[:, rows] = q.astype(BF16)
        gt[:, rows] = g.astype(BF16)
        qa[rows, :], ga[rows, :] = backward_queries(
            plan, query_features(plan, q, one_hot), g, ld_ref[:, rows]
        )
    for tile in range(plan.segs, len(plan.tiles)):
        for src, dst in tile_pieces(plan, starts, tile):
            qa[dst, :] = qa[src, :]
            ga[dst, :] = ga[src, :]
            for ref in (kat, vat, gt, qt):
                ref[:, dst] = ref[:, src]

    for tile in range(len(plan.tiles)):
        rows = slice(tile * SEG0, (tile + 1) * SEG0)
        parts = backward_tile(
            plan, qa[rows, :], kat[:, rows], ga[rows, 0:64], vat[:, rows], gt[:, rows], qt[:, rows]
        )
        if tile < plan.segs:
            for i, part in enumerate(parts):
                grads[i * hd : (i + 1) * hd, rows] = part
            continue
        for src, dst in tile_pieces(plan, starts, tile):
            at = slice(dst.start - rows.start, dst.stop - rows.start)
            for i, part in enumerate(parts):
                own = slice(i * hd, (i + 1) * hd)
                grads[own, src] = grads[own, src] + part[:, at]
    if ends:

        def store(slot, x):
            outs[slot][...] = x

        finished(plan, starts, [], grad2, far_refs, grads, store)


def finished(plan, starts, att_refs, grad2, far_refs, grads, store):
    hd = plan.hd
    more = grad2[...]
    if far_refs:
        far = sum(ref[...].astype(F32) for ref in far_refs)
        more = jnp.concatenate([more[0:hd], more[hd:] + far], axis=0)
    last_update(plan, starts, grads, slice(None), more, jnp.add, 0.0)
    scale = hd**-0.5
    for seg in range(plan.segs):
        rows = slice(seg * SEG0, (seg + 1) * SEG0)
        parts = [ref[:, rows] for ref in att_refs]
        parts += [(grads[0 : 2 * hd, rows] * scale).astype(BF16), grads[2 * hd : 3 * hd, rows].astype(BF16)]
        for d, x in enumerate(segment_to(plan, jnp.concatenate(parts, axis=0))):
            store(seg * plan.seg_dev + d, x)


def finish_body(plan, chunk, atts, table, tok_in, near_ref, *refs):
    att_refs, refs = refs[:atts], refs[atts:]
    grad2, far_refs, (out_ref, tok_out, grads) = refs[0], refs[1 : plan.far], refs[plan.far :]
    tok_out[...] = jnp.zeros_like(tok_out)
    grads[...] = near_ref[...]

    def store(slot, x):
        out_ref[near_index(plan) ^ slot] = x

    finished(plan, level_starts(plan, table, chunk), att_refs, grad2, far_refs, grads, store)


def unpack_body(plan, places, slotted, *refs):
    if slotted:
        y_ref, outs = refs[-1], refs[-1 - len(places) : -1]
        for j in range(plan.near):
            y_ref[near_index(plan) ^ j] = refs[j][...]
    else:
        y_ref, outs = refs[0], refs[-len(places) :]
    hd, width = plan.hd, plan.near * plan.hd
    order = class_order(plan.tok, plan.stride, (plan.tok, plan.tok), 1, 0)
    for out_ref, first in zip(outs, places):
        for col in range(out_ref.shape[1] // width):
            i = first + col
            x = jnp.concatenate([y_ref[d, i * hd : (i + 1) * hd, :] for d in range(plan.near)], axis=0)
            out_ref[:, col * width : (col + 1) * width] = dot(order, x, 1, 1).astype(BF16)


def body(queries, keys, values, out_grad, slide_lengths, head_offsets):
    tok_rows, model_width = queries.shape
    level_count, head_count = head_offsets.shape
    device_count = lax.axis_size("seq")
    plan = Plan(tok_rows, model_width, level_count, head_count, slide_lengths.shape[0], device_count)
    hd, chunks = plan.hd, plan.chunks
    groups = [list(range(i, i + plan.near)) for i in range(0, device_count, plan.near)]
    sds = jax.ShapeDtypeStruct
    near = plan.near

    def permuted(x, target):
        return lax.ppermute(x, "seq", [(i, target(i)) for i in range(device_count)])

    def swap(x):
        return lax.all_to_all(x, "seq", 0, 0, tiled=True, axis_index_groups=groups)

    def shifted(x, steps):
        return permuted(x, lambda i: (i + steps * near) % device_count)

    def traded(slots):
        return [slots[0]] + [permuted(slots[j], lambda i, j=j: i ^ j) for j in range(near - 1, 0, -1)][::-1]

    exchanges = [[(c, i) for i in range(3)] for c in range(chunks)]
    for c in range(chunks):
        exchanges[min(c + 1, chunks - 1)].append((c, 3))
    arrays = (queries, keys, values, out_grad)
    width = near * hd
    received, where = [], {}
    token = ()
    for pieces in exchanges:
        slotted = len(received) > 0
        block = (len(pieces) * hd, tok_rows)
        *packed, tok = kernel_call(
            partial(pack_body, plan, [c for c, _ in pieces], near + 1 if slotted else 1),
            (
                [sds(block, BF16)] * near + [sds(plan.table, F32)]
                if slotted
                else [sds((near,) + block, BF16)]
            )
            + [TOKEN],
            [ANY] * len(pieces) + [SMEM] * 2 * slotted + [ANY] * len(token),
            [
                pltpu.VMEM((len(pieces), tok_rows, width), BF16),
                pltpu.VMEM((width, tok_rows), BF16),
                pltpu.SemaphoreType.DMA((len(pieces),)),
            ],
            name="pack",
            limit=VMEM_LIMIT if slotted else PACK_LIMIT,
        )(*(arrays[i] for _, i in pieces), *(slide_lengths, head_offsets) * slotted, *token)
        token = (tok,)
        if slotted:
            table = packed.pop()
        for place, piece in enumerate(pieces):
            where[piece] = (len(received), place * hd)
        received.append(traded(packed) if slotted else [swap(packed[0])])

    n, n3, n2 = plan.rows, plan.all_rows, plan.last
    pair_flops = 20 * 2 * 128 * SEG0 * SEG0
    (token,) = token
    fronts = []
    for chunk in range(chunks):
        source, first = where[chunk, 0]
        near_x = received[source]
        last_rows = [sds((hd, n2), BF16), sds((2 * hd, n2), BF16)]
        operands = [(n3, 128), (128, n3), (64, n3)]
        raw, res = pltpu.VMEM((3 * hd, n), BF16), pltpu.VMEM((64, n3), F32)
        sums = sds((64, n), F32)
        make = partial(forward_body, plan, chunk, first)
        if chunk == 0:
            q2, kv2, acc, token = kernel_call(
                partial(make, len(near_x), "both"),
                last_rows + [sums, TOKEN],
                [VMEM, ANY] + [VMEM] * len(near_x),
                [raw] + [pltpu.VMEM(shape, BF16) for shape in operands] + [res],
                name=f"forward{chunk}",
            )(table, token, *near_x)
            far_kv = [shifted(kv2, s) for s in range(1, plan.far)]
        else:
            q2, kv2, *state, token = kernel_call(
                partial(make, len(near_x), "rows"),
                last_rows + [sds(shape, BF16) for shape in operands] + [TOKEN],
                [VMEM, ANY] + [VMEM] * len(near_x),
                [raw],
                name=f"rows{chunk}",
            )(table, token, *near_x)
            far_kv = [shifted(kv2, s) for s in range(1, plan.far)]
            acc, token = kernel_call(
                partial(make, 0, "sums"),
                [sums, TOKEN],
                [VMEM, ANY] + [VMEM] * 3,
                [res],
                name=f"sums{chunk}",
            )(table, token, *state)
        fronts.append((acc, q2, kv2, *far_kv))
    states = []
    for chunk, front in enumerate(fronts):
        source, first = where[chunk, 3]
        att, ld, grad2, far2, token = kernel_call(
            partial(last_body, plan, chunk, first, len(received[source])),
            [
                sds((hd, n), BF16),
                sds((8, n), F32),
                sds((3 * hd, n2), F32),
                sds((max(plan.far - 1, 1), 2 * hd, n2), BF16),
                TOKEN,
            ],
            [VMEM, ANY] + [VMEM] * (len(front) + len(received[source])),
            [pltpu.VMEM((64, n), F32), pltpu.VMEM((hd, n), BF16)],
            flops=4 * pair_flops,
            name=f"last{chunk}",
        )(table, token, *front[:3], *received[source], *front[3:])
        states.append((att, (ld, grad2, *(shifted(far2[s - 1], -s) for s in range(1, plan.far)))))
    full = sds((tok_rows, model_width), BF16)
    for chunk, (_, (ld, *tail)) in enumerate(states):
        atts = [s[0] for s in states] if chunk == 0 else []
        slotted = chunk == chunks - 1 and not atts
        count = len(atts) + 3
        sources = [where[chunk, 0], where[chunk, 3]]
        blocks = [len(received[x[0]]) for x in sources]
        block = sds((count * hd, tok_rows), BF16)
        grads = pltpu.VMEM((3 * hd, n), F32)
        *out, token = kernel_call(
            partial(backward_body, plan, chunk, [x[1] for x in sources], blocks, slotted),
            ([block] * near if slotted else [sds((3 * hd, n), F32)]) + [TOKEN],
            [VMEM, ANY] + [VMEM] * (1 + sum(blocks) + slotted * len(tail)),
            [
                pltpu.VMEM((n3, 128), BF16),
                pltpu.VMEM((128, n3), BF16),
                pltpu.VMEM((n3, 128), BF16),
                pltpu.VMEM((64, n3), BF16),
                pltpu.VMEM((hd, n3), BF16),
                pltpu.VMEM((hd, n3), BF16),
            ]
            + [grads] * slotted,
            flops=len(plan.tiles) * 5 * pair_flops,
            name=f"backward{chunk}",
        )(table, token, ld, *received[sources[0][0]], *received[sources[1][0]], *(tail if slotted else []))
        if not slotted:
            *out, token = kernel_call(
                partial(finish_body, plan, chunk, len(atts)),
                [sds((near,) + block.shape, BF16), TOKEN],
                [VMEM, ANY] + [VMEM] * (1 + len(atts) + len(tail)),
                [grads],
                name=f"finish{chunk}",
            )(table, token, *out, *atts, *tail)
        y = traded(out) if slotted else [swap(out[0])]
        scratch = [pltpu.VMEM((near,) + block.shape, BF16)] if slotted else []
        column = pl.BlockSpec((tok_rows, width), lambda i, c=chunk: (0, c))
        specs = [pl.BlockSpec(v.shape, lambda i, r=len(v.shape): (0,) * r) for v in y]
        if chunk == 0:
            attended, *outs = kernel_call(
                partial(unpack_body, plan, [0] + [chunks + i for i in range(3)], slotted),
                [full] * 4,
                specs,
                scratch,
                name="unpack",
                grid=(1,),
                out_specs=[pl.BlockSpec(full.shape, lambda i: (0, 0))] + [column] * 3,
            )(*y)
        else:
            outs = kernel_call(
                partial(unpack_body, plan, list(range(3)), slotted),
                [full] * 3,
                specs + [ANY] * 3,
                scratch,
                name="unpack",
                grid=(1,),
                out_specs=[column] * 3,
                input_output_aliases={len(y) + i: i for i in range(3)},
            )(*y, *outs)
    return (attended, *outs)


def solution(mesh):
    rows = P(("groups", "seq"), None)
    return jax.shard_map(
        body,
        mesh=mesh,
        in_specs=(rows, rows, rows, rows, P("groups"), P()),
        out_specs=(rows, rows, rows, rows),
        check_vma=False,
    )
```

```python
from functools import partial
import math

import jax
import jax.numpy as jnp
from jax import lax
from jax.experimental import pallas as pl
from jax.experimental.pallas import tpu as pltpu
from jax.sharding import PartitionSpec as P

SEG0 = 1024
BIG = 2.0**100
LOG2E = math.log2(math.e)
BF16 = jnp.bfloat16
F32 = jnp.float32
VMEM_LIMIT = 36 << 20
PACK_LIMIT = 63 << 20


class Plan:
    def __init__(self, tok_rows, model_width, level_count, head_count, slide_count, device_count):
        self.tok = tok_rows
        self.width = model_width
        self.levels = level_count
        self.hd = model_width // head_count
        self.slides = slide_count
        self.devices = device_count
        self.stride = device_count * tok_rows // SEG0
        self.bits = self.stride.bit_length() - 1
        self.near = min((SEG0 << (level_count - 2)) // tok_rows, device_count)
        self.far = device_count // self.near
        self.chunks = head_count // self.near
        self.segs = self.near * tok_rows // SEG0
        self.seg_dev = SEG0 // tok_rows
        self.cdev = tok_rows // self.stride
        self.cseg = SEG0 // self.stride
        self.rows = self.near * tok_rows
        self.last = self.segs * self.cseg
        self.tiles = []
        for level in range(level_count - 1):
            for first in range(0, self.segs, 1 << level):
                self.tiles.append((level, first))
        self.all_rows = len(self.tiles) * SEG0
        self.slide_pad = -(-slide_count // 8) * 8
        self.rest = 128 - 2 * self.hd - 8 - self.slide_pad
        self.aligned = self.cseg % 128 == 0
        self.table = (-(-self.table_row(self.chunks, 0) // 8) * 8, 128)
        assert self.rest >= 0 and self.hd + 16 <= 64 and self.hd % 16 == 0 and self.chunks > 1


    def level_bits(self, level):
        return level if level < self.levels - 1 else self.bits

    def table_row(self, chunk, level):
        return self.slide_pad + chunk * (self.levels + 1) + level


def reversed_bits(value, bits):
    out = value * 0
    for b in range(bits):
        out = out + ((value >> b) & 1) * (1 << (bits - 1 - b))
    return out


def dot(a, b, ca=1, cb=0, precision=None):
    return lax.dot_general(
        a, b, (((ca,), (cb,)), ((), ())), preferred_element_type=F32, precision=precision
    )


def iota(shape, axis):
    return lax.broadcasted_iota(jnp.int32, shape, axis)


def kernel_call(body, out_shape, in_specs, scratch=(), flops=0, name=None, limit=VMEM_LIMIT, **more):
    return pl.pallas_call(
        body,
        out_shape=out_shape,
        in_specs=in_specs,
        scratch_shapes=list(scratch),
        name=name,
        compiler_params=pltpu.CompilerParams(vmem_limit_bytes=limit),
        cost_estimate=pl.CostEstimate(flops=flops, bytes_accessed=1 << 20, transcendentals=0),
        **more,
    )


VMEM = pl.BlockSpec(memory_space=pltpu.VMEM)
SMEM = pl.BlockSpec(memory_space=pltpu.SMEM)
ANY = pl.BlockSpec(memory_space=pl.ANY)
TOKEN = jax.ShapeDtypeStruct((8, 128), F32)


def class_order(count, stride, shape, axis_row, axis_tok):
    row, tok = iota(shape, axis_row), iota(shape, axis_tok)
    size = count // stride
    want = (row % size) * stride + reversed_bits(row // size, stride.bit_length() - 1)
    return jnp.where(want == tok, 1.0, 0.0).astype(BF16)


def near_index(plan):
    return lax.rem(lax.axis_index("seq"), plan.near)


def pack_body(plan, columns, count_out, *refs):
    count = len(columns)
    ins, outs, (tok_out, rows, turned, sems) = refs[:count], refs[-4 - count_out : -4], refs[-4:]
    tok_out[...] = jnp.zeros_like(tok_out)
    hd, width = plan.hd, plan.near * plan.hd
    copies = [
        pltpu.make_async_copy(ref.at[:, c * width : (c + 1) * width], rows.at[i], sems.at[i])
        for i, (ref, c) in enumerate(zip(ins, columns))
    ]
    for copy in copies:
        copy.start()
    if count_out > 1:
        fill_table(plan, *refs[count : count + 2], outs[-1])
        outs = outs[:-1]
    order = class_order(plan.tok, plan.stride, (plan.tok, plan.tok), 0, 1)
    me = near_index(plan)
    for i, copy in enumerate(copies):
        copy.wait()
        x = dot(rows[i], order, 0, 1).astype(BF16)
        if len(outs) == 1:
            for j in range(plan.near):
                outs[0][j, i * hd : (i + 1) * hd, :] = x[j * hd : (j + 1) * hd, :]
        else:
            turned[...] = x
            for j in range(plan.near):
                first = pl.multiple_of((me ^ j) * hd, 16)
                outs[j][i * hd : (i + 1) * hd, :] = turned[pl.ds(first, hd), :]


def segment_from(plan, blocks):
    if plan.cdev % 64 == 0:
        return jnp.concatenate(
            [x[:, c * plan.cdev : (c + 1) * plan.cdev] for c in range(plan.stride) for x in blocks],
            axis=1,
        ).astype(F32)
    return dot(jnp.concatenate(blocks, axis=1), device_lanes(plan, 1, 0))


def device_lanes(plan, axis_dev, axis_seg):
    shape = (SEG0, SEG0)
    seg, dev = iota(shape, axis_dev), iota(shape, axis_seg)
    cls, inside = seg // plan.cseg, seg % plan.cseg
    want = inside // plan.cdev * plan.tok + cls * plan.cdev + inside % plan.cdev
    return jnp.where(want == dev, 1.0, 0.0).astype(BF16)


def segment_to(plan, x):
    if plan.cdev % 64 == 0:
        return [
            jnp.concatenate(
                [
                    x[:, c * plan.cseg + d * plan.cdev : c * plan.cseg + (d + 1) * plan.cdev]
                    for c in range(plan.stride)
                ],
                axis=1,
            )
            for d in range(plan.seg_dev)
        ]
    x = dot(x, device_lanes(plan, 0, 1)).astype(BF16)
    return [x[:, d * plan.tok : (d + 1) * plan.tok] for d in range(plan.seg_dev)]


def slide_rows(plan, pos, table):
    slide = jnp.zeros(pos.shape, jnp.int32)
    for i in range(plan.slides):
        slide = slide + jnp.where(pos.astype(F32) >= table[i : i + 1, 0:1], 1, 0)
    shape = (plan.slide_pad, pos.shape[1])
    return jnp.where(iota(shape, 0) == slide, 1.0, 0.0)


def key_features(plan, k, one_hot):
    n = k.shape[1]
    return jnp.concatenate(
        [k, k, jnp.ones((8, n), F32), one_hot, jnp.zeros((plan.rest, n), F32)], axis=0
    )


def query_features(plan, q, one_hot):
    n = q.shape[1]
    q = q * (plan.hd**-0.5 * LOG2E)
    high = q.astype(BF16).astype(F32)
    mask = (one_hot - 1.0) * BIG
    return jnp.concatenate(
        [high, q - high, jnp.zeros((8, n), F32), mask, jnp.zeros((plan.rest, n), F32)], axis=0
    )


def value_features(plan, v):
    n = v.shape[1]
    return jnp.concatenate([v, jnp.ones((8, n), F32), jnp.zeros((56 - plan.hd, n), F32)], axis=0)


def three_rows(x):
    a = x.astype(BF16).astype(F32)
    b = (x - a).astype(BF16).astype(F32)
    row = iota((8, x.shape[1]), 0)
    return jnp.where(row == 0, a, jnp.where(row == 1, b, jnp.where(row == 2, x - a - b, 0.0)))


def forward_tile(plan, s, values_t):
    peak = jnp.max(s, axis=0, keepdims=True)
    p = jnp.exp2(s - peak).astype(BF16)
    o = dot(values_t, p)
    return jnp.concatenate(
        [o[: plan.hd + 8], jnp.broadcast_to(peak, (56 - plan.hd, o.shape[1]))], axis=0
    )


def merged(plan, a, b):
    at = plan.hd + 8
    peak_a, peak_b = a[at : at + 1], b[at : at + 1]
    peak = jnp.maximum(peak_a, peak_b)
    both = a[:at] * jnp.exp2(peak_a - peak) + b[:at] * jnp.exp2(peak_b - peak)
    return jnp.concatenate([both, jnp.broadcast_to(peak, (64 - at, a.shape[1]))], axis=0)


def backward_tile(plan, qa, kat, ga, vat, gt, qt):
    n = qa.shape[0]
    step = min(n, SEG0 // 2)
    parts = [slice(i, i + step) for i in range(0, n, step)]
    weights = []
    for rows in parts:
        dp = dot(ga[rows], vat)
        p = jnp.exp2(dot(qa[rows], kat))
        weights.append((p.astype(BF16), (p * dp).astype(BF16)))
    query_t = [dot(kat[: plan.hd], ds, 1, 1) for _, ds in weights]
    key_t = sum(dot(qt[:, rows], ds) for rows, (_, ds) in zip(parts, weights))
    value_t = sum(dot(gt[:, rows], p) for rows, (p, _) in zip(parts, weights))
    return jnp.concatenate(query_t, axis=1), key_t, value_t


def tile_pieces(plan, starts, tile):
    level, first = plan.tiles[tile]
    rows = SEG0 >> level
    out = []
    for i in range(1 << level):
        src = pl.ds(pl.multiple_of((first + i) * SEG0 + starts[level], 128), rows)
        out.append((src, slice(tile * SEG0 + i * rows, tile * SEG0 + (i + 1) * rows)))
    return out


def last_slices(plan, starts):
    return [
        pl.ds(pl.multiple_of(seg * SEG0 + starts[-1], plan.cseg), plan.cseg) for seg in range(plan.segs)
    ]


def last_places(plan, starts, shape, axis_seg, axis_last):
    hit = iota(shape, axis_seg) == starts[-1] + iota(shape, axis_last)
    return jnp.where(hit, 1.0, 0.0)


def last_lanes(plan, starts, ref):
    if plan.aligned:
        return jnp.concatenate([ref[:, s] for s in last_slices(plan, starts)], axis=1)
    place = last_places(plan, starts, (SEG0, plan.cseg), 0, 1)
    exact = lax.Precision.HIGHEST
    parts = [
        dot(ref[:, g * SEG0 : (g + 1) * SEG0].astype(F32), place, precision=exact)
        for g in range(plan.segs)
    ]
    return jnp.concatenate(parts, axis=1).astype(ref.dtype)


def last_update(plan, starts, ref, rows, part, update, fill):
    if plan.aligned:
        for seg, s in enumerate(last_slices(plan, starts)):
            ref[rows, s] = update(ref[rows, s], part[:, seg * plan.cseg : (seg + 1) * plan.cseg])
        return
    place = last_places(plan, starts, (plan.cseg, SEG0), 1, 0)
    hit = jnp.max(place, axis=0, keepdims=True) > 0
    for seg in range(plan.segs):
        own = part[:, seg * plan.cseg : (seg + 1) * plan.cseg]
        own = jnp.where(hit, dot(own, place, precision=lax.Precision.HIGHEST), fill)
        s = slice(seg * SEG0, (seg + 1) * SEG0)
        ref[rows, s] = update(ref[rows, s], own)


def no_level(plan):
    return jnp.where(iota((64, 1), 0) >= plan.hd + 8, -BIG, 0.0)


def fill_table(plan, len_ref, off_ref, table):
    table[...] = jnp.zeros_like(table)

    def put(row, value):
        table[row : row + 1, :] = jnp.full((1, 128), value, jnp.int32).astype(F32)

    end = 0
    for i in range(plan.slides):
        end = end + len_ref[i]
        put(i, end)
    for chunk in range(plan.chunks):
        head = chunk * plan.near + near_index(plan)
        for level in range(plan.levels):
            bits = plan.level_bits(level)
            first = reversed_bits(off_ref[level, head] % (1 << bits), bits) * (SEG0 >> bits)
            put(plan.table_row(chunk, level), first)
        put(plan.table_row(chunk, plan.levels), off_ref[plan.levels - 1, head] % plan.stride)


def level_starts(plan, table, chunk):
    rows = [plan.table_row(chunk, level) for level in range(plan.levels)]
    return [jnp.max(table[row : row + 1, :]).astype(jnp.int32) for row in rows]


def slots_of(plan, refs):
    if len(refs) > 1:
        return refs
    return [refs[0].at[near_index(plan) ^ j] for j in range(plan.near)]


def segment_of(plan, slots, first, count, seg):
    return segment_from(
        plan,
        [
            slots[seg * plan.seg_dev + d][first : first + count * plan.hd, :]
            for d in range(plan.seg_dev)
        ],
    )


def slot_tokens(plan, seg, slot, inside):
    me = near_index(plan)
    seg = (me // plan.seg_dev) ^ seg
    return seg * SEG0 + (lax.rem(me, plan.seg_dev) ^ slot) * plan.tok + inside


def segment_slides(plan, seg, table):
    n = iota((1, SEG0), 1)
    inside = (n % plan.cdev) * plan.stride + reversed_bits(n // plan.cseg, plan.bits)
    pos = slot_tokens(plan, seg, n % plan.cseg // plan.cdev, inside)
    return slide_rows(plan, lax.axis_index("seq") // plan.near * plan.rows + pos, table)


def forward_body(plan, chunk, first, blocks, parts, table, tok_in, *refs):
    slots, refs = slots_of(plan, refs[:blocks]) if blocks else None, refs[blocks:]
    if parts == "rows":
        q2, kv2, ka, qat, vat, tok_out, raw = refs
    elif parts == "sums":
        ka, qat, vat, acc_ref, tok_out, res = refs
    else:
        q2, kv2, acc_ref, tok_out, raw, ka, qat, vat, res = refs
    tok_out[...] = jnp.zeros_like(tok_out)
    starts = level_starts(plan, table, chunk)
    if parts != "sums":
        forward_operands(plan, first, slots, table, starts, q2, kv2, ka, qat, vat, raw)
    if parts != "rows":
        forward_levels(plan, starts, ka, qat, vat, acc_ref, res)


def forward_operands(plan, first, slots, table, starts, q2, kv2, ka, qat, vat, raw):
    hd = plan.hd
    for seg in range(plan.segs):
        rows = slice(seg * SEG0, (seg + 1) * SEG0)
        xt = segment_of(plan, slots, first, 3, seg)
        raw[:, rows] = xt.astype(BF16)
        q, k, v = (xt[i * hd : (i + 1) * hd] for i in range(3))
        one_hot = segment_slides(plan, seg, table)
        ka[rows, :] = key_features(plan, k, one_hot).T.astype(BF16)
        qat[:, rows] = query_features(plan, q, one_hot).astype(BF16)
        vat[:, rows] = value_features(plan, v).astype(BF16)
    for tile in range(plan.segs, len(plan.tiles)):
        for src, dst in tile_pieces(plan, starts, tile):
            ka[dst, :] = ka[src, :]
            for ref in (qat, vat):
                ref[:, dst] = ref[:, src]
    last = last_lanes(plan, starts, raw)
    q2[...] = last[0:hd]
    kv2[...] = last[hd:]


def forward_levels(plan, starts, ka, qat, vat, acc_ref, res):
    tiles = [slice(t * SEG0, (t + 1) * SEG0) for t in range(len(plan.tiles))]
    scores = [dot(ka[rows, :], qat[:, rows]) for rows in tiles]
    for s, rows in zip(scores, tiles):
        res[:, rows] = forward_tile(plan, s, vat[:, rows])
    acc_ref[...] = res[:, 0 : plan.rows]
    for tile in range(plan.segs, len(plan.tiles)):
        for src, dst in tile_pieces(plan, starts, tile):
            acc_ref[:, src] = merged(plan, acc_ref[:, src], res[:, dst])


def last_body(plan, chunk, first, blocks, table, tok_in, acc_ref, q2, kv2, *rest):
    slots, rest = slots_of(plan, rest[:blocks]), rest[blocks:]
    far_in, (att_ref, ld_ref, grad_ref, far_ref, tok_out, acc, gt) = (
        rest[: plan.far - 1],
        rest[plan.far - 1 :],
    )
    hd = plan.hd
    tok_out[...] = jnp.zeros_like(tok_out)
    group = lax.axis_index("seq") // plan.near
    starts = level_starts(plan, table, chunk)
    row = plan.table_row(chunk, plan.levels)
    acc[...] = acc_ref[...]
    x = jnp.concatenate([ref[...].astype(F32) for ref in (kv2,) + far_in], axis=1)
    n = iota((1, SEG0), 1)
    owner = group - n // plan.last
    owner = jnp.where(owner < 0, owner + plan.far, owner)
    inside = (n % plan.cdev) * plan.stride + table[row : row + 1, 0:1].astype(jnp.int32)
    seg, slot = n % plan.last // plan.cseg, n % plan.cseg // plan.cdev
    pos = owner * plan.rows + slot_tokens(plan, seg, slot, inside)
    one_hot = slide_rows(plan, pos, table)
    key_f = key_features(plan, x[0:hd], one_hot)
    query_f = query_features(plan, q2[...].astype(F32), one_hot[:, 0 : plan.last])
    vat2 = value_features(plan, x[hd : 2 * hd]).astype(BF16)
    res = forward_tile(plan, dot(key_f.T.astype(BF16), query_f.astype(BF16)), vat2)
    last_update(plan, starts, acc, slice(None), res, partial(merged, plan), no_level(plan))
    for seg in range(plan.segs):
        rows = slice(seg * SEG0, (seg + 1) * SEG0)
        a = acc[:, rows]
        total = a[hd : hd + 1]
        att = (a[0:hd] / total).astype(BF16)
        att_ref[:, rows] = att
        log_total = a[hd + 8 : hd + 9] + jnp.log2(total)
        g = segment_of(plan, slots, first, 1, seg)
        gt[:, rows] = g.astype(BF16)
        grad_dot = jnp.sum(g * att.astype(F32), axis=0, keepdims=True)
        ld_ref[:, rows] = jnp.where(iota((8, SEG0), 0) == 0, log_total, grad_dot)
    g2 = last_lanes(plan, starts, gt)
    ld2 = last_lanes(plan, starts, ld_ref)
    qa2, ga2 = backward_queries(plan, query_f, g2.astype(F32), ld2)
    dq, dk, dv = backward_tile(plan, qa2, key_f.astype(BF16), ga2[:, 0:64], vat2, g2, q2[...])
    grad_ref[...] = jnp.concatenate(
        [dq, dk[:, 0 : plan.last], dv[:, 0 : plan.last]], axis=0
    )
    both = jnp.concatenate([dk, dv], axis=0)
    for s in range(1, plan.far):
        far_ref[s - 1] = both[:, s * plan.last : (s + 1) * plan.last].astype(BF16)


def backward_queries(plan, query_f, g, ld):
    hd = plan.hd
    query_f = jnp.concatenate(
        [query_f[0 : 2 * hd], three_rows(-ld[0:1]), query_f[2 * hd + 8 :]], axis=0
    )
    grad_f = jnp.concatenate(
        [g, three_rows(-ld[1:2]), jnp.zeros((120 - hd, g.shape[1]), F32)], axis=0
    )
    return query_f.T.astype(BF16), grad_f.T.astype(BF16)


def backward_body(plan, chunk, places, blocks, ends, table, tok_in, ld_ref, *refs):
    slots, refs = slots_of(plan, refs[: blocks[0]]), refs[blocks[0] :]
    g_slots, refs = slots_of(plan, refs[: blocks[1]]), refs[blocks[1] :]
    if ends:
        grad2, far_refs, outs, refs = refs[0], refs[1 : plan.far], refs[plan.far : -8], refs[-8:]
        tok_out, qa, kat, ga, vat, gt, qt, grads = refs
    else:
        grads, tok_out, qa, kat, ga, vat, gt, qt = refs
    hd = plan.hd
    tok_out[...] = jnp.zeros_like(tok_out)
    starts = level_starts(plan, table, chunk)
    for seg in range(plan.segs):
        rows = slice(seg * SEG0, (seg + 1) * SEG0)
        xt = segment_of(plan, slots, places[0], 3, seg)
        q, k, v = (xt[i * hd : (i + 1) * hd] for i in range(3))
        g = segment_of(plan, g_slots, places[1], 1, seg)
        one_hot = segment_slides(plan, seg, table)
        kat[:, rows] = key_features(plan, k, one_hot).astype(BF16)
        vat[:, rows] = value_features(plan, v).astype(BF16)
        qt[:, rows] = q.astype(BF16)
        gt[:, rows] = g.astype(BF16)
        qa[rows, :], ga[rows, :] = backward_queries(
            plan, query_features(plan, q, one_hot), g, ld_ref[:, rows]
        )
    for tile in range(plan.segs, len(plan.tiles)):
        for src, dst in tile_pieces(plan, starts, tile):
            qa[dst, :] = qa[src, :]
            ga[dst, :] = ga[src, :]
            for ref in (kat, vat, gt, qt):
                ref[:, dst] = ref[:, src]

    for tile in range(len(plan.tiles)):
        rows = slice(tile * SEG0, (tile + 1) * SEG0)
        parts = backward_tile(
            plan, qa[rows, :], kat[:, rows], ga[rows, 0:64], vat[:, rows], gt[:, rows], qt[:, rows]
        )
        if tile < plan.segs:
            for i, part in enumerate(parts):
                grads[i * hd : (i + 1) * hd, rows] = part
            continue
        for src, dst in tile_pieces(plan, starts, tile):
            at = slice(dst.start - rows.start, dst.stop - rows.start)
            for i, part in enumerate(parts):
                own = slice(i * hd, (i + 1) * hd)
                grads[own, src] = grads[own, src] + part[:, at]
    if ends:

        def store(slot, x):
            outs[slot][...] = x

        finished(plan, starts, [], grad2, far_refs, grads, store)


def finished(plan, starts, att_refs, grad2, far_refs, grads, store):
    hd = plan.hd
    more = grad2[...]
    if far_refs:
        far = sum(ref[...].astype(F32) for ref in far_refs)
        more = jnp.concatenate([more[0:hd], more[hd:] + far], axis=0)
    last_update(plan, starts, grads, slice(None), more, jnp.add, 0.0)
    scale = hd**-0.5
    for seg in range(plan.segs):
        rows = slice(seg * SEG0, (seg + 1) * SEG0)
        parts = [ref[:, rows] for ref in att_refs]
        parts += [(grads[0 : 2 * hd, rows] * scale).astype(BF16), grads[2 * hd : 3 * hd, rows].astype(BF16)]
        for d, x in enumerate(segment_to(plan, jnp.concatenate(parts, axis=0))):
            store(seg * plan.seg_dev + d, x)


def finish_body(plan, chunk, atts, table, tok_in, near_ref, *refs):
    att_refs, refs = refs[:atts], refs[atts:]
    grad2, far_refs, (out_ref, tok_out, grads) = refs[0], refs[1 : plan.far], refs[plan.far :]
    tok_out[...] = jnp.zeros_like(tok_out)
    grads[...] = near_ref[...]

    def store(slot, x):
        out_ref[near_index(plan) ^ slot] = x

    finished(plan, level_starts(plan, table, chunk), att_refs, grad2, far_refs, grads, store)


def unpack_body(plan, places, slotted, *refs):
    if slotted:
        y_ref, outs = refs[-1], refs[-1 - len(places) : -1]
        for j in range(plan.near):
            y_ref[near_index(plan) ^ j] = refs[plan.near - 1 - j][...]
    else:
        y_ref, outs = refs[0], refs[-len(places) :]
    hd, width = plan.hd, plan.near * plan.hd
    order = class_order(plan.tok, plan.stride, (plan.tok, plan.tok), 1, 0)
    for out_ref, first in zip(outs, places):
        for col in range(out_ref.shape[1] // width):
            i = first + col
            x = jnp.concatenate([y_ref[d, i * hd : (i + 1) * hd, :] for d in range(plan.near)], axis=0)
            out_ref[:, col * width : (col + 1) * width] = dot(order, x, 1, 1).astype(BF16)


def body(queries, keys, values, out_grad, slide_lengths, head_offsets):
    tok_rows, model_width = queries.shape
    level_count, head_count = head_offsets.shape
    device_count = lax.axis_size("seq")
    plan = Plan(tok_rows, model_width, level_count, head_count, slide_lengths.shape[0], device_count)
    hd, chunks = plan.hd, plan.chunks
    groups = [list(range(i, i + plan.near)) for i in range(0, device_count, plan.near)]
    sds = jax.ShapeDtypeStruct
    near = plan.near

    def permuted(x, target):
        return lax.ppermute(x, "seq", [(i, target(i)) for i in range(device_count)])

    def swap(x):
        return lax.all_to_all(x, "seq", 0, 0, tiled=True, axis_index_groups=groups)

    def shifted(x, steps):
        return permuted(x, lambda i: (i + steps * near) % device_count)

    def traded(slots):
        return [slots[0]] + [permuted(slots[j], lambda i, j=j: i ^ j) for j in range(1, near)]

    exchanges = [[(c, i) for i in range(3)] for c in range(chunks)]
    for c in range(chunks):
        exchanges[min(c + 1, chunks - 1)].append((c, 3))
    arrays = (queries, keys, values, out_grad)
    width = near * hd
    received, where = [], {}
    token = ()
    for pieces in exchanges:
        slotted = len(received) > 0
        block = (len(pieces) * hd, tok_rows)
        *packed, tok = kernel_call(
            partial(pack_body, plan, [c for c, _ in pieces], near + 1 if slotted else 1),
            (
                [sds(block, BF16)] * near + [sds(plan.table, F32)]
                if slotted
                else [sds((near,) + block, BF16)]
            )
            + [TOKEN],
            [ANY] * len(pieces) + [SMEM] * 2 * slotted + [ANY] * len(token),
            [
                pltpu.VMEM((len(pieces), tok_rows, width), BF16),
                pltpu.VMEM((width, tok_rows), BF16),
                pltpu.SemaphoreType.DMA((len(pieces),)),
            ],
            name="pack",
            limit=VMEM_LIMIT if slotted else PACK_LIMIT,
        )(*(arrays[i] for _, i in pieces), *(slide_lengths, head_offsets) * slotted, *token)
        token = (tok,)
        if slotted:
            table = packed.pop()
        for place, piece in enumerate(pieces):
            where[piece] = (len(received), place * hd)
        received.append(traded(packed) if slotted else [swap(packed[0])])

    n, n3, n2 = plan.rows, plan.all_rows, plan.last
    pair_flops = 20 * 2 * 128 * SEG0 * SEG0
    (token,) = token
    fronts = []
    for chunk in range(chunks):
        source, first = where[chunk, 0]
        near_x = received[source]
        last_rows = [sds((hd, n2), BF16), sds((2 * hd, n2), BF16)]
        operands = [(n3, 128), (128, n3), (64, n3)]
        raw, res = pltpu.VMEM((3 * hd, n), BF16), pltpu.VMEM((64, n3), F32)
        sums = sds((64, n), F32)
        make = partial(forward_body, plan, chunk, first)
        if chunk == 0:
            q2, kv2, acc, token = kernel_call(
                partial(make, len(near_x), "both"),
                last_rows + [sums, TOKEN],
                [VMEM, ANY] + [VMEM] * len(near_x),
                [raw] + [pltpu.VMEM(shape, BF16) for shape in operands] + [res],
                name=f"forward{chunk}",
            )(table, token, *near_x)
            far_kv = [shifted(kv2, s) for s in range(1, plan.far)]
        else:
            q2, kv2, *state, token = kernel_call(
                partial(make, len(near_x), "rows"),
                last_rows + [sds(shape, BF16) for shape in operands] + [TOKEN],
                [VMEM, ANY] + [VMEM] * len(near_x),
                [raw],
                name=f"rows{chunk}",
            )(table, token, *near_x)
            far_kv = [shifted(kv2, s) for s in range(1, plan.far)]
            acc, token = kernel_call(
                partial(make, 0, "sums"),
                [sums, TOKEN],
                [VMEM, ANY] + [VMEM] * 3,
                [res],
                name=f"sums{chunk}",
            )(table, token, *state)
        fronts.append((acc, q2, kv2, *far_kv))
    states = []
    for chunk, front in enumerate(fronts):
        source, first = where[chunk, 3]
        att, ld, grad2, far2, token = kernel_call(
            partial(last_body, plan, chunk, first, len(received[source])),
            [
                sds((hd, n), BF16),
                sds((8, n), F32),
                sds((3 * hd, n2), F32),
                sds((max(plan.far - 1, 1), 2 * hd, n2), BF16),
                TOKEN,
            ],
            [VMEM, ANY] + [VMEM] * (len(front) + len(received[source])),
            [pltpu.VMEM((64, n), F32), pltpu.VMEM((hd, n), BF16)],
            flops=4 * pair_flops,
            name=f"last{chunk}",
        )(table, token, *front[:3], *received[source], *front[3:])
        states.append((att, (ld, grad2, *(shifted(far2[s - 1], -s) for s in range(1, plan.far)))))
    full = sds((tok_rows, model_width), BF16)
    for chunk, (_, (ld, *tail)) in enumerate(states):
        atts = [s[0] for s in states] if chunk == 0 else []
        slotted = chunk == chunks - 1 and not atts
        count = len(atts) + 3
        sources = [where[chunk, 0], where[chunk, 3]]
        blocks = [len(received[x[0]]) for x in sources]
        block = sds((count * hd, tok_rows), BF16)
        grads = pltpu.VMEM((3 * hd, n), F32)
        *out, token = kernel_call(
            partial(backward_body, plan, chunk, [x[1] for x in sources], blocks, slotted),
            ([block] * near if slotted else [sds((3 * hd, n), F32)]) + [TOKEN],
            [VMEM, ANY] + [VMEM] * (1 + sum(blocks) + slotted * len(tail)),
            [
                pltpu.VMEM((n3, 128), BF16),
                pltpu.VMEM((128, n3), BF16),
                pltpu.VMEM((n3, 128), BF16),
                pltpu.VMEM((64, n3), BF16),
                pltpu.VMEM((hd, n3), BF16),
                pltpu.VMEM((hd, n3), BF16),
            ]
            + [grads] * slotted,
            flops=len(plan.tiles) * 5 * pair_flops,
            name=f"backward{chunk}",
        )(table, token, ld, *received[sources[0][0]], *received[sources[1][0]], *(tail if slotted else []))
        if not slotted:
            *out, token = kernel_call(
                partial(finish_body, plan, chunk, len(atts)),
                [sds((near,) + block.shape, BF16), TOKEN],
                [VMEM, ANY] + [VMEM] * (1 + len(atts) + len(tail)),
                [grads],
                name=f"finish{chunk}",
            )(table, token, *out, *atts, *tail)
        y = traded(out)[::-1] if slotted else [swap(out[0])]
        scratch = [pltpu.VMEM((near,) + block.shape, BF16)] if slotted else []
        column = pl.BlockSpec((tok_rows, width), lambda i, c=chunk: (0, c))
        specs = [pl.BlockSpec(v.shape, lambda i, r=len(v.shape): (0,) * r) for v in y]
        if chunk == 0:
            attended, *outs = kernel_call(
                partial(unpack_body, plan, [0] + [chunks + i for i in range(3)], slotted),
                [full] * 4,
                specs,
                scratch,
                name="unpack",
                grid=(1,),
                out_specs=[pl.BlockSpec(full.shape, lambda i: (0, 0))] + [column] * 3,
            )(*y)
        else:
            outs = kernel_call(
                partial(unpack_body, plan, list(range(3)), slotted),
                [full] * 3,
                specs + [ANY] * 3,
                scratch,
                name="unpack",
                grid=(1,),
                out_specs=[column] * 3,
                input_output_aliases={len(y) + i: i for i in range(3)},
            )(*y, *outs)
    return (attended, *outs)


def solution(mesh):
    rows = P(("groups", "seq"), None)
    return jax.shard_map(
        body,
        mesh=mesh,
        in_specs=(rows, rows, rows, rows, P("groups"), P()),
        out_specs=(rows, rows, rows, rows),
        check_vma=False,
    )
```

```python
from functools import partial
import math

import jax
import jax.numpy as jnp
from jax import lax
from jax.experimental import pallas as pl
from jax.experimental.pallas import tpu as pltpu
from jax.sharding import PartitionSpec as P

SEG0 = 1024
BIG = 2.0**100
LOG2E = math.log2(math.e)
BF16 = jnp.bfloat16
F32 = jnp.float32
VMEM_LIMIT = 36 << 20
PACK_LIMIT = 63 << 20


class Plan:
    def __init__(self, tok_rows, model_width, level_count, head_count, slide_count, device_count):
        self.tok = tok_rows
        self.width = model_width
        self.levels = level_count
        self.hd = model_width // head_count
        self.slides = slide_count
        self.devices = device_count
        self.stride = device_count * tok_rows // SEG0
        self.bits = self.stride.bit_length() - 1
        self.near = min((SEG0 << (level_count - 2)) // tok_rows, device_count)
        self.far = device_count // self.near
        self.chunks = head_count // self.near
        self.segs = self.near * tok_rows // SEG0
        self.seg_dev = SEG0 // tok_rows
        self.cdev = tok_rows // self.stride
        self.cseg = SEG0 // self.stride
        self.rows = self.near * tok_rows
        self.last = self.segs * self.cseg
        self.tiles = []
        for level in range(level_count - 1):
            for first in range(0, self.segs, 1 << level):
                self.tiles.append((level, first))
        self.all_rows = len(self.tiles) * SEG0
        self.slide_pad = -(-slide_count // 8) * 8
        self.rest = 128 - 2 * self.hd - 8 - self.slide_pad
        self.aligned = self.cseg % 128 == 0
        self.table = (-(-self.table_row(self.chunks, 0) // 8) * 8, 128)
        assert self.rest >= 0 and self.hd + 16 <= 64 and self.hd % 16 == 0 and self.chunks > 1


    def level_bits(self, level):
        return level if level < self.levels - 1 else self.bits

    def table_row(self, chunk, level):
        return self.slide_pad + chunk * (self.levels + 1) + level


def reversed_bits(value, bits):
    out = value * 0
    for b in range(bits):
        out = out + ((value >> b) & 1) * (1 << (bits - 1 - b))
    return out


def dot(a, b, ca=1, cb=0, precision=None):
    return lax.dot_general(
        a, b, (((ca,), (cb,)), ((), ())), preferred_element_type=F32, precision=precision
    )


def iota(shape, axis):
    return lax.broadcasted_iota(jnp.int32, shape, axis)


def kernel_call(body, out_shape, in_specs, scratch=(), flops=0, name=None, limit=VMEM_LIMIT, **more):
    return pl.pallas_call(
        body,
        out_shape=out_shape,
        in_specs=in_specs,
        scratch_shapes=list(scratch),
        name=name,
        compiler_params=pltpu.CompilerParams(vmem_limit_bytes=limit),
        cost_estimate=pl.CostEstimate(flops=flops, bytes_accessed=1 << 20, transcendentals=0),
        **more,
    )


VMEM = pl.BlockSpec(memory_space=pltpu.VMEM)
SMEM = pl.BlockSpec(memory_space=pltpu.SMEM)
ANY = pl.BlockSpec(memory_space=pl.ANY)
TOKEN = jax.ShapeDtypeStruct((8, 128), F32)


def class_order(count, stride, shape, axis_row, axis_tok):
    row, tok = iota(shape, axis_row), iota(shape, axis_tok)
    size = count // stride
    want = (row % size) * stride + reversed_bits(row // size, stride.bit_length() - 1)
    return jnp.where(want == tok, 1.0, 0.0).astype(BF16)


def near_index(plan):
    return lax.rem(lax.axis_index("seq"), plan.near)


def pack_body(plan, columns, count_out, *refs):
    count = len(columns)
    ins, outs, (tok_out, rows, turned, sems) = refs[:count], refs[-4 - count_out : -4], refs[-4:]
    tok_out[...] = jnp.zeros_like(tok_out)
    hd, width = plan.hd, plan.near * plan.hd
    copies = [
        pltpu.make_async_copy(ref.at[:, c * width : (c + 1) * width], rows.at[i], sems.at[i])
        for i, (ref, c) in enumerate(zip(ins, columns))
    ]
    for copy in copies:
        copy.start()
    if count_out > 1:
        fill_table(plan, *refs[count : count + 2], outs[-1])
        outs = outs[:-1]
    order = class_order(plan.tok, plan.stride, (plan.tok, plan.tok), 0, 1)
    me = near_index(plan)
    for i, copy in enumerate(copies):
        copy.wait()
        x = dot(rows[i], order, 0, 1).astype(BF16)
        if len(outs) == 1:
            for j in range(plan.near):
                outs[0][j, i * hd : (i + 1) * hd, :] = x[j * hd : (j + 1) * hd, :]
        else:
            turned[...] = x
            for j in range(plan.near):
                first = pl.multiple_of((me ^ j) * hd, 16)
                outs[j][i * hd : (i + 1) * hd, :] = turned[pl.ds(first, hd), :]


def segment_from(plan, blocks):
    if plan.cdev % 64 == 0:
        return jnp.concatenate(
            [x[:, c * plan.cdev : (c + 1) * plan.cdev] for c in range(plan.stride) for x in blocks],
            axis=1,
        ).astype(F32)
    return dot(jnp.concatenate(blocks, axis=1), device_lanes(plan, 1, 0))


def device_lanes(plan, axis_dev, axis_seg):
    shape = (SEG0, SEG0)
    seg, dev = iota(shape, axis_dev), iota(shape, axis_seg)
    cls, inside = seg // plan.cseg, seg % plan.cseg
    want = inside // plan.cdev * plan.tok + cls * plan.cdev + inside % plan.cdev
    return jnp.where(want == dev, 1.0, 0.0).astype(BF16)


def segment_to(plan, x):
    if plan.cdev % 64 == 0:
        return [
            jnp.concatenate(
                [
                    x[:, c * plan.cseg + d * plan.cdev : c * plan.cseg + (d + 1) * plan.cdev]
                    for c in range(plan.stride)
                ],
                axis=1,
            )
            for d in range(plan.seg_dev)
        ]
    x = dot(x, device_lanes(plan, 0, 1)).astype(BF16)
    return [x[:, d * plan.tok : (d + 1) * plan.tok] for d in range(plan.seg_dev)]


def slide_rows(plan, pos, table):
    slide = jnp.zeros(pos.shape, jnp.int32)
    for i in range(plan.slides):
        slide = slide + jnp.where(pos.astype(F32) >= table[i : i + 1, 0:1], 1, 0)
    shape = (plan.slide_pad, pos.shape[1])
    return jnp.where(iota(shape, 0) == slide, 1.0, 0.0)


def key_features(plan, k, one_hot):
    n = k.shape[1]
    return jnp.concatenate(
        [k, k, jnp.ones((8, n), F32), one_hot, jnp.zeros((plan.rest, n), F32)], axis=0
    )


def query_features(plan, q, one_hot):
    n = q.shape[1]
    q = q * (plan.hd**-0.5 * LOG2E)
    high = q.astype(BF16).astype(F32)
    mask = (one_hot - 1.0) * BIG
    return jnp.concatenate(
        [high, q - high, jnp.zeros((8, n), F32), mask, jnp.zeros((plan.rest, n), F32)], axis=0
    )


def value_features(plan, v):
    n = v.shape[1]
    return jnp.concatenate([v, jnp.ones((8, n), F32), jnp.zeros((56 - plan.hd, n), F32)], axis=0)


def three_rows(x):
    a = x.astype(BF16).astype(F32)
    b = (x - a).astype(BF16).astype(F32)
    row = iota((8, x.shape[1]), 0)
    return jnp.where(row == 0, a, jnp.where(row == 1, b, jnp.where(row == 2, x - a - b, 0.0)))


def forward_tile(plan, s, values_t):
    peak = jnp.max(s, axis=0, keepdims=True)
    p = jnp.exp2(s - peak).astype(BF16)
    o = dot(values_t, p)
    return jnp.concatenate(
        [o[: plan.hd + 8], jnp.broadcast_to(peak, (56 - plan.hd, o.shape[1]))], axis=0
    )


def merged(plan, a, b):
    at = plan.hd + 8
    peak_a, peak_b = a[at : at + 1], b[at : at + 1]
    peak = jnp.maximum(peak_a, peak_b)
    both = a[:at] * jnp.exp2(peak_a - peak) + b[:at] * jnp.exp2(peak_b - peak)
    return jnp.concatenate([both, jnp.broadcast_to(peak, (64 - at, a.shape[1]))], axis=0)


def backward_tile(plan, qa, kat, ga, vat, gt, qt):
    n = qa.shape[0]
    step = min(n, SEG0 // 2)
    parts = [slice(i, i + step) for i in range(0, n, step)]
    weights = []
    for rows in parts:
        dp = dot(ga[rows], vat)
        p = jnp.exp2(dot(qa[rows], kat))
        weights.append((p.astype(BF16), (p * dp).astype(BF16)))
    query_t = [dot(kat[: plan.hd], ds, 1, 1) for _, ds in weights]
    key_t = sum(dot(qt[:, rows], ds) for rows, (_, ds) in zip(parts, weights))
    value_t = sum(dot(gt[:, rows], p) for rows, (p, _) in zip(parts, weights))
    return jnp.concatenate(query_t, axis=1), key_t, value_t


def tile_pieces(plan, starts, tile):
    level, first = plan.tiles[tile]
    rows = SEG0 >> level
    out = []
    for i in range(1 << level):
        src = pl.ds(pl.multiple_of((first + i) * SEG0 + starts[level], 128), rows)
        out.append((src, slice(tile * SEG0 + i * rows, tile * SEG0 + (i + 1) * rows)))
    return out


def last_slices(plan, starts):
    return [
        pl.ds(pl.multiple_of(seg * SEG0 + starts[-1], plan.cseg), plan.cseg) for seg in range(plan.segs)
    ]


def last_places(plan, starts, shape, axis_seg, axis_last):
    hit = iota(shape, axis_seg) == starts[-1] + iota(shape, axis_last)
    return jnp.where(hit, 1.0, 0.0)


def last_lanes(plan, starts, ref):
    if plan.aligned:
        return jnp.concatenate([ref[:, s] for s in last_slices(plan, starts)], axis=1)
    place = last_places(plan, starts, (SEG0, plan.cseg), 0, 1)
    exact = lax.Precision.HIGHEST
    parts = [
        dot(ref[:, g * SEG0 : (g + 1) * SEG0].astype(F32), place, precision=exact)
        for g in range(plan.segs)
    ]
    return jnp.concatenate(parts, axis=1).astype(ref.dtype)


def last_update(plan, starts, ref, rows, part, update, fill):
    if plan.aligned:
        for seg, s in enumerate(last_slices(plan, starts)):
            ref[rows, s] = update(ref[rows, s], part[:, seg * plan.cseg : (seg + 1) * plan.cseg])
        return
    place = last_places(plan, starts, (plan.cseg, SEG0), 1, 0)
    hit = jnp.max(place, axis=0, keepdims=True) > 0
    for seg in range(plan.segs):
        own = part[:, seg * plan.cseg : (seg + 1) * plan.cseg]
        own = jnp.where(hit, dot(own, place, precision=lax.Precision.HIGHEST), fill)
        s = slice(seg * SEG0, (seg + 1) * SEG0)
        ref[rows, s] = update(ref[rows, s], own)


def no_level(plan):
    return jnp.where(iota((64, 1), 0) >= plan.hd + 8, -BIG, 0.0)


def fill_table(plan, len_ref, off_ref, table):
    table[...] = jnp.zeros_like(table)

    def put(row, value):
        table[row : row + 1, :] = jnp.full((1, 128), value, jnp.int32).astype(F32)

    end = 0
    for i in range(plan.slides):
        end = end + len_ref[i]
        put(i, end)
    for chunk in range(plan.chunks):
        head = chunk * plan.near + near_index(plan)
        for level in range(plan.levels):
            bits = plan.level_bits(level)
            first = reversed_bits(off_ref[level, head] % (1 << bits), bits) * (SEG0 >> bits)
            put(plan.table_row(chunk, level), first)
        put(plan.table_row(chunk, plan.levels), off_ref[plan.levels - 1, head] % plan.stride)


def level_starts(plan, table, chunk):
    rows = [plan.table_row(chunk, level) for level in range(plan.levels)]
    return [jnp.max(table[row : row + 1, :]).astype(jnp.int32) for row in rows]


def slots_of(plan, refs):
    if len(refs) > 1:
        return refs
    return [refs[0].at[near_index(plan) ^ j] for j in range(plan.near)]


def segment_of(plan, slots, first, count, seg):
    return segment_from(
        plan,
        [
            slots[seg * plan.seg_dev + d][first : first + count * plan.hd, :]
            for d in range(plan.seg_dev)
        ],
    )


def slot_tokens(plan, seg, slot, inside):
    me = near_index(plan)
    seg = (me // plan.seg_dev) ^ seg
    return seg * SEG0 + (lax.rem(me, plan.seg_dev) ^ slot) * plan.tok + inside


def segment_slides(plan, seg, table):
    n = iota((1, SEG0), 1)
    inside = (n % plan.cdev) * plan.stride + reversed_bits(n // plan.cseg, plan.bits)
    pos = slot_tokens(plan, seg, n % plan.cseg // plan.cdev, inside)
    return slide_rows(plan, lax.axis_index("seq") // plan.near * plan.rows + pos, table)


def forward_body(plan, chunk, first, blocks, parts, table, tok_in, *refs):
    slots, refs = slots_of(plan, refs[:blocks]) if blocks else None, refs[blocks:]
    if parts == "rows":
        q2, kv2, ka, qat, vat, tok_out, raw = refs
    elif parts == "sums":
        ka, qat, vat, acc_ref, tok_out, res = refs
    else:
        q2, kv2, acc_ref, tok_out, raw, ka, qat, vat, res = refs
    tok_out[...] = jnp.zeros_like(tok_out)
    starts = level_starts(plan, table, chunk)
    if parts != "sums":
        forward_operands(plan, first, slots, table, starts, q2, kv2, ka, qat, vat, raw)
    if parts != "rows":
        forward_levels(plan, starts, ka, qat, vat, acc_ref, res)


def forward_operands(plan, first, slots, table, starts, q2, kv2, ka, qat, vat, raw):
    hd = plan.hd
    for seg in range(plan.segs):
        rows = slice(seg * SEG0, (seg + 1) * SEG0)
        xt = segment_of(plan, slots, first, 3, seg)
        raw[:, rows] = xt.astype(BF16)
        q, k, v = (xt[i * hd : (i + 1) * hd] for i in range(3))
        one_hot = segment_slides(plan, seg, table)
        ka[rows, :] = key_features(plan, k, one_hot).astype(BF16).T
        qat[:, rows] = query_features(plan, q, one_hot).astype(BF16)
        vat[:, rows] = value_features(plan, v).astype(BF16)
    for tile in range(plan.segs, len(plan.tiles)):
        for src, dst in tile_pieces(plan, starts, tile):
            ka[dst, :] = ka[src, :]
            for ref in (qat, vat):
                ref[:, dst] = ref[:, src]
    last = last_lanes(plan, starts, raw)
    q2[...] = last[0:hd]
    kv2[...] = last[hd:]


def forward_levels(plan, starts, ka, qat, vat, acc_ref, res):
    tiles = [slice(t * SEG0, (t + 1) * SEG0) for t in range(len(plan.tiles))]
    scores = [dot(ka[rows, :], qat[:, rows]) for rows in tiles]
    for s, rows in zip(scores, tiles):
        res[:, rows] = forward_tile(plan, s, vat[:, rows])
    acc_ref[...] = res[:, 0 : plan.rows]
    for tile in range(plan.segs, len(plan.tiles)):
        for src, dst in tile_pieces(plan, starts, tile):
            acc_ref[:, src] = merged(plan, acc_ref[:, src], res[:, dst])


def last_body(plan, chunk, first, blocks, table, tok_in, acc_ref, q2, kv2, *rest):
    slots, rest = slots_of(plan, rest[:blocks]), rest[blocks:]
    far_in, (att_ref, ld_ref, grad_ref, far_ref, tok_out, acc, gt) = (
        rest[: plan.far - 1],
        rest[plan.far - 1 :],
    )
    hd = plan.hd
    tok_out[...] = jnp.zeros_like(tok_out)
    group = lax.axis_index("seq") // plan.near
    starts = level_starts(plan, table, chunk)
    row = plan.table_row(chunk, plan.levels)
    acc[...] = acc_ref[...]
    x = jnp.concatenate([ref[...].astype(F32) for ref in (kv2,) + far_in], axis=1)
    n = iota((1, SEG0), 1)
    owner = group - n // plan.last
    owner = jnp.where(owner < 0, owner + plan.far, owner)
    inside = (n % plan.cdev) * plan.stride + table[row : row + 1, 0:1].astype(jnp.int32)
    seg, slot = n % plan.last // plan.cseg, n % plan.cseg // plan.cdev
    pos = owner * plan.rows + slot_tokens(plan, seg, slot, inside)
    one_hot = slide_rows(plan, pos, table)
    key_f = key_features(plan, x[0:hd], one_hot)
    query_f = query_features(plan, q2[...].astype(F32), one_hot[:, 0 : plan.last])
    vat2 = value_features(plan, x[hd : 2 * hd]).astype(BF16)
    res = forward_tile(plan, dot(key_f.astype(BF16).T, query_f.astype(BF16)), vat2)
    last_update(plan, starts, acc, slice(None), res, partial(merged, plan), no_level(plan))
    for seg in range(plan.segs):
        rows = slice(seg * SEG0, (seg + 1) * SEG0)
        a = acc[:, rows]
        total = a[hd : hd + 1]
        att = (a[0:hd] / total).astype(BF16)
        att_ref[:, rows] = att
        log_total = a[hd + 8 : hd + 9] + jnp.log2(total)
        g = segment_of(plan, slots, first, 1, seg)
        gt[:, rows] = g.astype(BF16)
        grad_dot = jnp.sum(g * att.astype(F32), axis=0, keepdims=True)
        ld_ref[:, rows] = jnp.where(iota((8, SEG0), 0) == 0, log_total, grad_dot)
    g2 = last_lanes(plan, starts, gt)
    ld2 = last_lanes(plan, starts, ld_ref)
    qa2, ga2 = backward_queries(plan, query_f, g2.astype(F32), ld2)
    dq, dk, dv = backward_tile(plan, qa2, key_f.astype(BF16), ga2[:, 0:64], vat2, g2, q2[...])
    grad_ref[...] = jnp.concatenate(
        [dq, dk[:, 0 : plan.last], dv[:, 0 : plan.last]], axis=0
    )
    both = jnp.concatenate([dk, dv], axis=0)
    for s in range(1, plan.far):
        far_ref[s - 1] = both[:, s * plan.last : (s + 1) * plan.last].astype(BF16)


def backward_queries(plan, query_f, g, ld):
    hd = plan.hd
    query_f = jnp.concatenate(
        [query_f[0 : 2 * hd], three_rows(-ld[0:1]), query_f[2 * hd + 8 :]], axis=0
    )
    grad_f = jnp.concatenate(
        [g, three_rows(-ld[1:2]), jnp.zeros((120 - hd, g.shape[1]), F32)], axis=0
    )
    return query_f.astype(BF16).T, grad_f.astype(BF16).T


def backward_body(plan, chunk, places, blocks, ends, table, tok_in, ld_ref, *refs):
    slots, refs = slots_of(plan, refs[: blocks[0]]), refs[blocks[0] :]
    g_slots, refs = slots_of(plan, refs[: blocks[1]]), refs[blocks[1] :]
    if ends:
        grad2, far_refs, outs, refs = refs[0], refs[1 : plan.far], refs[plan.far : -8], refs[-8:]
        tok_out, qa, kat, ga, vat, gt, qt, grads = refs
    else:
        grads, tok_out, qa, kat, ga, vat, gt, qt = refs
    hd = plan.hd
    tok_out[...] = jnp.zeros_like(tok_out)
    starts = level_starts(plan, table, chunk)
    for seg in range(plan.segs):
        rows = slice(seg * SEG0, (seg + 1) * SEG0)
        xt = segment_of(plan, slots, places[0], 3, seg)
        q, k, v = (xt[i * hd : (i + 1) * hd] for i in range(3))
        g = segment_of(plan, g_slots, places[1], 1, seg)
        one_hot = segment_slides(plan, seg, table)
        kat[:, rows] = key_features(plan, k, one_hot).astype(BF16)
        vat[:, rows] = value_features(plan, v).astype(BF16)
        qt[:, rows] = q.astype(BF16)
        gt[:, rows] = g.astype(BF16)
        qa[rows, :], ga[rows, :] = backward_queries(
            plan, query_features(plan, q, one_hot), g, ld_ref[:, rows]
        )
    for tile in range(plan.segs, len(plan.tiles)):
        for src, dst in tile_pieces(plan, starts, tile):
            qa[dst, :] = qa[src, :]
            ga[dst, :] = ga[src, :]
            for ref in (kat, vat, gt, qt):
                ref[:, dst] = ref[:, src]

    for tile in range(len(plan.tiles)):
        rows = slice(tile * SEG0, (tile + 1) * SEG0)
        parts = backward_tile(
            plan, qa[rows, :], kat[:, rows], ga[rows, 0:64], vat[:, rows], gt[:, rows], qt[:, rows]
        )
        if tile < plan.segs:
            for i, part in enumerate(parts):
                grads[i * hd : (i + 1) * hd, rows] = part
            continue
        for src, dst in tile_pieces(plan, starts, tile):
            at = slice(dst.start - rows.start, dst.stop - rows.start)
            for i, part in enumerate(parts):
                own = slice(i * hd, (i + 1) * hd)
                grads[own, src] = grads[own, src] + part[:, at]
    if ends:

        def store(slot, x):
            outs[slot][...] = x

        finished(plan, starts, [], grad2, far_refs, grads, store)


def finished(plan, starts, att_refs, grad2, far_refs, grads, store):
    hd = plan.hd
    more = grad2[...]
    if far_refs:
        far = sum(ref[...].astype(F32) for ref in far_refs)
        more = jnp.concatenate([more[0:hd], more[hd:] + far], axis=0)
    last_update(plan, starts, grads, slice(None), more, jnp.add, 0.0)
    scale = hd**-0.5
    for seg in range(plan.segs):
        rows = slice(seg * SEG0, (seg + 1) * SEG0)
        parts = [ref[:, rows] for ref in att_refs]
        parts += [(grads[0 : 2 * hd, rows] * scale).astype(BF16), grads[2 * hd : 3 * hd, rows].astype(BF16)]
        for d, x in enumerate(segment_to(plan, jnp.concatenate(parts, axis=0))):
            store(seg * plan.seg_dev + d, x)


def finish_body(plan, chunk, atts, table, tok_in, near_ref, *refs):
    att_refs, refs = refs[:atts], refs[atts:]
    grad2, far_refs, (out_ref, tok_out, grads) = refs[0], refs[1 : plan.far], refs[plan.far :]
    tok_out[...] = jnp.zeros_like(tok_out)
    grads[...] = near_ref[...]

    def store(slot, x):
        out_ref[near_index(plan) ^ slot] = x

    finished(plan, level_starts(plan, table, chunk), att_refs, grad2, far_refs, grads, store)


def unpack_body(plan, places, slotted, *refs):
    if slotted:
        y_ref, outs = refs[-1], refs[-1 - len(places) : -1]
        for j in range(plan.near):
            y_ref[near_index(plan) ^ j] = refs[plan.near - 1 - j][...]
    else:
        y_ref, outs = refs[0], refs[-len(places) :]
    hd, width = plan.hd, plan.near * plan.hd
    order = class_order(plan.tok, plan.stride, (plan.tok, plan.tok), 1, 0)
    for out_ref, first in zip(outs, places):
        for col in range(out_ref.shape[1] // width):
            i = first + col
            x = jnp.concatenate([y_ref[d, i * hd : (i + 1) * hd, :] for d in range(plan.near)], axis=0)
            out_ref[:, col * width : (col + 1) * width] = dot(order, x, 1, 1).astype(BF16)


def body(queries, keys, values, out_grad, slide_lengths, head_offsets):
    tok_rows, model_width = queries.shape
    level_count, head_count = head_offsets.shape
    device_count = lax.axis_size("seq")
    plan = Plan(tok_rows, model_width, level_count, head_count, slide_lengths.shape[0], device_count)
    hd, chunks = plan.hd, plan.chunks
    groups = [list(range(i, i + plan.near)) for i in range(0, device_count, plan.near)]
    sds = jax.ShapeDtypeStruct
    near = plan.near

    def permuted(x, target):
        return lax.ppermute(x, "seq", [(i, target(i)) for i in range(device_count)])

    def swap(x):
        return lax.all_to_all(x, "seq", 0, 0, tiled=True, axis_index_groups=groups)

    def shifted(x, steps):
        return permuted(x, lambda i: (i + steps * near) % device_count)

    def traded(slots):
        return [slots[0]] + [permuted(slots[j], lambda i, j=j: i ^ j) for j in range(1, near)]

    exchanges = [[(c, i) for i in range(3)] for c in range(chunks)]
    for c in range(chunks):
        exchanges[min(c + 1, chunks - 1)].append((c, 3))
    arrays = (queries, keys, values, out_grad)
    width = near * hd
    received, where = [], {}
    token = ()
    for pieces in exchanges:
        slotted = len(received) > 0
        block = (len(pieces) * hd, tok_rows)
        *packed, tok = kernel_call(
            partial(pack_body, plan, [c for c, _ in pieces], near + 1 if slotted else 1),
            (
                [sds(block, BF16)] * near + [sds(plan.table, F32)]
                if slotted
                else [sds((near,) + block, BF16)]
            )
            + [TOKEN],
            [ANY] * len(pieces) + [SMEM] * 2 * slotted + [ANY] * len(token),
            [
                pltpu.VMEM((len(pieces), tok_rows, width), BF16),
                pltpu.VMEM((width, tok_rows), BF16),
                pltpu.SemaphoreType.DMA((len(pieces),)),
            ],
            name="pack",
            limit=VMEM_LIMIT if slotted else PACK_LIMIT,
        )(*(arrays[i] for _, i in pieces), *(slide_lengths, head_offsets) * slotted, *token)
        token = (tok,)
        if slotted:
            table = packed.pop()
        for place, piece in enumerate(pieces):
            where[piece] = (len(received), place * hd)
        received.append(traded(packed) if slotted else [swap(packed[0])])

    n, n3, n2 = plan.rows, plan.all_rows, plan.last
    pair_flops = 20 * 2 * 128 * SEG0 * SEG0
    (token,) = token
    fronts = []
    for chunk in range(chunks):
        source, first = where[chunk, 0]
        near_x = received[source]
        last_rows = [sds((hd, n2), BF16), sds((2 * hd, n2), BF16)]
        operands = [(n3, 128), (128, n3), (64, n3)]
        raw, res = pltpu.VMEM((3 * hd, n), BF16), pltpu.VMEM((64, n3), F32)
        sums = sds((64, n), F32)
        make = partial(forward_body, plan, chunk, first)
        if chunk == 0:
            q2, kv2, acc, token = kernel_call(
                partial(make, len(near_x), "both"),
                last_rows + [sums, TOKEN],
                [VMEM, ANY] + [VMEM] * len(near_x),
                [raw] + [pltpu.VMEM(shape, BF16) for shape in operands] + [res],
                name=f"forward{chunk}",
            )(table, token, *near_x)
            far_kv = [shifted(kv2, s) for s in range(1, plan.far)]
        else:
            q2, kv2, *state, token = kernel_call(
                partial(make, len(near_x), "rows"),
                last_rows + [sds(shape, BF16) for shape in operands] + [TOKEN],
                [VMEM, ANY] + [VMEM] * len(near_x),
                [raw],
                name=f"rows{chunk}",
            )(table, token, *near_x)
            far_kv = [shifted(kv2, s) for s in range(1, plan.far)]
            acc, token = kernel_call(
                partial(make, 0, "sums"),
                [sums, TOKEN],
                [VMEM, ANY] + [VMEM] * 3,
                [res],
                name=f"sums{chunk}",
            )(table, token, *state)
        fronts.append((acc, q2, kv2, *far_kv))
    states = []
    for chunk, front in enumerate(fronts):
        source, first = where[chunk, 3]
        att, ld, grad2, far2, token = kernel_call(
            partial(last_body, plan, chunk, first, len(received[source])),
            [
                sds((hd, n), BF16),
                sds((8, n), F32),
                sds((3 * hd, n2), F32),
                sds((max(plan.far - 1, 1), 2 * hd, n2), BF16),
                TOKEN,
            ],
            [VMEM, ANY] + [VMEM] * (len(front) + len(received[source])),
            [pltpu.VMEM((64, n), F32), pltpu.VMEM((hd, n), BF16)],
            flops=4 * pair_flops,
            name=f"last{chunk}",
        )(table, token, *front[:3], *received[source], *front[3:])
        states.append((att, (ld, grad2, *(shifted(far2[s - 1], -s) for s in range(1, plan.far)))))
    full = sds((tok_rows, model_width), BF16)
    for chunk, (_, (ld, *tail)) in enumerate(states):
        atts = [s[0] for s in states] if chunk == 0 else []
        slotted = chunk == chunks - 1 and not atts
        count = len(atts) + 3
        sources = [where[chunk, 0], where[chunk, 3]]
        blocks = [len(received[x[0]]) for x in sources]
        block = sds((count * hd, tok_rows), BF16)
        grads = pltpu.VMEM((3 * hd, n), F32)
        *out, token = kernel_call(
            partial(backward_body, plan, chunk, [x[1] for x in sources], blocks, slotted),
            ([block] * near if slotted else [sds((3 * hd, n), F32)]) + [TOKEN],
            [VMEM, ANY] + [VMEM] * (1 + sum(blocks) + slotted * len(tail)),
            [
                pltpu.VMEM((n3, 128), BF16),
                pltpu.VMEM((128, n3), BF16),
                pltpu.VMEM((n3, 128), BF16),
                pltpu.VMEM((64, n3), BF16),
                pltpu.VMEM((hd, n3), BF16),
                pltpu.VMEM((hd, n3), BF16),
            ]
            + [grads] * slotted,
            flops=len(plan.tiles) * 5 * pair_flops,
            name=f"backward{chunk}",
        )(table, token, ld, *received[sources[0][0]], *received[sources[1][0]], *(tail if slotted else []))
        if not slotted:
            *out, token = kernel_call(
                partial(finish_body, plan, chunk, len(atts)),
                [sds((near,) + block.shape, BF16), TOKEN],
                [VMEM, ANY] + [VMEM] * (1 + len(atts) + len(tail)),
                [grads],
                name=f"finish{chunk}",
            )(table, token, *out, *atts, *tail)
        y = traded(out)[::-1] if slotted else [swap(out[0])]
        scratch = [pltpu.VMEM((near,) + block.shape, BF16)] if slotted else []
        column = pl.BlockSpec((tok_rows, width), lambda i, c=chunk: (0, c))
        specs = [pl.BlockSpec(v.shape, lambda i, r=len(v.shape): (0,) * r) for v in y]
        if chunk == 0:
            attended, *outs = kernel_call(
                partial(unpack_body, plan, [0] + [chunks + i for i in range(3)], slotted),
                [full] * 4,
                specs,
                scratch,
                name="unpack",
                grid=(1,),
                out_specs=[pl.BlockSpec(full.shape, lambda i: (0, 0))] + [column] * 3,
            )(*y)
        else:
            outs = kernel_call(
                partial(unpack_body, plan, list(range(3)), slotted),
                [full] * 3,
                specs + [ANY] * 3,
                scratch,
                name="unpack",
                grid=(1,),
                out_specs=[column] * 3,
                input_output_aliases={len(y) + i: i for i in range(3)},
            )(*y, *outs)
    return (attended, *outs)


def solution(mesh):
    rows = P(("groups", "seq"), None)
    return jax.shard_map(
        body,
        mesh=mesh,
        in_specs=(rows, rows, rows, rows, P("groups"), P()),
        out_specs=(rows, rows, rows, rows),
        check_vma=False,
    )
```
